32 devices in a mesh: orb: 4 (over y, x), aux: 8 (over z, core).
Axes of the slice: x: 2, y: 2, z: 4, core: 2. Of those that a mesh axis runs over, the one named last changes fastest.
Arguments:
- b_rows: bfloat16 [2048, 32, 2, 128], P('aux', 'orb'), may hold values from -6 to 6
- col_blocks: int32 [4, 2], P('orb'), may hold values from 0 to 3, all different within a row
- g_occ: bfloat16 [2, 32, 32], P(None, 'orb'), may hold values from -1 to 1
- occ_live: int32 [2, 4, 4], replicated, may hold values 0 or 1
- g_virt: bfloat16 [2, 4, 128, 128], P(None, 'orb', 'aux'), may hold values from -0.5 to 0.5
- tau_weight: float32 [2], replicated, may hold values from 0.5 to 2
Outputs:
- chi: float32 [256, 2048], P('orb', 'aux')
The draws below stay inside these ranges and needn't reach their ends.
Inputs may be any that keep to these rules, and one draw needn't show every extreme that they name: `col_blocks`: each row group lists 2 different column blocks, and every column block is listed by some row group.
All inputs are finite; a program needn't handle non-finite values.
Results may differ from the reference program's by a relative error of at most 0.0041.
Values may be sent and summed in bfloat16 or wider, within the bound.
No kernel may reach another device: no remote copies, remote signals or barrier semaphores. Data moves between devices by JAX's collectives and lax.ppermute only.
A program may use at most 128 MiB of HBM per device.

```python
import math
import jax
import jax.numpy as jnp
from jax import lax

AUX_DEV = 256
TILE = 128
RD = 8
TAU = 2
AUX = 2048
GROUPS = 4
NROW = 32
NBLK = 4
K = 2


def touch_ends(drawn, own_key, least, high):
    dims = drawn.shape
    place = [jax.random.randint(jax.random.fold_in(own_key, axis), (), 0, dims[axis]) for axis in range(len(dims))]
    drawn = drawn.at[tuple(place)].set(least)
    longest = dims.index(max(dims))
    place[longest] = (place[longest] + 1) % dims[longest]
    return drawn.at[tuple(place)].set(high)


def level_of(own_key, shape, cuts, low, largest):
    level = 1.0
    for axis_at, parts in cuts:
        steps = jax.random.uniform(jax.random.fold_in(jax.random.fold_in(own_key, 6), axis_at), (parts,), jnp.float32, low / len(cuts), largest / len(cuts))
        level = level * jnp.repeat(jnp.exp(steps), shape[axis_at] // parts).reshape((-1,) + (1,) * (len(shape) - 1 - axis_at))
    return level


def distinct(key, rows, amount, top, lift):
    order = jax.random.permutation(jax.random.fold_in(key, 1), amount)
    boost = order
    for power in range(3):
        boost = boost * boost // amount
    boost = boost * lift // amount
    tickets = jax.random.randint(jax.random.fold_in(key, 2), (rows, amount), 0, 4096) + boost
    sure = jax.random.permutation(jax.random.fold_in(key, 3), rows)[jnp.arange(amount) % rows]
    tickets = jnp.where(jnp.arange(rows)[:, None] == sure[None, :], 1 << 14, tickets)
    priority = tickets * amount + jnp.arange(amount)
    return lax.top_k(priority.astype(jnp.int32), top)[1].astype(jnp.int32)


def centred(stream_key, shape, deviation, reach, pieces=(), kind=jnp.bfloat16):
    values = jax.random.normal(stream_key, shape, jnp.float32) * deviation
    if len(pieces) > 0:
        values = level_of(stream_key, shape, pieces, -0.22, 0.18) * values
    return jnp.clip(values, min=-reach, max=reach).astype(kind)


def setup_inputs(seed: int = 0) -> dict:
    seeds = jax.random.split(jax.random.key(seed), 7)
    return {
        "b_rows": centred(seeds[0], (AUX, NROW, K, TILE), 1.0, 6.0, ((0, 8), (1, 4))),
        "col_blocks": distinct(seeds[1], GROUPS, NBLK, K, 8192),
        "g_occ": centred(seeds[2], (TAU, NROW, NROW), NROW ** -0.5, 1.0, ((1, 4),)),
        "occ_live": touch_ends((jax.random.randint(seeds[3], (TAU, GROUPS, GROUPS), 0, 4) < 3).astype(jnp.int32), jax.random.fold_in(seeds[3], 1), 0, 1),
        "g_virt": centred(seeds[4], (TAU, NBLK, TILE, TILE), TILE ** -0.5, 0.5, ((1, 4), (2, 8))),
        "tau_weight": jnp.clip(jnp.exp(jax.random.uniform(seeds[5], (TAU,), jnp.float32, math.log(0.5), math.log(2.0))), 0.5, 2.0),
    }


def reference(b_rows, col_blocks, g_occ, occ_live, g_virt, tau_weight):
    live_mask = jnp.repeat(jnp.repeat(occ_live, RD, axis=1), RD, axis=2).astype(jnp.bfloat16)
    occ_masked = g_occ * live_mask
    blocks = jnp.arange(NBLK, dtype=jnp.int32)
    scale = 1.0 / math.sqrt(NROW * TILE * NBLK)

    def one_aux(aux_rows):
        grouped = aux_rows.reshape(AUX_DEV, GROUPS, RD, K, TILE).astype(jnp.float32)

        def one_column(total, column):
            chosen = (col_blocks == column).astype(jnp.float32)
            col_dense = jnp.einsum('pgrkc,gk->pgrc', grouped, chosen).reshape(AUX_DEV, NROW, TILE).astype(jnp.bfloat16)
            for moment in range(TAU):
                virt_block = g_virt[moment][column]
                virt_prod = jnp.dot(col_dense.reshape(AUX_DEV * NROW, TILE), virt_block, preferred_element_type=jnp.float32)
                virt_prod = virt_prod.astype(jnp.bfloat16).reshape(AUX_DEV, NROW, TILE)
                occ_prod = jnp.einsum('mn,qnc->qmc', occ_masked[moment].astype(jnp.float32), col_dense.astype(jnp.float32)).astype(jnp.bfloat16)
                term = jnp.einsum('pmc,qmc->qp', virt_prod.astype(jnp.float32), occ_prod.astype(jnp.float32))
                total = total + tau_weight[moment] * term
            return (total, None)
        total, unused = lax.scan(one_column, jnp.zeros((AUX_DEV, AUX_DEV), jnp.float32), blocks)
        return total * scale
    per_aux = lax.map(one_aux, b_rows.reshape(AUX // AUX_DEV, AUX_DEV, NROW, K, TILE))
    return jnp.transpose(per_aux, (1, 0, 2)).reshape(AUX_DEV, AUX)
```

```python
import functools
import math

import jax
import jax.numpy as jnp
from jax import lax
from jax.experimental import pallas as pl
from jax.experimental.pallas import tpu as pltpu
from jax.sharding import PartitionSpec as P

SUB = 8
PAIR = 16
F32 = jnp.float32
BF16 = jnp.bfloat16


def iota(shape, dim):
    return lax.broadcasted_iota(jnp.int32, shape, dim)


def dot(a, b):
    return jnp.dot(a, b, preferred_element_type=F32)


def pack_kernel(orb_count, rows_dev, slot_count, steps, me_ref, col_ref, b_ref, occ_ref, *outs):
    me = me_ref[0]
    half_rows = rows_dev * SUB
    out_rows = 2 * half_rows
    in_rows = PAIR * rows_dev * slot_count
    line = iota((out_rows, in_rows), 0)
    place = iota((out_rows, in_rows), 1)
    half = line // half_rows
    row = (line % half_rows) // SUB
    func = half * SUB + line % SUB
    first = (func * rows_dev + row) * slot_count
    pick = jnp.concatenate(
        [jnp.where(place == first + slot, 1.0, 0.0).astype(BF16) for slot in range(slot_count)], 0
    )
    total = steps * out_rows
    for out in outs:
        out[total:, :] = jnp.zeros((out.shape[0] - total, out.shape[1]), BF16)
        out[total:, : occ_ref.shape[1]] = occ_ref[...]

    def step(index, carry):
        source = b_ref[pl.ds(pl.multiple_of(index * in_rows, in_rows), in_rows), :]
        moved = dot(pick, source).astype(BF16)
        slots = [moved[slot * out_rows : (slot + 1) * out_rows] for slot in range(slot_count)]
        zero = jnp.zeros_like(slots[0])
        for distance, out in enumerate(outs):
            value = zero
            for slot in range(slot_count):
                value = jnp.where(col_ref[0, slot] == me ^ distance, slots[slot], value)
            out[pl.ds(pl.multiple_of(index * out_rows, out_rows), out_rows), :] = value
        return carry

    lax.fori_loop(0, steps, step, 0, unroll=min(steps, 4))


def work_kernel(
    orb_count, aux_count, rows_dev, tau_count, steps, share_rows,
    me_ref, live_ref, tau_ref, virt_ref, *refs,
):
    blocks, outs = refs[:orb_count], refs[orb_count : 2 * orb_count]
    mix_ref, occ_ref, virt_out = refs[2 * orb_count :]
    me, aux_me = me_ref[0], me_ref[1]
    rows = orb_count * rows_dev
    half_rows = rows_dev * SUB
    tile = blocks[0].shape[1]
    total = steps * 2 * half_rows
    part = tile // aux_count
    parts = []
    line = iota((tile, virt_ref.shape[0]), 0)
    place = iota((tile, virt_ref.shape[0]), 1)
    for moment in range(tau_count):
        wanted = (((line // part) ^ aux_me) * tau_count + moment) * part + line % part
        parts.append(dot(jnp.where(place == wanted, 1.0, 0.0).astype(BF16), virt_ref[...]).astype(BF16))
    virt = jnp.concatenate(parts, 1)
    occ_all = jnp.concatenate([block[total : total + tau_count * rows_dev, :] for block in blocks], 0)
    left_shape = (tau_count * rows * SUB, occ_all.shape[0])
    line = iota(left_shape, 0)
    moment_of = line // (rows * SUB)
    row_of = (line % (rows * SUB)) // SUB
    wanted = ((row_of // rows_dev) * tau_count + moment_of) * rows_dev + row_of % rows_dev
    left = jnp.where(iota(left_shape, 1) == wanted, 1.0, 0.0).astype(BF16)
    right_shape = (tile, rows * SUB)
    col_of = iota(right_shape, 1) // SUB
    wanted = ((col_of // rows_dev) ^ me) * rows_dev + col_of % rows_dev
    right = jnp.where(iota(right_shape, 0) == wanted, 1.0, 0.0).astype(BF16)
    spread = dot(dot(left, occ_all).astype(BF16), right)
    same = iota((half_rows, rows * SUB), 0) % SUB == iota((half_rows, rows * SUB), 1) % SUB
    group_of = iota((1, rows * SUB), 1) // half_rows
    for moment in range(tau_count):
        for row_group in range(orb_count):
            live = jnp.zeros((1, rows * SUB), jnp.int32)
            for col_group in range(orb_count):
                value = live_ref[(moment * orb_count + (me ^ row_group)) * orb_count + (me ^ col_group)]
                live = jnp.where(group_of == col_group, value, live)
            at = (moment * orb_count + row_group) * half_rows
            keep = jnp.logical_and(same, live != 0)
            mix_ref[at : at + half_rows, :] = jnp.where(keep, spread[at : at + half_rows], 0.0).astype(BF16)

    def step(index, carry):
        occ_halves, virt_halves = [], []
        for half in range(2):
            at = pl.multiple_of((index * 2 + half) * half_rows, half_rows)
            dense = jnp.concatenate([block[pl.ds(at, half_rows), :] for block in blocks], 0)
            occ_halves.append(dot(mix_ref[...], dense).reshape(tau_count * rows, SUB, tile))
            virt_halves.append(dot(dense, virt).reshape(rows, SUB, tau_count * tile))
        occ = jnp.concatenate(occ_halves, 1).astype(BF16)
        vir = jnp.concatenate(virt_halves, 1).astype(BF16)
        here = pl.ds(pl.multiple_of(index * PAIR, PAIR), PAIR)
        for moment in range(tau_count):
            for row in range(rows):
                at = (moment * rows + row) * tile
                occ_ref[here, at : at + tile] = occ[moment * rows + row]
                virt_out[here, at : at + tile] = vir[row, :, moment * tile : (moment + 1) * tile]
        return carry

    lax.fori_loop(0, steps, step, 0)
    chi = None
    depth = rows * tile
    part = min(depth, 4096)
    for moment in range(tau_count):
        for piece in range(depth // part):
            at = moment * depth + piece * part
            term = lax.dot_general(
                occ_ref[:, at : at + part], virt_out[:, at : at + part],
                (((1,), (1,)), ((), ())), preferred_element_type=F32,
            ) * tau_ref[moment]
            chi = term if chi is None else chi + term
    occ_rows = chi * (1.0 / math.sqrt(rows * tile * orb_count))
    hold = outs[0]
    funcs = occ_rows.shape[0]
    for distance, out in enumerate(outs):
        picked = occ_rows[0:share_rows]
        for owner in range(1, orb_count):
            picked = jnp.where(me ^ distance == owner, occ_rows[owner * share_rows : (owner + 1) * share_rows], picked)
        out[...] = picked


def on_device(b_rows, col_blocks, g_occ, occ_live, g_virt, tau_weight):
    orb_count = lax.axis_size("orb")
    aux_count = lax.axis_size("aux")
    aux_dev, rows_dev, slot_count, tile = b_rows.shape
    tau_count = g_occ.shape[0]
    rows = orb_count * rows_dev
    steps = aux_dev // PAIR
    share_rows = aux_dev // orb_count
    me = jnp.stack([lax.axis_index("orb"), lax.axis_index("aux")]).astype(jnp.int32)
    smem = pl.BlockSpec(memory_space=pltpu.SMEM)
    vmem = pl.BlockSpec(memory_space=pltpu.VMEM)
    occ_rows = tau_count * rows_dev
    block = jax.ShapeDtypeStruct((aux_dev * rows_dev + occ_rows, tile), BF16)
    blocks = pl.pallas_call(
        functools.partial(pack_kernel, orb_count, rows_dev, slot_count, steps),
        out_shape=[block] * orb_count,
        in_specs=[smem, smem, vmem, vmem],
        out_specs=[vmem] * orb_count,
        compiler_params=pltpu.CompilerParams(vmem_limit_bytes=32 << 20),
        name="pack",
    )(me, col_blocks, b_rows.reshape(-1, tile), g_occ.reshape(occ_rows, -1))
    dense = [blocks[0]]
    for distance in range(1, orb_count):
        dense.append(lax.ppermute(blocks[distance], "orb", [(i, i ^ distance) for i in range(orb_count)]))
    virt = g_virt.reshape(1, -1, tile)
    distance = 1
    while distance < aux_count:
        other = lax.ppermute(virt, "aux", [(i, i ^ distance) for i in range(aux_count)])
        virt = jnp.concatenate([virt, other], 0)
        distance *= 2
    shares = pl.pallas_call(
        functools.partial(work_kernel, orb_count, aux_count, rows_dev, tau_count, steps, share_rows),
        out_shape=[jax.ShapeDtypeStruct((share_rows, aux_dev), F32)] * orb_count,
        in_specs=[smem, smem, smem, vmem] + [vmem] * orb_count,
        out_specs=[vmem] * orb_count,
        scratch_shapes=[
            pltpu.VMEM((tau_count * rows * SUB, rows * SUB), BF16),
            pltpu.VMEM((aux_dev, tau_count * rows * tile), BF16),
            pltpu.VMEM((aux_dev, tau_count * rows * tile), BF16),
        ],
        compiler_params=pltpu.CompilerParams(vmem_limit_bytes=60 << 20),
        name="work",
    )(me, occ_live.reshape(-1), tau_weight, virt.reshape(-1, tile), *dense)
    total = shares[0]
    for distance in range(1, orb_count):
        total = total + lax.ppermute(shares[distance], "orb", [(i, i ^ distance) for i in range(orb_count)])
    return total


def solution(mesh):
    in_specs = (
        P("aux", "orb", None, None),
        P("orb", None),
        P(None, "orb", None),
        P(),
        P(None, "orb", "aux", None),
        P(),
    )
    out_specs = P("orb", "aux")
    return jax.shard_map(
        on_device, mesh=mesh, in_specs=in_specs, out_specs=out_specs, check_vma=False
    )
```

```python
import functools
import math

import jax
import jax.numpy as jnp
from jax import lax
from jax.experimental import pallas as pl
from jax.experimental.pallas import tpu as pltpu
from jax.sharding import PartitionSpec as P

SUB = 8
PAIR = 16
F32 = jnp.float32
BF16 = jnp.bfloat16


def iota(shape, dim):
    return lax.broadcasted_iota(jnp.int32, shape, dim)


def dot(a, b):
    return jnp.dot(a, b, preferred_element_type=F32)


def pack_kernel(rows_dev, slot_count, chunks, pieces, col_hbm, b_hbm, occ_hbm, *refs):
    orb_count = lax.axis_size("orb")
    count = len(chunks) * orb_count
    outs, helds = refs[:count], refs[count : 2 * count]
    b_ref, occ_ref, col_ref, b_sem, occ_sem, col_sem, out_sem = refs[2 * count :]
    me = lax.axis_index("orb")
    half_rows = rows_dev * SUB
    out_rows = 2 * half_rows
    in_rows = PAIR * rows_dev * slot_count
    steps = sum(chunks)
    piece_steps = steps // pieces
    piece_rows = piece_steps * in_rows

    def fetch(piece):
        here = pl.ds(piece * piece_rows, piece_rows)
        return pltpu.make_async_copy(b_hbm.at[here], b_ref.at[here], b_sem.at[piece])

    occ_copy = pltpu.make_async_copy(occ_hbm, occ_ref, occ_sem)
    col_copy = pltpu.make_async_copy(col_hbm, col_ref, col_sem)
    col_copy.start()
    for piece in range(pieces):
        fetch(piece).start()
    occ_copy.start()
    line = iota((out_rows, in_rows), 0)
    place = iota((out_rows, in_rows), 1)
    half = line // half_rows
    row = (line % half_rows) // SUB
    func = half * SUB + line % SUB
    first = (func * rows_dev + row) * slot_count
    pick = jnp.concatenate(
        [jnp.where(place == first + slot, 1.0, 0.0).astype(BF16) for slot in range(slot_count)], 0
    )
    occ_copy.wait()
    total = chunks[0] * out_rows
    for held in helds[:orb_count]:
        held[total:, :] = jnp.zeros((held.shape[0] - total, held.shape[1]), BF16)
        held[total:, : occ_ref.shape[1]] = occ_ref[...]
    col_copy.wait()

    def step(index, group, start):
        at = pl.multiple_of(index * in_rows, in_rows)
        moved = dot(pick, b_ref[pl.ds(at, in_rows), :]).astype(BF16)
        slots = [moved[slot * out_rows : (slot + 1) * out_rows] for slot in range(slot_count)]
        zero = jnp.zeros_like(slots[0])
        for distance, held in enumerate(group):
            value = zero
            for slot in range(slot_count):
                value = jnp.where(col_ref[0, slot] == me ^ distance, slots[slot], value)
            held[pl.ds(pl.multiple_of((index - start) * out_rows, out_rows), out_rows), :] = value

    sent = []
    start = 0
    for number, chunk in enumerate(chunks):
        group = range(number * orb_count, (number + 1) * orb_count)
        for piece in range(start // piece_steps, (start + chunk) // piece_steps):
            fetch(piece).wait()
            low = piece * piece_steps
            lax.fori_loop(
                low, low + piece_steps,
                lambda index, carry: (step(index, [helds[at] for at in group], start), carry)[1],
                0, unroll=True,
            )
            top = low - start + piece_steps
            low_row = (low - start) * out_rows
            high_row = helds[group[0]].shape[0] if top == chunk else top * out_rows
            for distance, at in enumerate(group):
                here = pl.ds(low_row, high_row - low_row)
                copy = pltpu.make_async_copy(helds[at].at[here], outs[at].at[here], out_sem.at[piece, distance])
                copy.start()
                sent.append(copy)
        start += chunk
    for copy in sent:
        copy.wait()


def join_kernel(one_ref, two_ref, out_ref):
    out_ref[: one_ref.shape[0], :] = one_ref[...]
    out_ref[one_ref.shape[0] :, :] = two_ref[...]


def order_virt(sizes, virt_refs, virt_out):
    orb_count, aux_count, rows_dev, tau_count = sizes
    aux_me = lax.axis_index("aux")
    tile = virt_refs[0].shape[1]
    part = tile // aux_count
    virt_all = jnp.concatenate([ref[...] for ref in virt_refs], 0)
    line = iota((tile, virt_all.shape[0]), 0)
    place = iota((tile, virt_all.shape[0]), 1)
    for moment in range(tau_count):
        wanted = (((line // part) ^ aux_me) * tau_count + moment) * part + line % part
        chosen = dot(jnp.where(place == wanted, 1.0, 0.0).astype(BF16), virt_all)
        virt_out[:, moment * tile : (moment + 1) * tile] = chosen.astype(BF16)


def spread_occ(sizes, live_ref, blocks, total, mix_out):
    orb_count, aux_count, rows_dev, tau_count = sizes
    me = lax.axis_index("orb")
    rows = orb_count * rows_dev
    half_rows = rows_dev * SUB
    tile = blocks[0].shape[1]
    occ_all = jnp.concatenate([block[total : total + tau_count * rows_dev, :] for block in blocks], 0)
    left_shape = (tau_count * rows * SUB, occ_all.shape[0])
    line = iota(left_shape, 0)
    moment_of = line // (rows * SUB)
    row_of = (line % (rows * SUB)) // SUB
    wanted = ((row_of // rows_dev) * tau_count + moment_of) * rows_dev + row_of % rows_dev
    left = jnp.where(iota(left_shape, 1) == wanted, 1.0, 0.0).astype(BF16)
    right_shape = (tile, rows * SUB)
    col_of = iota(right_shape, 1) // SUB
    wanted = ((col_of // rows_dev) ^ me) * rows_dev + col_of % rows_dev
    right = jnp.where(iota(right_shape, 0) == wanted, 1.0, 0.0).astype(BF16)
    spread = dot(dot(left, occ_all).astype(BF16), right)
    same = iota((half_rows, rows * SUB), 0) % SUB == iota((half_rows, rows * SUB), 1) % SUB
    group_of = iota((1, rows * SUB), 1) // half_rows
    for moment in range(tau_count):
        for row_group in range(orb_count):
            live = jnp.zeros((1, rows * SUB), jnp.int32)
            for col_group in range(orb_count):
                value = live_ref[moment, me ^ row_group, me ^ col_group]
                live = jnp.where(group_of == col_group, value, live)
            at = (moment * orb_count + row_group) * half_rows
            keep = jnp.logical_and(same, live != 0)
            mix_out[at : at + half_rows, :] = jnp.where(keep, spread[at : at + half_rows], 0.0).astype(BF16)


def products(sizes, steps, blocks, mix_ref, virt_ref, occ_out, vir_out):
    orb_count, aux_count, rows_dev, tau_count = sizes
    rows = orb_count * rows_dev
    half_rows = rows_dev * SUB
    tile = blocks[0].shape[1]

    def step(index, carry):
        here = pl.ds(pl.multiple_of(index * PAIR, PAIR), PAIR)
        halves = []
        for half in range(2):
            at = pl.multiple_of((index * 2 + half) * half_rows, half_rows)
            halves.append(jnp.concatenate([block[pl.ds(at, half_rows), :] for block in blocks], 0))
        if occ_out is not None:
            occ = dot(mix_ref[...], jnp.concatenate(halves, 1))
            occ = [occ[:, half * tile : (half + 1) * tile].reshape(tau_count * rows, SUB, tile) for half in range(2)]
            occ = jnp.concatenate(occ, 1).astype(BF16)
            for row in range(tau_count * rows):
                occ_out[here, row * tile : (row + 1) * tile] = occ[row]
        if vir_out is not None:
            vir = dot(jnp.concatenate(halves, 0), virt_ref[...]).reshape(2, rows, SUB, tau_count * tile)
            vir = jnp.concatenate([vir[0], vir[1]], 1).astype(BF16)
            for moment in range(tau_count):
                for row in range(rows):
                    at = (moment * rows + row) * tile
                    vir_out[here, at : at + tile] = vir[row, :, moment * tile : (moment + 1) * tile]
        return carry

    lax.fori_loop(0, steps, step, 0, unroll=2)


def occ_kernel(sizes, steps, live_ref, *refs):
    blocks, (mix_out, occ_out) = refs[: sizes[0]], refs[sizes[0] :]
    spread_occ(sizes, live_ref, blocks, steps * 2 * sizes[2] * SUB, mix_out)
    products(sizes, steps, blocks, mix_out, None, occ_out, None)


def vir_kernel(sizes, steps, *refs):
    blocks, virt_refs = refs[: sizes[0]], refs[sizes[0] : -3]
    anchor, virt_out, vir_out = refs[-3:]
    order_virt(sizes, virt_refs, virt_out)
    products(sizes, steps, blocks, None, virt_out, None, vir_out)


def last_kernel(sizes, steps, share_rows, tau_ref, mix_ref, virt_ref, occ_first, vir_first, *refs):
    orb_count, aux_count, rows_dev, tau_count = sizes
    blocks, outs = refs[:orb_count], refs[orb_count : 2 * orb_count]
    occ_last, vir_last = refs[2 * orb_count :]
    products(sizes, steps, blocks, mix_ref, virt_ref, occ_last, vir_last)
    me = lax.axis_index("orb")
    rows = orb_count * rows_dev
    tile = blocks[0].shape[1]
    depth = rows * tile
    part = min(depth, 4096)
    chi = None
    for moment in range(tau_count):
        for piece in range(depth // part):
            here = slice(moment * depth + piece * part, moment * depth + (piece + 1) * part)
            term = lax.dot_general(
                jnp.concatenate([occ_first[:, here], occ_last[:, here]], 0),
                jnp.concatenate([vir_first[:, here], vir_last[:, here]], 0),
                (((1,), (1,)), ((), ())), preferred_element_type=F32,
            ) * tau_ref[moment]
            chi = term if chi is None else chi + term
    chi = chi * (1.0 / math.sqrt(rows * tile * orb_count))
    for distance, out in enumerate(outs):
        picked = chi[0:share_rows]
        for owner in range(1, orb_count):
            picked = jnp.where(me ^ distance == owner, chi[owner * share_rows : (owner + 1) * share_rows], picked)
        out[...] = picked


def on_device(b_rows, col_blocks, g_occ, occ_live, g_virt, tau_weight):
    orb_count = lax.axis_size("orb")
    aux_count = lax.axis_size("aux")
    aux_dev, rows_dev, slot_count, tile = b_rows.shape
    tau_count = g_occ.shape[0]
    rows = orb_count * rows_dev
    share_rows = aux_dev // orb_count
    sizes = (orb_count, aux_count, rows_dev, tau_count)
    smem = pl.BlockSpec(memory_space=pltpu.SMEM)
    vmem = pl.BlockSpec(memory_space=pltpu.VMEM)

    def call(kernel, name, out_shape, in_specs, scratch, spare, out_spec=vmem):
        held = sum(math.prod(shape.shape) * 2 for shape in scratch if shape.dtype == BF16)
        return pl.pallas_call(
            kernel,
            out_shape=out_shape,
            in_specs=in_specs,
            out_specs=[out_spec] * len(out_shape),
            scratch_shapes=scratch,
            compiler_params=pltpu.CompilerParams(vmem_limit_bytes=min(held + (spare << 20), 60 << 20)),
            name=name,
        )

    def xor(value, axis, distance):
        return lax.ppermute(value, axis, [(i, i ^ distance) for i in range(lax.axis_size(axis))])

    def half(value):
        return jax.ShapeDtypeStruct(value, BF16)

    all_steps = aux_dev // PAIR
    chunks = (all_steps // 2, all_steps - all_steps // 2)
    occ_rows = tau_count * rows_dev
    b_flat = b_rows.reshape(-1, tile)
    occ_flat = g_occ.reshape(occ_rows, -1)
    hbm = pl.BlockSpec(memory_space=pl.ANY)
    pieces = math.gcd(4, all_steps)
    shapes = [
        (steps * PAIR * rows_dev + (0 if number else occ_rows), tile)
        for number, steps in enumerate(chunks) for _ in range(orb_count)
    ]
    blocks = call(
        functools.partial(pack_kernel, rows_dev, slot_count, chunks, pieces), "pack",
        [half(shape) for shape in shapes], [hbm] * 3,
        [pltpu.VMEM(shape, BF16) for shape in shapes] + [
            pltpu.VMEM(b_flat.shape, BF16), pltpu.VMEM(occ_flat.shape, BF16), pltpu.SMEM(col_blocks.shape, jnp.int32),
            pltpu.SemaphoreType.DMA((pieces,)), pltpu.SemaphoreType.DMA, pltpu.SemaphoreType.DMA,
            pltpu.SemaphoreType.DMA((pieces, orb_count)),
        ], 54, hbm,
    )(col_blocks, b_flat, occ_flat)
    dense = []
    for number in range(len(chunks)):
        own, *others = blocks[number * orb_count : (number + 1) * orb_count]
        dense.append([own] + [xor(value, "orb", d + 1) for d, value in enumerate(others)])
    virt = g_virt.reshape(-1, tile)
    virt = call(join_kernel, "join", [half((2 * virt.shape[0], tile))], [vmem] * 2, [], 2)(virt, xor(virt, "aux", 1))[0]
    virts = [virt] + [xor(virt, "aux", d) for d in range(2, aux_count, 2)]
    wide = half((chunks[0] * PAIR, tau_count * rows * tile))
    mix, occ_first = call(
        functools.partial(occ_kernel, sizes, chunks[0]), "occ",
        [half((tau_count * rows * SUB, rows * SUB)), wide],
        [smem] + [vmem] * orb_count, [], 8,
    )(occ_live, *dense[0])
    virt, vir_first = call(
        functools.partial(vir_kernel, sizes, chunks[0]), "vir",
        [half((tile, tau_count * tile)), wide],
        [vmem] * (orb_count + len(virts)) + [hbm], [], 8,
    )(*dense[0], *virts, mix)
    shares = call(
        functools.partial(last_kernel, sizes, chunks[1], share_rows), "last",
        [jax.ShapeDtypeStruct((share_rows, aux_dev), F32)] * orb_count,
        [smem] + [vmem] * (4 + orb_count),
        [pltpu.VMEM((chunks[1] * PAIR, tau_count * rows * tile), BF16)] * 2, 12,
    )(tau_weight, mix, virt, occ_first, vir_first, *dense[1])
    total = shares[0]
    for distance in range(1, orb_count):
        total = total + xor(shares[distance], "orb", distance)
    return total


def solution(mesh):
    in_specs = (
        P("aux", "orb", None, None),
        P("orb", None),
        P(None, "orb", None),
        P(),
        P(None, "orb", "aux", None),
        P(),
    )
    out_specs = P("orb", "aux")
    return jax.shard_map(
        on_device, mesh=mesh, in_specs=in_specs, out_specs=out_specs, check_vma=False
    )
```

```python
import functools
import math

import jax
import jax.numpy as jnp
from jax import lax
from jax.experimental import pallas as pl
from jax.experimental.pallas import tpu as pltpu
from jax.sharding import PartitionSpec as P

SUB = 8
PAIR = 16
F32 = jnp.float32
BF16 = jnp.bfloat16


def iota(shape, dim):
    return lax.broadcasted_iota(jnp.int32, shape, dim)


def dot(a, b):
    return jnp.dot(a, b, preferred_element_type=F32)


def partners(count):
    return [0] + sorted(range(1, count), key=lambda distance: (-distance.bit_count(), distance))


def pick_static(index, values):
    found = jnp.zeros_like(index)
    for place, value in enumerate(values):
        found = jnp.where(index == place, value, found)
    return found


def pack_kernel(rows_dev, slot_count, chunks, pieces, col_hbm, b_hbm, occ_hbm, *refs):
    orb_count = lax.axis_size("orb")
    count = len(chunks) * orb_count
    outs, helds = refs[:count], refs[count : 2 * count]
    b_ref, occ_ref, col_ref, b_sem, occ_sem, col_sem, out_sem = refs[2 * count :]
    me = lax.axis_index("orb")
    half_rows = rows_dev * SUB
    out_rows = 2 * half_rows
    in_rows = PAIR * rows_dev * slot_count
    steps = sum(chunks)
    piece_steps = steps // pieces
    piece_rows = piece_steps * in_rows

    def fetch(piece):
        here = pl.ds(piece * piece_rows, piece_rows)
        return pltpu.make_async_copy(b_hbm.at[here], b_ref.at[here], b_sem.at[piece])

    occ_copy = pltpu.make_async_copy(occ_hbm, occ_ref, occ_sem)
    col_copy = pltpu.make_async_copy(col_hbm, col_ref, col_sem)
    col_copy.start()
    for piece in range(pieces):
        fetch(piece).start()
    occ_copy.start()
    line = iota((out_rows, in_rows), 0)
    place = iota((out_rows, in_rows), 1)
    half = line // half_rows
    row = (line % half_rows) // SUB
    func = half * SUB + line % SUB
    first = (func * rows_dev + row) * slot_count
    pick = jnp.concatenate(
        [jnp.where(place == first + slot, 1.0, 0.0).astype(BF16) for slot in range(slot_count)], 0
    )
    occ_copy.wait()
    total = chunks[0] * out_rows
    for held in helds[:orb_count]:
        held[total:, :] = jnp.zeros((held.shape[0] - total, held.shape[1]), BF16)
        held[total:, : occ_ref.shape[1]] = occ_ref[...]
    col_copy.wait()

    def step(index, group, start):
        at = pl.multiple_of(index * in_rows, in_rows)
        moved = dot(pick, b_ref[pl.ds(at, in_rows), :]).astype(BF16)
        slots = [moved[slot * out_rows : (slot + 1) * out_rows] for slot in range(slot_count)]
        zero = jnp.zeros_like(slots[0])
        for distance, held in zip(partners(orb_count), group):
            value = zero
            for slot in range(slot_count):
                value = jnp.where(col_ref[0, slot] == me ^ distance, slots[slot], value)
            held[pl.ds(pl.multiple_of((index - start) * out_rows, out_rows), out_rows), :] = value

    sent = []
    start = 0
    for number, chunk in enumerate(chunks):
        group = range(number * orb_count, (number + 1) * orb_count)
        for piece in range(start // piece_steps, (start + chunk) // piece_steps):
            fetch(piece).wait()
            low = piece * piece_steps
            lax.fori_loop(
                low, low + piece_steps,
                lambda index, carry: (step(index, [helds[at] for at in group], start), carry)[1],
                0, unroll=True,
            )
            top = low - start + piece_steps
            low_row = (low - start) * out_rows
            high_row = helds[group[0]].shape[0] if top == chunk else top * out_rows
            for place, at in enumerate(group):
                here = pl.ds(low_row, high_row - low_row)
                copy = pltpu.make_async_copy(helds[at].at[here], outs[at].at[here], out_sem.at[piece, place])
                copy.start()
                sent.append(copy)
        start += chunk
    for copy in sent:
        copy.wait()


def stage_kernel(orb_count, own_count, live_hbm, one_ref, two_ref, *refs):
    owns, outs = refs[:own_count], refs[own_count : 2 * own_count]
    live_out, join_out, live_ref, live_sem, own_sem = refs[2 * own_count :]
    live_copy = pltpu.make_async_copy(live_hbm, live_ref, live_sem)
    live_copy.start()
    copies = [pltpu.make_async_copy(own, out, own_sem.at[at]) for at, (own, out) in enumerate(zip(owns, outs))]
    for copy in copies:
        copy.start()
    join_out[: one_ref.shape[0], :] = one_ref[...]
    join_out[one_ref.shape[0] :, :] = two_ref[...]
    live_copy.wait()
    me = lax.axis_index("orb")
    order = partners(orb_count)
    tau_count = live_ref.shape[0]
    width = live_out.shape[1]
    group_of = iota((1, width), 1) // (width // orb_count)
    for moment in range(tau_count):
        for row_group in range(orb_count):
            live = jnp.zeros((1, width), jnp.int32)
            for col_group in range(orb_count):
                value = live_ref[moment, me ^ order[row_group], me ^ order[col_group]]
                live = jnp.where(group_of == col_group, value, live)
            at = moment * orb_count + row_group
            live_out[at : at + 1, :] = live
    for copy in copies:
        copy.wait()


def join_kernel(one_ref, two_ref, out_ref):
    out_ref[: one_ref.shape[0], :] = one_ref[...]
    out_ref[one_ref.shape[0] :, :] = two_ref[...]


def order_virt(sizes, virt_refs, virt_out):
    orb_count, aux_count, rows_dev, tau_count = sizes
    aux_me = lax.axis_index("aux")
    tile = virt_refs[0].shape[1]
    part = tile // aux_count
    virt_all = jnp.concatenate([ref[...] for ref in virt_refs], 0)
    line = iota((tile, virt_all.shape[0]), 0)
    place = iota((tile, virt_all.shape[0]), 1)
    for moment in range(tau_count):
        wanted = (((line // part) ^ aux_me) * tau_count + moment) * part + line % part
        chosen = dot(jnp.where(place == wanted, 1.0, 0.0).astype(BF16), virt_all)
        virt_out[:, moment * tile : (moment + 1) * tile] = chosen.astype(BF16)


def spread_occ(sizes, live_ref, blocks, total, mix_out):
    orb_count, aux_count, rows_dev, tau_count = sizes
    me = lax.axis_index("orb")
    rows = orb_count * rows_dev
    half_rows = rows_dev * SUB
    tile = blocks[0].shape[1]
    occ_all = jnp.concatenate([block[total : total + tau_count * rows_dev, :] for block in blocks], 0)
    left_shape = (tau_count * rows * SUB, occ_all.shape[0])
    line = iota(left_shape, 0)
    moment_of = line // (rows * SUB)
    row_of = (line % (rows * SUB)) // SUB
    wanted = ((row_of // rows_dev) * tau_count + moment_of) * rows_dev + row_of % rows_dev
    left = jnp.where(iota(left_shape, 1) == wanted, 1.0, 0.0).astype(BF16)
    right_shape = (tile, rows * SUB)
    col_of = iota(right_shape, 1) // SUB
    group = pick_static(col_of // rows_dev, partners(orb_count)) ^ me
    wanted = group * rows_dev + col_of % rows_dev
    right = jnp.where(iota(right_shape, 0) == wanted, 1.0, 0.0).astype(BF16)
    spread = dot(dot(left, occ_all).astype(BF16), right)
    same = iota((half_rows, rows * SUB), 0) % SUB == iota((half_rows, rows * SUB), 1) % SUB
    for at in range(tau_count * orb_count):
        here = slice(at * half_rows, (at + 1) * half_rows)
        keep = jnp.logical_and(same, live_ref[at : at + 1, :] != 0)
        mix_out[here, :] = jnp.where(keep, spread[here], 0.0).astype(BF16)


def products(sizes, steps, blocks, mix_ref, virt_ref, occ_out, vir_out):
    orb_count, aux_count, rows_dev, tau_count = sizes
    rows = orb_count * rows_dev
    half_rows = rows_dev * SUB
    tile = blocks[0].shape[1]

    def step(index, carry):
        here = pl.ds(pl.multiple_of(index * PAIR, PAIR), PAIR)
        halves = []
        for half in range(2):
            at = pl.multiple_of((index * 2 + half) * half_rows, half_rows)
            halves.append(jnp.concatenate([block[pl.ds(at, half_rows), :] for block in blocks], 0))
        if occ_out is not None:
            occ = dot(mix_ref[...], jnp.concatenate(halves, 1))
            occ = [occ[:, half * tile : (half + 1) * tile].reshape(tau_count * rows, SUB, tile) for half in range(2)]
            occ = jnp.concatenate(occ, 1).astype(BF16)
            for row in range(tau_count * rows):
                occ_out[here, row * tile : (row + 1) * tile] = occ[row]
        if vir_out is not None:
            vir = dot(jnp.concatenate(halves, 0), virt_ref[...]).reshape(2, rows, SUB, tau_count * tile)
            vir = jnp.concatenate([vir[0], vir[1]], 1).astype(BF16)
            for moment in range(tau_count):
                for row in range(rows):
                    at = (moment * rows + row) * tile
                    vir_out[here, at : at + tile] = vir[row, :, moment * tile : (moment + 1) * tile]
        return carry

    lax.fori_loop(0, steps, step, 0, unroll=2)


def occ_kernel(sizes, steps, live_ref, *refs):
    blocks, (mix_out, occ_out) = refs[: sizes[0]], refs[sizes[0] :]
    spread_occ(sizes, live_ref, blocks, steps * 2 * sizes[2] * SUB, mix_out)
    products(sizes, steps, blocks, mix_out, None, occ_out, None)


def vir_kernel(sizes, steps, *refs):
    blocks, virt_refs = refs[: sizes[0]], refs[sizes[0] : -3]
    anchor, virt_out, vir_out = refs[-3:]
    order_virt(sizes, virt_refs, virt_out)
    products(sizes, steps, blocks, None, virt_out, None, vir_out)


def last_kernel(sizes, steps, share_rows, tau_ref, mix_ref, virt_ref, occ_first, vir_first, *refs):
    orb_count, aux_count, rows_dev, tau_count = sizes
    blocks, outs = refs[:orb_count], refs[orb_count : 2 * orb_count]
    occ_last, vir_last = refs[2 * orb_count :]
    products(sizes, steps, blocks, mix_ref, virt_ref, occ_last, vir_last)
    me = lax.axis_index("orb")
    rows = orb_count * rows_dev
    tile = blocks[0].shape[1]
    depth = rows * tile
    part = min(depth, 4096)
    chi = None
    for moment in range(tau_count):
        for piece in range(depth // part):
            here = slice(moment * depth + piece * part, moment * depth + (piece + 1) * part)
            term = lax.dot_general(
                jnp.concatenate([occ_first[:, here], occ_last[:, here]], 0),
                jnp.concatenate([vir_first[:, here], vir_last[:, here]], 0),
                (((1,), (1,)), ((), ())), preferred_element_type=F32,
            ) * tau_ref[moment]
            chi = term if chi is None else chi + term
    chi = chi * (1.0 / math.sqrt(rows * tile * orb_count))
    for distance, out in zip(partners(orb_count), outs):
        picked = chi[0:share_rows]
        for owner in range(1, orb_count):
            picked = jnp.where(me ^ distance == owner, chi[owner * share_rows : (owner + 1) * share_rows], picked)
        out[...] = picked


def on_device(b_rows, col_blocks, g_occ, occ_live, g_virt, tau_weight):
    orb_count = lax.axis_size("orb")
    aux_count = lax.axis_size("aux")
    aux_dev, rows_dev, slot_count, tile = b_rows.shape
    tau_count = g_occ.shape[0]
    rows = orb_count * rows_dev
    share_rows = aux_dev // orb_count
    sizes = (orb_count, aux_count, rows_dev, tau_count)
    smem = pl.BlockSpec(memory_space=pltpu.SMEM)
    vmem = pl.BlockSpec(memory_space=pltpu.VMEM)

    def call(kernel, name, out_shape, in_specs, scratch, spare, out_spec=vmem):
        held = sum(math.prod(shape.shape) * 2 for shape in scratch if shape.dtype == BF16)
        return pl.pallas_call(
            kernel,
            out_shape=out_shape,
            in_specs=in_specs,
            out_specs=[out_spec] * len(out_shape),
            scratch_shapes=scratch,
            compiler_params=pltpu.CompilerParams(vmem_limit_bytes=min(held + (spare << 20), 60 << 20)),
            name=name,
        )

    def xor(value, axis, distance):
        return lax.ppermute(value, axis, [(i, i ^ distance) for i in range(lax.axis_size(axis))])

    def half(value):
        return jax.ShapeDtypeStruct(value, BF16)

    all_steps = aux_dev // PAIR
    chunks = (all_steps * 12 // 16, all_steps - all_steps * 12 // 16)
    occ_rows = tau_count * rows_dev
    b_flat = b_rows.reshape(-1, tile)
    occ_flat = g_occ.reshape(occ_rows, -1)
    hbm = pl.BlockSpec(memory_space=pl.ANY)
    pieces = math.gcd(4, all_steps)
    shapes = [
        (steps * PAIR * rows_dev + (0 if number else occ_rows), tile)
        for number, steps in enumerate(chunks) for _ in range(orb_count)
    ]
    blocks = call(
        functools.partial(pack_kernel, rows_dev, slot_count, chunks, pieces), "pack",
        [half(shape) for shape in shapes], [hbm] * 3,
        [pltpu.VMEM(shape, BF16) for shape in shapes] + [
            pltpu.VMEM(b_flat.shape, BF16), pltpu.VMEM(occ_flat.shape, BF16), pltpu.SMEM(col_blocks.shape, jnp.int32),
            pltpu.SemaphoreType.DMA((pieces,)), pltpu.SemaphoreType.DMA, pltpu.SemaphoreType.DMA,
            pltpu.SemaphoreType.DMA((pieces, orb_count)),
        ], 54, hbm,
    )(col_blocks, b_flat, occ_flat)
    order = partners(orb_count)
    dense = []
    for number in range(len(chunks)):
        own, *others = blocks[number * orb_count : (number + 1) * orb_count]
        dense.append([own] + [xor(value, "orb", d) for d, value in zip(order[1:], others)])
    virt = g_virt.reshape(-1, tile)
    owns = [blocks[number * orb_count] for number in range(len(chunks))]
    *owns, live, virt = call(
        functools.partial(stage_kernel, orb_count, len(chunks)), "stage",
        [half(own.shape) for own in owns]
        + [jax.ShapeDtypeStruct((tau_count * orb_count, rows * SUB), jnp.int32), half((2 * virt.shape[0], tile))],
        [hbm, vmem, vmem] + [hbm] * len(owns),
        [pltpu.SMEM(occ_live.shape, jnp.int32), pltpu.SemaphoreType.DMA, pltpu.SemaphoreType.DMA((len(owns),))], 4,
    )(occ_live, virt, xor(virt, "aux", 1), *owns)
    for own, group in zip(owns, dense):
        group[0] = own
    distance = 2
    while distance < aux_count:
        pair = half((2 * virt.shape[0], tile))
        virt = call(join_kernel, "join", [pair], [vmem] * 2, [], 2)(virt, xor(virt, "aux", distance))[0]
        distance *= 2
    virts = [virt]
    wide = half((chunks[0] * PAIR, tau_count * rows * tile))
    mix, occ_first = call(
        functools.partial(occ_kernel, sizes, chunks[0]), "occ",
        [half((tau_count * rows * SUB, rows * SUB)), wide],
        [vmem] * (1 + orb_count), [], 8,
    )(live, *dense[0])
    virt, vir_first = call(
        functools.partial(vir_kernel, sizes, chunks[0]), "vir",
        [half((tile, tau_count * tile)), wide],
        [vmem] * (orb_count + len(virts)) + [hbm], [], 8,
    )(*dense[0], *virts, mix)
    shares = call(
        functools.partial(last_kernel, sizes, chunks[1], share_rows), "last",
        [jax.ShapeDtypeStruct((share_rows, aux_dev), F32)] * orb_count,
        [smem] + [vmem] * (4 + orb_count),
        [pltpu.VMEM((chunks[1] * PAIR, tau_count * rows * tile), BF16)] * 2, 12,
    )(tau_weight, mix, virt, occ_first, vir_first, *dense[1])
    total = shares[0]
    for distance, share in zip(order[1:], shares[1:]):
        total = total + xor(share, "orb", distance)
    return total


def solution(mesh):
    in_specs = (
        P("aux", "orb", None, None),
        P("orb", None),
        P(None, "orb", None),
        P(),
        P(None, "orb", "aux", None),
        P(),
    )
    out_specs = P("orb", "aux")
    return jax.shard_map(
        on_device, mesh=mesh, in_specs=in_specs, out_specs=out_specs, check_vma=False
    )
```

```python
import functools
import math

import jax
import jax.numpy as jnp
from jax import lax
from jax.experimental import pallas as pl
from jax.experimental.pallas import tpu as pltpu
from jax.sharding import PartitionSpec as P

SUB = 8
PAIR = 16
UNROLL = 16
F32 = jnp.float32
BF16 = jnp.bfloat16


def iota(shape, dim):
    return lax.broadcasted_iota(jnp.int32, shape, dim)


def dot(a, b):
    return jnp.dot(a, b, preferred_element_type=F32)


def partners(count):
    return [0] + sorted(range(1, count), key=lambda distance: (-distance.bit_count(), distance))


def pick_static(index, values):
    found = jnp.zeros_like(index)
    for place, value in enumerate(values):
        found = jnp.where(index == place, value, found)
    return found


def pack_kernel(rows_dev, slot_count, chunks, pieces, col_hbm, b_hbm, occ_hbm, *refs):
    orb_count = lax.axis_size("orb")
    count = len(chunks) * orb_count
    outs, helds = refs[:count], refs[count : 2 * count]
    b_ref, occ_ref, col_ref, b_sem, occ_sem, col_sem, out_sem = refs[2 * count :]
    me = lax.axis_index("orb")
    half_rows = rows_dev * SUB
    out_rows = 2 * half_rows
    in_rows = PAIR * rows_dev * slot_count
    steps = sum(chunks)
    piece_steps = steps // pieces
    piece_rows = piece_steps * in_rows

    def fetch(piece):
        here = pl.ds(piece * piece_rows, piece_rows)
        return pltpu.make_async_copy(b_hbm.at[here], b_ref.at[here], b_sem.at[piece])

    occ_copy = pltpu.make_async_copy(occ_hbm, occ_ref, occ_sem)
    col_copy = pltpu.make_async_copy(col_hbm, col_ref, col_sem)
    col_copy.start()
    for piece in range(pieces):
        fetch(piece).start()
    occ_copy.start()
    line = iota((out_rows, in_rows), 0)
    place = iota((out_rows, in_rows), 1)
    half = line // half_rows
    row = (line % half_rows) // SUB
    func = half * SUB + line % SUB
    first = (func * rows_dev + row) * slot_count
    pick = jnp.concatenate(
        [jnp.where(place == first + slot, 1.0, 0.0).astype(BF16) for slot in range(slot_count)], 0
    )
    occ_copy.wait()
    total = chunks[0] * out_rows
    for held in helds[:orb_count]:
        held[total:, :] = jnp.zeros((held.shape[0] - total, held.shape[1]), BF16)
        held[total:, : occ_ref.shape[1]] = occ_ref[...]
    col_copy.wait()

    def step(index, group, start):
        at = pl.multiple_of(index * in_rows, in_rows)
        moved = dot(pick, b_ref[pl.ds(at, in_rows), :]).astype(BF16)
        slots = [moved[slot * out_rows : (slot + 1) * out_rows] for slot in range(slot_count)]
        zero = jnp.zeros_like(slots[0])
        for distance, held in zip(partners(orb_count), group):
            value = zero
            for slot in range(slot_count):
                value = jnp.where(col_ref[0, slot] == me ^ distance, slots[slot], value)
            held[pl.ds(pl.multiple_of((index - start) * out_rows, out_rows), out_rows), :] = value

    sent = []
    start = 0
    for number, chunk in enumerate(chunks):
        group = range(number * orb_count, (number + 1) * orb_count)
        for piece in range(start // piece_steps, (start + chunk) // piece_steps):
            fetch(piece).wait()
            low = piece * piece_steps
            lax.fori_loop(
                low, low + piece_steps,
                lambda index, carry: (step(index, [helds[at] for at in group], start), carry)[1],
                0, unroll=True,
            )
            top = low - start + piece_steps
            low_row = (low - start) * out_rows
            high_row = helds[group[0]].shape[0] if top == chunk else top * out_rows
            for place, at in enumerate(group):
                here = pl.ds(low_row, high_row - low_row)
                copy = pltpu.make_async_copy(helds[at].at[here], outs[at].at[here], out_sem.at[piece, place])
                copy.start()
                sent.append(copy)
        start += chunk
    for copy in sent:
        copy.wait()


def stage_kernel(orb_count, own_count, live_hbm, one_ref, two_ref, *refs):
    owns, outs = refs[:own_count], refs[own_count : 2 * own_count]
    live_out, join_out, live_ref, live_sem, own_sem = refs[2 * own_count :]
    live_copy = pltpu.make_async_copy(live_hbm, live_ref, live_sem)
    live_copy.start()
    copies = [pltpu.make_async_copy(own, out, own_sem.at[at]) for at, (own, out) in enumerate(zip(owns, outs))]
    for copy in copies:
        copy.start()
    join_out[: one_ref.shape[0], :] = one_ref[...]
    join_out[one_ref.shape[0] :, :] = two_ref[...]
    live_copy.wait()
    me = lax.axis_index("orb")
    order = partners(orb_count)
    tau_count = live_ref.shape[0]
    width = live_out.shape[1]
    group_of = iota((1, width), 1) // (width // orb_count)
    for moment in range(tau_count):
        for row_group in range(orb_count):
            live = jnp.zeros((1, width), jnp.int32)
            for col_group in range(orb_count):
                value = live_ref[moment, me ^ order[row_group], me ^ order[col_group]]
                live = jnp.where(group_of == col_group, value, live)
            at = moment * orb_count + row_group
            live_out[at : at + 1, :] = live
    for copy in copies:
        copy.wait()


def join_kernel(one_ref, two_ref, out_ref):
    out_ref[: one_ref.shape[0], :] = one_ref[...]
    out_ref[one_ref.shape[0] :, :] = two_ref[...]


def order_virt(sizes, virt_refs, virt_out):
    orb_count, aux_count, rows_dev, tau_count = sizes
    aux_me = lax.axis_index("aux")
    tile = virt_refs[0].shape[1]
    part = tile // aux_count
    virt_all = jnp.concatenate([ref[...] for ref in virt_refs], 0)
    line = iota((tile, virt_all.shape[0]), 0)
    place = iota((tile, virt_all.shape[0]), 1)
    for moment in range(tau_count):
        wanted = (((line // part) ^ aux_me) * tau_count + moment) * part + line % part
        chosen = dot(jnp.where(place == wanted, 1.0, 0.0).astype(BF16), virt_all)
        virt_out[:, moment * tile : (moment + 1) * tile] = chosen.astype(BF16)


def spread_occ(sizes, live_ref, blocks, total, mix_out):
    orb_count, aux_count, rows_dev, tau_count = sizes
    me = lax.axis_index("orb")
    rows = orb_count * rows_dev
    half_rows = rows_dev * SUB
    tile = blocks[0].shape[1]
    occ_all = jnp.concatenate([block[total : total + tau_count * rows_dev, :] for block in blocks], 0)
    left_shape = (tau_count * rows * SUB, occ_all.shape[0])
    line = iota(left_shape, 0)
    moment_of = line // (rows * SUB)
    row_of = (line % (rows * SUB)) // SUB
    wanted = ((row_of // rows_dev) * tau_count + moment_of) * rows_dev + row_of % rows_dev
    left = jnp.where(iota(left_shape, 1) == wanted, 1.0, 0.0).astype(BF16)
    right_shape = (tile, rows * SUB)
    col_of = iota(right_shape, 1) // SUB
    group = pick_static(col_of // rows_dev, partners(orb_count)) ^ me
    wanted = group * rows_dev + col_of % rows_dev
    right = jnp.where(iota(right_shape, 0) == wanted, 1.0, 0.0).astype(BF16)
    spread = dot(dot(left, occ_all).astype(BF16), right)
    same = iota((half_rows, rows * SUB), 0) % SUB == iota((half_rows, rows * SUB), 1) % SUB
    for at in range(tau_count * orb_count):
        here = slice(at * half_rows, (at + 1) * half_rows)
        keep = jnp.logical_and(same, live_ref[at : at + 1, :] != 0)
        mix_out[here, :] = jnp.where(keep, spread[here], 0.0).astype(BF16)


def products(sizes, steps, blocks, mix_ref, virt_ref, occ_out, vir_out):
    orb_count, aux_count, rows_dev, tau_count = sizes
    rows = orb_count * rows_dev
    half_rows = rows_dev * SUB
    tile = blocks[0].shape[1]

    def step(index, carry):
        here = pl.ds(pl.multiple_of(index * PAIR, PAIR), PAIR)
        halves = []
        for half in range(2):
            at = pl.multiple_of((index * 2 + half) * half_rows, half_rows)
            halves.append(jnp.concatenate([block[pl.ds(at, half_rows), :] for block in blocks], 0))
        if occ_out is not None:
            occ = dot(mix_ref[...], jnp.concatenate(halves, 1))
            occ = [occ[:, half * tile : (half + 1) * tile].reshape(tau_count * rows, SUB, tile) for half in range(2)]
            occ = jnp.concatenate(occ, 1).astype(BF16)
            for row in range(tau_count * rows):
                occ_out[here, row * tile : (row + 1) * tile] = occ[row]
        if vir_out is not None:
            vir = dot(jnp.concatenate(halves, 0), virt_ref[...]).reshape(2, rows, SUB, tau_count * tile)
            vir = jnp.concatenate([vir[0], vir[1]], 1).astype(BF16)
            for moment in range(tau_count):
                for row in range(rows):
                    at = (moment * rows + row) * tile
                    vir_out[here, at : at + tile] = vir[row, :, moment * tile : (moment + 1) * tile]
        return carry

    lax.fori_loop(0, steps, step, 0, unroll=min(steps, UNROLL))


def occ_kernel(sizes, steps, live_ref, *refs):
    blocks, (mix_out, occ_out) = refs[: sizes[0]], refs[sizes[0] :]
    spread_occ(sizes, live_ref, blocks, steps * 2 * sizes[2] * SUB, mix_out)
    products(sizes, steps, blocks, mix_out, None, occ_out, None)


def vir_kernel(sizes, steps, *refs):
    blocks, virt_refs = refs[: sizes[0]], refs[sizes[0] : -3]
    anchor, virt_out, vir_out = refs[-3:]
    order_virt(sizes, virt_refs, virt_out)
    products(sizes, steps, blocks, None, virt_out, None, vir_out)


def last_kernel(sizes, steps, share_rows, tau_ref, mix_ref, virt_ref, occ_first, vir_first, *refs):
    orb_count, aux_count, rows_dev, tau_count = sizes
    blocks, outs = refs[:orb_count], refs[orb_count : 2 * orb_count]
    occ_last, vir_last = refs[2 * orb_count :]
    products(sizes, steps, blocks, mix_ref, virt_ref, occ_last, vir_last)
    me = lax.axis_index("orb")
    rows = orb_count * rows_dev
    tile = blocks[0].shape[1]
    depth = rows * tile
    part = min(depth, 4096)
    chi = None
    for moment in range(tau_count):
        for piece in range(depth // part):
            here = slice(moment * depth + piece * part, moment * depth + (piece + 1) * part)
            term = lax.dot_general(
                jnp.concatenate([occ_first[:, here], occ_last[:, here]], 0),
                jnp.concatenate([vir_first[:, here], vir_last[:, here]], 0),
                (((1,), (1,)), ((), ())), preferred_element_type=F32,
            ) * tau_ref[moment]
            chi = term if chi is None else chi + term
    chi = chi * (1.0 / math.sqrt(rows * tile * orb_count))
    for distance, out in zip(partners(orb_count), outs):
        picked = chi[0:share_rows]
        for owner in range(1, orb_count):
            picked = jnp.where(me ^ distance == owner, chi[owner * share_rows : (owner + 1) * share_rows], picked)
        out[...] = picked


def on_device_dense(b_rows, col_blocks, g_occ, occ_live, g_virt, tau_weight):
    orb_count = lax.axis_size("orb")
    aux_count = lax.axis_size("aux")
    aux_dev, rows_dev, slot_count, tile = b_rows.shape
    tau_count = g_occ.shape[0]
    rows = orb_count * rows_dev
    share_rows = aux_dev // orb_count
    sizes = (orb_count, aux_count, rows_dev, tau_count)
    smem = pl.BlockSpec(memory_space=pltpu.SMEM)
    vmem = pl.BlockSpec(memory_space=pltpu.VMEM)

    def call(kernel, name, out_shape, in_specs, scratch, spare, out_spec=vmem):
        held = sum(math.prod(shape.shape) * 2 for shape in scratch if shape.dtype == BF16)
        return pl.pallas_call(
            kernel,
            out_shape=out_shape,
            in_specs=in_specs,
            out_specs=[out_spec] * len(out_shape),
            scratch_shapes=scratch,
            compiler_params=pltpu.CompilerParams(vmem_limit_bytes=min(held + (spare << 20), 60 << 20)),
            name=name,
        )

    def xor(value, axis, distance):
        return lax.ppermute(value, axis, [(i, i ^ distance) for i in range(lax.axis_size(axis))])

    def half(value):
        return jax.ShapeDtypeStruct(value, BF16)

    all_steps = aux_dev // PAIR
    chunks = (all_steps * 12 // 16, all_steps - all_steps * 12 // 16)
    occ_rows = tau_count * rows_dev
    b_flat = b_rows.reshape(-1, tile)
    occ_flat = g_occ.reshape(occ_rows, -1)
    hbm = pl.BlockSpec(memory_space=pl.ANY)
    pieces = math.gcd(4, all_steps)
    shapes = [
        (steps * PAIR * rows_dev + (0 if number else occ_rows), tile)
        for number, steps in enumerate(chunks) for _ in range(orb_count)
    ]
    blocks = call(
        functools.partial(pack_kernel, rows_dev, slot_count, chunks, pieces), "pack",
        [half(shape) for shape in shapes], [hbm] * 3,
        [pltpu.VMEM(shape, BF16) for shape in shapes] + [
            pltpu.VMEM(b_flat.shape, BF16), pltpu.VMEM(occ_flat.shape, BF16), pltpu.SMEM(col_blocks.shape, jnp.int32),
            pltpu.SemaphoreType.DMA((pieces,)), pltpu.SemaphoreType.DMA, pltpu.SemaphoreType.DMA,
            pltpu.SemaphoreType.DMA((pieces, orb_count)),
        ], 54, hbm,
    )(col_blocks, b_flat, occ_flat)
    order = partners(orb_count)
    dense = []
    for number in range(len(chunks)):
        own, *others = blocks[number * orb_count : (number + 1) * orb_count]
        dense.append([own] + [xor(value, "orb", d) for d, value in zip(order[1:], others)])
    virt = g_virt.reshape(-1, tile)
    owns = [blocks[number * orb_count] for number in range(len(chunks))]
    *owns, live, virt = call(
        functools.partial(stage_kernel, orb_count, len(chunks)), "stage",
        [half(own.shape) for own in owns]
        + [jax.ShapeDtypeStruct((tau_count * orb_count, rows * SUB), jnp.int32), half((2 * virt.shape[0], tile))],
        [hbm, vmem, vmem] + [hbm] * len(owns),
        [pltpu.SMEM(occ_live.shape, jnp.int32), pltpu.SemaphoreType.DMA, pltpu.SemaphoreType.DMA((len(owns),))], 4,
    )(occ_live, virt, xor(virt, "aux", 1), *owns)
    for own, group in zip(owns, dense):
        group[0] = own
    distance = 2
    while distance < aux_count:
        pair = half((2 * virt.shape[0], tile))
        virt = call(join_kernel, "join", [pair], [vmem] * 2, [], 2)(virt, xor(virt, "aux", distance))[0]
        distance *= 2
    virts = [virt]
    wide = half((chunks[0] * PAIR, tau_count * rows * tile))
    mix, occ_first = call(
        functools.partial(occ_kernel, sizes, chunks[0]), "occ",
        [half((tau_count * rows * SUB, rows * SUB)), wide],
        [vmem] * (1 + orb_count), [], 8,
    )(live, *dense[0])
    virt, vir_first = call(
        functools.partial(vir_kernel, sizes, chunks[0]), "vir",
        [half((tile, tau_count * tile)), wide],
        [vmem] * (orb_count + len(virts)) + [hbm], [], 8,
    )(*dense[0], *virts, mix)
    shares = call(
        functools.partial(last_kernel, sizes, chunks[1], share_rows), "last",
        [jax.ShapeDtypeStruct((share_rows, aux_dev), F32)] * orb_count,
        [smem] + [vmem] * (4 + orb_count),
        [pltpu.VMEM((chunks[1] * PAIR, tau_count * rows * tile), BF16)] * 2, 12,
    )(tau_weight, mix, virt, occ_first, vir_first, *dense[1])
    total = shares[0]
    for distance, share in zip(order[1:], shares[1:]):
        total = total + xor(share, "orb", distance)
    return total


class Message:
    def __init__(self, virt_rows, occ_rows):
        self.virt = slice(0, virt_rows)
        self.occ = slice(virt_rows, virt_rows + occ_rows)
        self.list = slice(virt_rows + occ_rows, virt_rows + occ_rows + 16)
        self.rows = virt_rows + occ_rows + 16


def equal(one, two):
    return jnp.where(one == two, 1.0, 0.0)


def at_group(group, values):
    found = values[0]
    for place in range(1, len(values)):
        found = jnp.where(group == place, values[place], found)
    return found


class Choice:
    def __init__(self, message, refs):
        me = lax.axis_index("orb")
        near = []
        for ref in refs:
            row = ref[message.list, :].astype(F32)[0:1, :]
            near.append([row[:, slot : slot + 1] for slot in range(2)])
        lists = [[at_group(me ^ group, [near[d][slot] for d in range(4)]) for slot in range(2)] for group in range(4)]
        shape = (8, 128)
        index = iota(shape, 0) * shape[1] + iota(shape, 1)
        bits = [((index >> place) & 1).astype(F32) for place in range(8)]
        sent_x = [lists[g][0] + bits[g] * (lists[g][1] - lists[g][0]) for g in range(4)]
        sent_y = [lists[g][0] + bits[4 + g] * (lists[g][1] - lists[g][0]) for g in range(4)]
        good = jnp.where(index < 256, 1.0, 0.0)
        for one, two in ((0, 1), (2, 3), (0, 2), (1, 3), (0, 3), (1, 2)):
            for slot in range(2):
                column = lists[one][slot]
                shared = jnp.maximum(equal(column, lists[two][0]), equal(column, lists[two][1]))
                if two == one ^ 1:
                    met = jnp.maximum(equal(sent_x[one], column), equal(sent_x[two], column))
                elif two == one ^ 2:
                    met = jnp.maximum(equal(sent_y[one], column), equal(sent_y[two], column))
                else:
                    met = jnp.maximum(
                        equal(sent_x[one], column) * equal(sent_y[two], column),
                        equal(sent_y[one], column) * equal(sent_x[two], column),
                    )
                good = good * jnp.maximum(met, 1.0 - shared)
        number = jnp.where(good > 0.5, index.astype(F32), 1024.0)
        number = jnp.min(jnp.min(number, axis=1, keepdims=True), axis=0, keepdims=True)
        chosen = []
        for place in range(8):
            rest = jnp.floor(number * (1.0 / (1 << place)))
            chosen.append(rest - 2.0 * jnp.floor(rest * 0.5))
        all_x = [lists[g][0] + chosen[g] * (lists[g][1] - lists[g][0]) for g in range(4)]
        all_y = [lists[g][0] + chosen[4 + g] * (lists[g][1] - lists[g][0]) for g in range(4)]
        self.own = at_group(me, [lists[g][0] for g in range(4)]), at_group(me, [lists[g][1] for g in range(4)])
        self.slot_x = at_group(me, chosen[:4])
        self.slot_y = at_group(me, chosen[4:])
        got_x, got_y = at_group(me ^ 1, all_x), at_group(me ^ 2, all_y)
        self.got = got_x, got_y
        one = jnp.ones_like(got_x)
        foreign = one - jnp.maximum(equal(got_x, self.own[0]), equal(got_x, self.own[1]))
        self.third = foreign * got_x + (one - foreign) * got_y
        first_x = jnp.where(me < (me ^ 1), one, one - equal(at_group(me, all_x), got_x))
        first_y = jnp.where(me < (me ^ 2), one, one - equal(at_group(me, all_y), got_y))
        also = equal(at_group(me ^ 2, all_x), got_x) * equal(at_group(me ^ 1, all_y), got_x)
        first_far = jnp.where(me < (me ^ 3), one, one - also)
        zero = jnp.zeros_like(one)
        with_x = [equal(got_x, column) * first_x for column in self.own]
        with_y = [equal(got_y, column) * first_y for column in self.own]
        far = equal(got_x, got_y) * first_far
        self.pairs = [
            [one, zero, with_x[0], with_y[0]],
            [zero, one, with_x[1], with_y[1]],
            [with_x[0], with_x[1], zero, far],
            [with_y[0], with_y[1], far, zero],
        ]


def message_kernel(message, virt_hbm, occ_hbm, col_hbm, out_hbm, out_ref, occ_ref, col_ref, sem):
    copies = [
        pltpu.make_async_copy(virt_hbm, out_ref.at[message.virt], sem.at[0]),
        pltpu.make_async_copy(occ_hbm, occ_ref, sem.at[1]),
        pltpu.make_async_copy(col_hbm, col_ref, sem.at[2]),
    ]
    for copy in copies:
        copy.start()
    tile = out_ref.shape[1]
    out_ref[message.occ, :] = jnp.zeros((occ_ref.shape[0], tile), BF16)
    for copy in copies:
        copy.wait()
    out_ref[message.occ, : occ_ref.shape[1]] = occ_ref[...]
    row, lane = iota((16, tile), 0), iota((16, tile), 1)
    value = jnp.zeros((16, tile), F32)
    for slot in range(col_ref.shape[1]):
        here = jnp.logical_and(row == 0, lane == slot)
        value = jnp.where(here, col_ref[0, slot].astype(F32), value)
    out_ref[message.list, :] = value.astype(BF16)
    copy = pltpu.make_async_copy(out_ref, out_hbm, sem.at[3])
    copy.start()
    copy.wait()


def own_kernel(rows_dev, steps, b_ref, *outs):
    half_rows = rows_dev * SUB
    out_rows = 2 * half_rows
    in_rows = PAIR * rows_dev * 2
    line = iota((out_rows, in_rows), 0)
    place = iota((out_rows, in_rows), 1)
    func = (line // half_rows) * SUB + line % SUB
    first = (func * rows_dev + (line % half_rows) // SUB) * 2
    pick = jnp.concatenate([jnp.where(place == first + slot, 1.0, 0.0).astype(BF16) for slot in range(2)], 0)
    for index in range(steps):
        moved = dot(pick, b_ref[index * in_rows : (index + 1) * in_rows, :]).astype(BF16)
        for slot, out in enumerate(outs):
            out[index * out_rows : (index + 1) * out_rows, :] = moved[slot * out_rows : (slot + 1) * out_rows]


def send_kernel(message, *refs):
    messages, (own0, own1, to_x, to_y, virt_out) = refs[:4], refs[4:]
    choice = Choice(message, messages)
    to_x[...] = jnp.where(choice.slot_x > 0.5, own1[...], own0[...])
    to_y[...] = jnp.where(choice.slot_y > 0.5, own1[...], own0[...])
    me = lax.axis_index("orb")
    rows = message.virt.stop
    for slot, column in enumerate((choice.own[0], choice.own[1], choice.third)):
        total = jnp.zeros((rows, virt_out.shape[1]), F32)
        for distance in range(4):
            weight = equal(column, (me ^ distance).astype(F32))
            total = total + weight * messages[distance][message.virt, :].astype(F32)
        virt_out[slot * rows : (slot + 1) * rows, :] = total.astype(BF16)


def aux_steps(aux_count):
    steps = []
    distance = aux_count // 2
    while distance:
        steps.append(distance)
        distance //= 2
    return steps


def aux_order(aux_count):
    order = [0]
    for distance in aux_steps(aux_count):
        order = order + [value ^ distance for value in order]
    return order


def virt_kernel(sizes, message, *refs):
    aux_count, rows_dev, tau_count = sizes
    messages, (virt_ref, virt_out) = refs[:4], refs[4:]
    choice = Choice(message, messages)
    aux_me = lax.axis_index("aux")
    tile = virt_ref.shape[1]
    part = tile // aux_count
    order = aux_order(aux_count)
    line = iota((tile, virt_ref.shape[0]), 0)
    place = iota((tile, virt_ref.shape[0]), 1)
    virts = []
    for slot in range(3):
        columns = []
        for moment in range(tau_count):
            held = pick_static((line // part) ^ aux_me, [order.index(value) for value in range(aux_count)])
            wanted = ((held * 3 + slot) * tau_count + moment) * part + line % part
            columns.append(dot(jnp.where(place == wanted, 1.0, 0.0).astype(BF16), virt_ref[...]))
        virts.append(jnp.concatenate(columns, 1))
    virt_out[0] = virts[0].astype(BF16)
    virt_out[1] = virts[1].astype(BF16)
    for at, column in enumerate(choice.got):
        one, two = equal(column, choice.own[0]), equal(column, choice.own[1])
        virt_out[2 + at] = (one * virts[0] + two * virts[1] + (1.0 - one - two) * virts[2]).astype(BF16)


def mix_kernel(sizes, message, live_ref, *refs):
    aux_count, rows_dev, tau_count = sizes
    messages, mix_out = refs[:4], refs[4]
    choice = Choice(message, messages)
    me = lax.axis_index("orb")
    tile = messages[0].shape[1]
    rows = 4 * rows_dev
    half_rows = rows_dev * SUB
    groups = [me, me, me ^ 1, me ^ 2]
    occ_all = jnp.concatenate([messages[at][message.occ, :] for at in (0, 0, 1, 2)], 0)
    left_shape = (tau_count * rows * SUB, occ_all.shape[0])
    line = iota(left_shape, 0)
    row_of = (line % (rows * SUB)) // SUB
    wanted = ((row_of // rows_dev) * tau_count + line // (rows * SUB)) * rows_dev + row_of % rows_dev
    left = jnp.where(iota(left_shape, 1) == wanted, 1.0, 0.0).astype(BF16)
    right_shape = (tile, rows * SUB)
    col_of = iota(right_shape, 1) // SUB
    wanted = pick_static(col_of // rows_dev, groups) * rows_dev + col_of % rows_dev
    right = jnp.where(iota(right_shape, 0) == wanted, 1.0, 0.0).astype(BF16)
    spread = dot(dot(left, occ_all).astype(BF16), right)
    same = iota((half_rows, rows * SUB), 0) % SUB == iota((half_rows, rows * SUB), 1) % SUB
    group_of = iota((1, rows * SUB), 1) // half_rows
    for moment in range(tau_count):
        for one in range(4):
            live = jnp.zeros((1, rows * SUB), F32)
            for two in range(4):
                value = live_ref[moment, groups[one], groups[two]].astype(F32) * choice.pairs[one][two]
                live = jnp.where(group_of == two, value, live)
            at = (moment * 4 + one) * half_rows
            keep = jnp.logical_and(same, live != 0.0)
            mix_out[at : at + half_rows, :] = jnp.where(keep, spread[at : at + half_rows], 0.0).astype(BF16)


def work_kernel(rows_dev, tau_count, steps, scale, tau_ref, mix_ref, virt_ref, *refs):
    blocks, outs, (occ_ref, vir_ref) = refs[:4], refs[4:8], refs[8:]
    rows = 4 * rows_dev
    half_rows = rows_dev * SUB
    tile = blocks[0].shape[1]

    def step(index, carry):
        here = pl.ds(pl.multiple_of(index * PAIR, PAIR), PAIR)
        halves = []
        for half in range(2):
            at = pl.multiple_of((index * 2 + half) * half_rows, half_rows)
            halves.append(jnp.concatenate([block[pl.ds(at, half_rows), :] for block in blocks], 0))
        occ = dot(mix_ref[...], jnp.concatenate(halves, 1))
        occ = [occ[:, half * tile : (half + 1) * tile].reshape(tau_count * rows, SUB, tile) for half in range(2)]
        occ = jnp.concatenate(occ, 1).astype(BF16)
        for row in range(tau_count * rows):
            occ_ref[here, row * tile : (row + 1) * tile] = occ[row]
        for group, block in enumerate(blocks):
            both = block[pl.ds(pl.multiple_of(index * 2 * half_rows, half_rows), 2 * half_rows), :]
            vir = dot(both, virt_ref[group]).reshape(2, rows_dev, SUB, tau_count * tile)
            vir = jnp.concatenate([vir[0], vir[1]], 1).astype(BF16)
            for moment in range(tau_count):
                for row in range(rows_dev):
                    at = (moment * rows + group * rows_dev + row) * tile
                    vir_ref[here, at : at + tile] = vir[row, :, moment * tile : (moment + 1) * tile]
        return carry

    lax.fori_loop(0, steps, step, 0, unroll=min(steps, UNROLL))
    depth = rows * tile
    chi = None
    for moment in range(tau_count):
        here = slice(moment * depth, (moment + 1) * depth)
        term = lax.dot_general(
            occ_ref[:, here], vir_ref[:, here], (((1,), (1,)), ((), ())), preferred_element_type=F32
        ) * tau_ref[moment]
        chi = term if chi is None else chi + term
    chi = chi * scale
    me = lax.axis_index("orb")
    share_rows = outs[0].shape[0]
    for distance, out in zip(partners(4), outs):
        picked = chi[0:share_rows]
        for owner in range(1, 4):
            picked = jnp.where(me ^ distance == owner, chi[owner * share_rows : (owner + 1) * share_rows], picked)
        out[...] = picked


def on_device_square(b_rows, col_blocks, g_occ, occ_live, g_virt, tau_weight):
    orb_count = lax.axis_size("orb")
    aux_count = lax.axis_size("aux")
    aux_dev, rows_dev, slot_count, tile = b_rows.shape
    tau_count = g_occ.shape[0]
    rows = orb_count * rows_dev
    steps = aux_dev // PAIR
    share_rows = aux_dev // orb_count
    sizes = (aux_count, rows_dev, tau_count)
    scale = 1.0 / math.sqrt(rows * tile * orb_count)
    smem = pl.BlockSpec(memory_space=pltpu.SMEM)
    vmem = pl.BlockSpec(memory_space=pltpu.VMEM)
    hbm = pl.BlockSpec(memory_space=pl.ANY)

    def call(kernel, name, out_shape, in_specs, scratch, limit, out_spec=vmem):
        return pl.pallas_call(
            kernel, out_shape=out_shape, in_specs=in_specs, out_specs=[out_spec] * len(out_shape),
            scratch_shapes=scratch, compiler_params=pltpu.CompilerParams(vmem_limit_bytes=limit << 20), name=name,
        )

    def xor(value, axis, distance):
        return lax.ppermute(value, axis, [(i, i ^ distance) for i in range(lax.axis_size(axis))])

    def half(*shape):
        return jax.ShapeDtypeStruct(shape, BF16)

    flat = b_rows.reshape(-1, tile)
    virt = g_virt.reshape(-1, tile)
    occ = g_occ.reshape(tau_count * rows_dev, -1)
    message = Message(virt.shape[0], occ.shape[0])
    dma = pltpu.SemaphoreType.DMA
    (sent,) = call(
        functools.partial(message_kernel, message), "message", [half(message.rows, tile)], [hbm] * 3,
        [
            pltpu.VMEM((message.rows, tile), BF16), pltpu.VMEM(occ.shape, BF16),
            pltpu.SMEM(col_blocks.shape, jnp.int32), dma((4,)),
        ], 60, hbm,
    )(virt, occ, col_blocks)
    came = {distance: xor(sent, "orb", distance) for distance in partners(orb_count)[1:]}
    messages = [sent] + [came[distance] for distance in range(1, orb_count)]
    block = half(aux_dev * rows_dev, tile)
    owns = call(functools.partial(own_kernel, rows_dev, steps), "own", [block] * 2, [vmem], [], 6)(flat)
    to_x, to_y, virt = call(
        functools.partial(send_kernel, message), "send",
        [block] * 2 + [half(3 * message.virt.stop, tile)], [vmem] * 6, [], 6,
    )(*messages, *owns)
    from_x, from_y = xor(to_x, "orb", 1), xor(to_y, "orb", 2)
    for distance in aux_steps(aux_count):
        virt = call(join_kernel, "join", [half(2 * virt.shape[0], tile)], [vmem] * 2, [], 4)(
            virt, xor(virt, "aux", distance)
        )[0]
    (mix,) = call(
        functools.partial(mix_kernel, sizes, message), "mix",
        [half(tau_count * rows * SUB, rows * SUB)], [smem] + [vmem] * 4, [], 8,
    )(occ_live, *messages)
    (virt,) = call(
        functools.partial(virt_kernel, sizes, message), "virt",
        [half(4, tile, tau_count * tile)], [vmem] * 5, [], 8,
    )(*messages, virt)
    wide = tau_count * rows * tile
    shares = call(
        functools.partial(work_kernel, rows_dev, tau_count, steps, scale), "work",
        [jax.ShapeDtypeStruct((share_rows, aux_dev), F32)] * orb_count, [smem] + [vmem] * 6,
        [pltpu.VMEM((aux_dev, wide), BF16), pltpu.VMEM((aux_dev, wide), BF16)], 24,
    )(tau_weight, mix, virt, *owns, from_x, from_y)
    total = shares[0]
    for distance, share in zip(partners(orb_count)[1:], shares[1:]):
        total = total + xor(share, "orb", distance)
    return total


def on_device(b_rows, col_blocks, g_occ, occ_live, g_virt, tau_weight):
    square = lax.axis_size("orb") == 4 and b_rows.shape[2] == 2
    plan = on_device_square if square else on_device_dense
    return plan(b_rows, col_blocks, g_occ, occ_live, g_virt, tau_weight)


def solution(mesh):
    in_specs = (
        P("aux", "orb", None, None),
        P("orb", None),
        P(None, "orb", None),
        P(),
        P(None, "orb", "aux", None),
        P(),
    )
    out_specs = P("orb", "aux")
    return jax.shard_map(
        on_device, mesh=mesh, in_specs=in_specs, out_specs=out_specs, check_vma=False
    )
```

```python
import functools
import math

import jax
import jax.numpy as jnp
from jax import lax
from jax.experimental import pallas as pl
from jax.experimental.pallas import tpu as pltpu
from jax.sharding import PartitionSpec as P

SUB = 8
PAIR = 16
UNROLL = 16
F32 = jnp.float32
BF16 = jnp.bfloat16


def iota(shape, dim):
    return lax.broadcasted_iota(jnp.int32, shape, dim)


def dot(a, b):
    return jnp.dot(a, b, preferred_element_type=F32)


def partners(count):
    return [0] + sorted(range(1, count), key=lambda distance: (-distance.bit_count(), distance))


def pick_static(index, values):
    found = jnp.zeros_like(index)
    for place, value in enumerate(values):
        found = jnp.where(index == place, value, found)
    return found


def pack_kernel(rows_dev, slot_count, chunks, pieces, col_hbm, b_hbm, occ_hbm, *refs):
    orb_count = lax.axis_size("orb")
    count = len(chunks) * orb_count
    outs, helds = refs[:count], refs[count : 2 * count]
    b_ref, occ_ref, col_ref, b_sem, occ_sem, col_sem, out_sem = refs[2 * count :]
    me = lax.axis_index("orb")
    half_rows = rows_dev * SUB
    out_rows = 2 * half_rows
    in_rows = PAIR * rows_dev * slot_count
    steps = sum(chunks)
    piece_steps = steps // pieces
    piece_rows = piece_steps * in_rows

    def fetch(piece):
        here = pl.ds(piece * piece_rows, piece_rows)
        return pltpu.make_async_copy(b_hbm.at[here], b_ref.at[here], b_sem.at[piece])

    occ_copy = pltpu.make_async_copy(occ_hbm, occ_ref, occ_sem)
    col_copy = pltpu.make_async_copy(col_hbm, col_ref, col_sem)
    col_copy.start()
    for piece in range(pieces):
        fetch(piece).start()
    occ_copy.start()
    line = iota((out_rows, in_rows), 0)
    place = iota((out_rows, in_rows), 1)
    half = line // half_rows
    row = (line % half_rows) // SUB
    func = half * SUB + line % SUB
    first = (func * rows_dev + row) * slot_count
    pick = jnp.concatenate(
        [jnp.where(place == first + slot, 1.0, 0.0).astype(BF16) for slot in range(slot_count)], 0
    )
    occ_copy.wait()
    total = chunks[0] * out_rows
    for held in helds[:orb_count]:
        held[total:, :] = jnp.zeros((held.shape[0] - total, held.shape[1]), BF16)
        held[total:, : occ_ref.shape[1]] = occ_ref[...]
    col_copy.wait()

    def step(index, group, start):
        at = pl.multiple_of(index * in_rows, in_rows)
        moved = dot(pick, b_ref[pl.ds(at, in_rows), :]).astype(BF16)
        slots = [moved[slot * out_rows : (slot + 1) * out_rows] for slot in range(slot_count)]
        zero = jnp.zeros_like(slots[0])
        for distance, held in zip(partners(orb_count), group):
            value = zero
            for slot in range(slot_count):
                value = jnp.where(col_ref[0, slot] == me ^ distance, slots[slot], value)
            held[pl.ds(pl.multiple_of((index - start) * out_rows, out_rows), out_rows), :] = value

    sent = []
    start = 0
    for number, chunk in enumerate(chunks):
        group = range(number * orb_count, (number + 1) * orb_count)
        for piece in range(start // piece_steps, (start + chunk) // piece_steps):
            fetch(piece).wait()
            low = piece * piece_steps
            lax.fori_loop(
                low, low + piece_steps,
                lambda index, carry: (step(index, [helds[at] for at in group], start), carry)[1],
                0, unroll=True,
            )
            top = low - start + piece_steps
            low_row = (low - start) * out_rows
            high_row = helds[group[0]].shape[0] if top == chunk else top * out_rows
            for place, at in enumerate(group):
                here = pl.ds(low_row, high_row - low_row)
                copy = pltpu.make_async_copy(helds[at].at[here], outs[at].at[here], out_sem.at[piece, place])
                copy.start()
                sent.append(copy)
        start += chunk
    for copy in sent:
        copy.wait()


def stage_kernel(orb_count, own_count, live_hbm, one_ref, two_ref, *refs):
    owns, outs = refs[:own_count], refs[own_count : 2 * own_count]
    live_out, join_out, live_ref, live_sem, own_sem = refs[2 * own_count :]
    live_copy = pltpu.make_async_copy(live_hbm, live_ref, live_sem)
    live_copy.start()
    copies = [pltpu.make_async_copy(own, out, own_sem.at[at]) for at, (own, out) in enumerate(zip(owns, outs))]
    for copy in copies:
        copy.start()
    join_out[: one_ref.shape[0], :] = one_ref[...]
    join_out[one_ref.shape[0] :, :] = two_ref[...]
    live_copy.wait()
    me = lax.axis_index("orb")
    order = partners(orb_count)
    tau_count = live_ref.shape[0]
    width = live_out.shape[1]
    group_of = iota((1, width), 1) // (width // orb_count)
    for moment in range(tau_count):
        for row_group in range(orb_count):
            live = jnp.zeros((1, width), jnp.int32)
            for col_group in range(orb_count):
                value = live_ref[moment, me ^ order[row_group], me ^ order[col_group]]
                live = jnp.where(group_of == col_group, value, live)
            at = moment * orb_count + row_group
            live_out[at : at + 1, :] = live
    for copy in copies:
        copy.wait()


def join_after_kernel(one_ref, two_ref, anchor, out_ref):
    join_kernel(one_ref, two_ref, out_ref)


def join_kernel(one_ref, two_ref, out_ref):
    out_ref[: one_ref.shape[0], :] = one_ref[...]
    out_ref[one_ref.shape[0] :, :] = two_ref[...]


def order_virt(sizes, virt_refs, virt_out):
    orb_count, aux_count, rows_dev, tau_count = sizes
    aux_me = lax.axis_index("aux")
    tile = virt_refs[0].shape[1]
    part = tile // aux_count
    virt_all = jnp.concatenate([ref[...] for ref in virt_refs], 0)
    line = iota((tile, virt_all.shape[0]), 0)
    place = iota((tile, virt_all.shape[0]), 1)
    for moment in range(tau_count):
        wanted = (((line // part) ^ aux_me) * tau_count + moment) * part + line % part
        chosen = dot(jnp.where(place == wanted, 1.0, 0.0).astype(BF16), virt_all)
        virt_out[:, moment * tile : (moment + 1) * tile] = chosen.astype(BF16)


def spread_occ(sizes, live_ref, blocks, total, mix_out):
    orb_count, aux_count, rows_dev, tau_count = sizes
    me = lax.axis_index("orb")
    rows = orb_count * rows_dev
    half_rows = rows_dev * SUB
    tile = blocks[0].shape[1]
    occ_all = jnp.concatenate([block[total : total + tau_count * rows_dev, :] for block in blocks], 0)
    left_shape = (tau_count * rows * SUB, occ_all.shape[0])
    line = iota(left_shape, 0)
    moment_of = line // (rows * SUB)
    row_of = (line % (rows * SUB)) // SUB
    wanted = ((row_of // rows_dev) * tau_count + moment_of) * rows_dev + row_of % rows_dev
    left = jnp.where(iota(left_shape, 1) == wanted, 1.0, 0.0).astype(BF16)
    right_shape = (tile, rows * SUB)
    col_of = iota(right_shape, 1) // SUB
    group = pick_static(col_of // rows_dev, partners(orb_count)) ^ me
    wanted = group * rows_dev + col_of % rows_dev
    right = jnp.where(iota(right_shape, 0) == wanted, 1.0, 0.0).astype(BF16)
    spread = dot(dot(left, occ_all).astype(BF16), right)
    same = iota((half_rows, rows * SUB), 0) % SUB == iota((half_rows, rows * SUB), 1) % SUB
    for at in range(tau_count * orb_count):
        here = slice(at * half_rows, (at + 1) * half_rows)
        keep = jnp.logical_and(same, live_ref[at : at + 1, :] != 0)
        mix_out[here, :] = jnp.where(keep, spread[here], 0.0).astype(BF16)


def products(sizes, steps, blocks, mix_ref, virt_ref, occ_out, vir_out):
    orb_count, aux_count, rows_dev, tau_count = sizes
    rows = orb_count * rows_dev
    half_rows = rows_dev * SUB
    tile = blocks[0].shape[1]

    def step(index, carry):
        here = pl.ds(pl.multiple_of(index * PAIR, PAIR), PAIR)
        halves = []
        for half in range(2):
            at = pl.multiple_of((index * 2 + half) * half_rows, half_rows)
            halves.append(jnp.concatenate([block[pl.ds(at, half_rows), :] for block in blocks], 0))
        if occ_out is not None:
            occ = dot(mix_ref[...], jnp.concatenate(halves, 1))
            occ = [occ[:, half * tile : (half + 1) * tile].reshape(tau_count * rows, SUB, tile) for half in range(2)]
            occ = jnp.concatenate(occ, 1).astype(BF16)
            for row in range(tau_count * rows):
                occ_out[here, row * tile : (row + 1) * tile] = occ[row]
        if vir_out is not None:
            vir = dot(jnp.concatenate(halves, 0), virt_ref[...]).reshape(2, rows, SUB, tau_count * tile)
            vir = jnp.concatenate([vir[0], vir[1]], 1).astype(BF16)
            for moment in range(tau_count):
                for row in range(rows):
                    at = (moment * rows + row) * tile
                    vir_out[here, at : at + tile] = vir[row, :, moment * tile : (moment + 1) * tile]
        return carry

    lax.fori_loop(0, steps, step, 0, unroll=min(steps, UNROLL))


def occ_kernel(sizes, steps, live_ref, *refs):
    blocks, (mix_out, occ_out) = refs[: sizes[0]], refs[sizes[0] :]
    spread_occ(sizes, live_ref, blocks, steps * 2 * sizes[2] * SUB, mix_out)
    products(sizes, steps, blocks, mix_out, None, occ_out, None)


def vir_kernel(sizes, steps, *refs):
    blocks, virt_refs = refs[: sizes[0]], refs[sizes[0] : -3]
    anchor, virt_out, vir_out = refs[-3:]
    order_virt(sizes, virt_refs, virt_out)
    products(sizes, steps, blocks, None, virt_out, None, vir_out)


def last_kernel(sizes, steps, share_rows, tau_ref, mix_ref, virt_ref, occ_first, vir_first, *refs):
    orb_count, aux_count, rows_dev, tau_count = sizes
    blocks, outs = refs[:orb_count], refs[orb_count : 2 * orb_count]
    occ_last, vir_last = refs[2 * orb_count :]
    products(sizes, steps, blocks, mix_ref, virt_ref, occ_last, vir_last)
    me = lax.axis_index("orb")
    rows = orb_count * rows_dev
    tile = blocks[0].shape[1]
    depth = rows * tile
    part = min(depth, 4096)
    chi = None
    for moment in range(tau_count):
        for piece in range(depth // part):
            here = slice(moment * depth + piece * part, moment * depth + (piece + 1) * part)
            term = lax.dot_general(
                jnp.concatenate([occ_first[:, here], occ_last[:, here]], 0),
                jnp.concatenate([vir_first[:, here], vir_last[:, here]], 0),
                (((1,), (1,)), ((), ())), preferred_element_type=F32,
            ) * tau_ref[moment]
            chi = term if chi is None else chi + term
    chi = chi * (1.0 / math.sqrt(rows * tile * orb_count))
    for distance, out in zip(partners(orb_count), outs):
        picked = chi[0:share_rows]
        for owner in range(1, orb_count):
            picked = jnp.where(me ^ distance == owner, chi[owner * share_rows : (owner + 1) * share_rows], picked)
        out[...] = picked


def on_device_dense(b_rows, col_blocks, g_occ, occ_live, g_virt, tau_weight):
    orb_count = lax.axis_size("orb")
    aux_count = lax.axis_size("aux")
    aux_dev, rows_dev, slot_count, tile = b_rows.shape
    tau_count = g_occ.shape[0]
    rows = orb_count * rows_dev
    share_rows = aux_dev // orb_count
    sizes = (orb_count, aux_count, rows_dev, tau_count)
    smem = pl.BlockSpec(memory_space=pltpu.SMEM)
    vmem = pl.BlockSpec(memory_space=pltpu.VMEM)

    def call(kernel, name, out_shape, in_specs, scratch, spare, out_spec=vmem):
        held = sum(math.prod(shape.shape) * 2 for shape in scratch if shape.dtype == BF16)
        return pl.pallas_call(
            kernel,
            out_shape=out_shape,
            in_specs=in_specs,
            out_specs=[out_spec] * len(out_shape),
            scratch_shapes=scratch,
            compiler_params=pltpu.CompilerParams(vmem_limit_bytes=min(held + (spare << 20), 60 << 20)),
            name=name,
        )

    def xor(value, axis, distance):
        return lax.ppermute(value, axis, [(i, i ^ distance) for i in range(lax.axis_size(axis))])

    def half(value):
        return jax.ShapeDtypeStruct(value, BF16)

    all_steps = aux_dev // PAIR
    chunks = (all_steps * 12 // 16, all_steps - all_steps * 12 // 16)
    occ_rows = tau_count * rows_dev
    b_flat = b_rows.reshape(-1, tile)
    occ_flat = g_occ.reshape(occ_rows, -1)
    hbm = pl.BlockSpec(memory_space=pl.ANY)
    pieces = math.gcd(4, all_steps)
    shapes = [
        (steps * PAIR * rows_dev + (0 if number else occ_rows), tile)
        for number, steps in enumerate(chunks) for _ in range(orb_count)
    ]
    blocks = call(
        functools.partial(pack_kernel, rows_dev, slot_count, chunks, pieces), "pack",
        [half(shape) for shape in shapes], [hbm] * 3,
        [pltpu.VMEM(shape, BF16) for shape in shapes] + [
            pltpu.VMEM(b_flat.shape, BF16), pltpu.VMEM(occ_flat.shape, BF16), pltpu.SMEM(col_blocks.shape, jnp.int32),
            pltpu.SemaphoreType.DMA((pieces,)), pltpu.SemaphoreType.DMA, pltpu.SemaphoreType.DMA,
            pltpu.SemaphoreType.DMA((pieces, orb_count)),
        ], 54, hbm,
    )(col_blocks, b_flat, occ_flat)
    order = partners(orb_count)
    dense = []
    for number in range(len(chunks)):
        own, *others = blocks[number * orb_count : (number + 1) * orb_count]
        dense.append([own] + [xor(value, "orb", d) for d, value in zip(order[1:], others)])
    virt = g_virt.reshape(-1, tile)
    owns = [blocks[number * orb_count] for number in range(len(chunks))]
    *owns, live, virt = call(
        functools.partial(stage_kernel, orb_count, len(chunks)), "stage",
        [half(own.shape) for own in owns]
        + [jax.ShapeDtypeStruct((tau_count * orb_count, rows * SUB), jnp.int32), half((2 * virt.shape[0], tile))],
        [hbm, vmem, vmem] + [hbm] * len(owns),
        [pltpu.SMEM(occ_live.shape, jnp.int32), pltpu.SemaphoreType.DMA, pltpu.SemaphoreType.DMA((len(owns),))], 4,
    )(occ_live, virt, xor(virt, "aux", 1), *owns)
    for own, group in zip(owns, dense):
        group[0] = own
    distance = 2
    while distance < aux_count:
        pair = half((2 * virt.shape[0], tile))
        virt = call(join_kernel, "join", [pair], [vmem] * 2, [], 2)(virt, xor(virt, "aux", distance))[0]
        distance *= 2
    virts = [virt]
    wide = half((chunks[0] * PAIR, tau_count * rows * tile))
    mix, occ_first = call(
        functools.partial(occ_kernel, sizes, chunks[0]), "occ",
        [half((tau_count * rows * SUB, rows * SUB)), wide],
        [vmem] * (1 + orb_count), [], 8,
    )(live, *dense[0])
    virt, vir_first = call(
        functools.partial(vir_kernel, sizes, chunks[0]), "vir",
        [half((tile, tau_count * tile)), wide],
        [vmem] * (orb_count + len(virts)) + [hbm], [], 8,
    )(*dense[0], *virts, mix)
    shares = call(
        functools.partial(last_kernel, sizes, chunks[1], share_rows), "last",
        [jax.ShapeDtypeStruct((share_rows, aux_dev), F32)] * orb_count,
        [smem] + [vmem] * (4 + orb_count),
        [pltpu.VMEM((chunks[1] * PAIR, tau_count * rows * tile), BF16)] * 2, 12,
    )(tau_weight, mix, virt, occ_first, vir_first, *dense[1])
    total = shares[0]
    for distance, share in zip(order[1:], shares[1:]):
        total = total + xor(share, "orb", distance)
    return total


class Message:
    def __init__(self, virt_rows, occ_rows):
        self.virt = slice(0, virt_rows)
        self.occ = slice(virt_rows, virt_rows + occ_rows)
        self.list = slice(virt_rows + occ_rows, virt_rows + occ_rows + 16)
        self.rows = virt_rows + occ_rows + 16


def equal(one, two):
    return jnp.where(one == two, 1.0, 0.0)


def by_distance(refs):
    return [refs[partners(4).index(distance)] for distance in range(4)]


def at_group(group, values):
    found = values[0]
    for place in range(1, len(values)):
        found = jnp.where(group == place, values[place], found)
    return found


class Choice:
    def __init__(self, message, refs):
        me = lax.axis_index("orb")
        near = []
        for ref in refs:
            row = ref[message.list, :].astype(F32)[0:1, :]
            near.append([row[:, slot : slot + 1] for slot in range(2)])
        lists = [[at_group(me ^ group, [near[d][slot] for d in range(4)]) for slot in range(2)] for group in range(4)]
        shape = (8, 128)
        index = iota(shape, 0) * shape[1] + iota(shape, 1)
        bits = [((index >> place) & 1).astype(F32) for place in range(8)]
        sent_x = [lists[g][0] + bits[g] * (lists[g][1] - lists[g][0]) for g in range(4)]
        sent_y = [lists[g][0] + bits[4 + g] * (lists[g][1] - lists[g][0]) for g in range(4)]
        good = jnp.where(index < 256, 1.0, 0.0)
        for one, two in ((0, 1), (2, 3), (0, 2), (1, 3), (0, 3), (1, 2)):
            for slot in range(2):
                column = lists[one][slot]
                shared = jnp.maximum(equal(column, lists[two][0]), equal(column, lists[two][1]))
                if two == one ^ 1:
                    met = jnp.maximum(equal(sent_x[one], column), equal(sent_x[two], column))
                elif two == one ^ 2:
                    met = jnp.maximum(equal(sent_y[one], column), equal(sent_y[two], column))
                else:
                    met = jnp.maximum(
                        equal(sent_x[one], column) * equal(sent_y[two], column),
                        equal(sent_y[one], column) * equal(sent_x[two], column),
                    )
                good = good * jnp.maximum(met, 1.0 - shared)
        number = jnp.where(good > 0.5, index.astype(F32), 1024.0)
        number = jnp.min(jnp.min(number, axis=1, keepdims=True), axis=0, keepdims=True)
        chosen = []
        for place in range(8):
            rest = jnp.floor(number * (1.0 / (1 << place)))
            chosen.append(rest - 2.0 * jnp.floor(rest * 0.5))
        all_x = [lists[g][0] + chosen[g] * (lists[g][1] - lists[g][0]) for g in range(4)]
        all_y = [lists[g][0] + chosen[4 + g] * (lists[g][1] - lists[g][0]) for g in range(4)]
        self.own = at_group(me, [lists[g][0] for g in range(4)]), at_group(me, [lists[g][1] for g in range(4)])
        self.slot_x = at_group(me, chosen[:4])
        self.slot_y = at_group(me, chosen[4:])
        got_x, got_y = at_group(me ^ 1, all_x), at_group(me ^ 2, all_y)
        self.got = got_x, got_y
        one = jnp.ones_like(got_x)
        foreign = one - jnp.maximum(equal(got_x, self.own[0]), equal(got_x, self.own[1]))
        self.third = foreign * got_x + (one - foreign) * got_y
        first_x = jnp.where(me < (me ^ 1), one, one - equal(at_group(me, all_x), got_x))
        first_y = jnp.where(me < (me ^ 2), one, one - equal(at_group(me, all_y), got_y))
        also = equal(at_group(me ^ 2, all_x), got_x) * equal(at_group(me ^ 1, all_y), got_x)
        first_far = jnp.where(me < (me ^ 3), one, one - also)
        zero = jnp.zeros_like(one)
        with_x = [equal(got_x, column) * first_x for column in self.own]
        with_y = [equal(got_y, column) * first_y for column in self.own]
        far = equal(got_x, got_y) * first_far
        self.pairs = [
            [one, zero, with_x[0], with_y[0]],
            [zero, one, with_x[1], with_y[1]],
            [with_x[0], with_x[1], zero, far],
            [with_y[0], with_y[1], far, zero],
        ]


class Chosen:
    def __init__(self, ref):
        values = [ref[0:1, place : place + 1] for place in range(20)]
        self.own, self.got = values[0:2], values[2:4]
        self.pairs = [values[4 + 4 * block : 8 + 4 * block] for block in range(4)]

    @staticmethod
    def leave(choice, ref):
        values = [*choice.own, *choice.got] + [value for row in choice.pairs for value in row]
        lane = iota(ref.shape, 1)
        total = jnp.zeros(ref.shape, F32)
        for place, value in enumerate(values):
            total = jnp.where(lane == place, value, total)
        ref[...] = total


def message_kernel(message, virt_hbm, occ_hbm, col_hbm, *refs):
    *outs, out_ref, occ_ref, col_ref, sem = refs
    copies = [
        pltpu.make_async_copy(virt_hbm, out_ref.at[message.virt], sem.at[0]),
        pltpu.make_async_copy(occ_hbm, occ_ref, sem.at[1]),
        pltpu.make_async_copy(col_hbm, col_ref, sem.at[2]),
    ]
    for copy in copies:
        copy.start()
    tile = out_ref.shape[1]
    out_ref[message.occ, :] = jnp.zeros((occ_ref.shape[0], tile), BF16)
    for copy in copies:
        copy.wait()
    out_ref[message.occ, : occ_ref.shape[1]] = occ_ref[...]
    row, lane = iota((16, tile), 0), iota((16, tile), 1)
    value = jnp.zeros((16, tile), F32)
    for slot in range(col_ref.shape[1]):
        here = jnp.logical_and(row == 0, lane == slot)
        value = jnp.where(here, col_ref[0, slot].astype(F32), value)
    out_ref[message.list, :] = value.astype(BF16)
    copies = [pltpu.make_async_copy(out_ref, out, sem.at[3 + at]) for at, out in enumerate(outs)]
    for copy in copies:
        copy.start()
    for copy in copies:
        copy.wait()


def own_kernel(rows_dev, steps, b_ref, *outs):
    half_rows = rows_dev * SUB
    out_rows = 2 * half_rows
    in_rows = PAIR * rows_dev * 2
    line = iota((out_rows, in_rows), 0)
    place = iota((out_rows, in_rows), 1)
    func = (line // half_rows) * SUB + line % SUB
    first = (func * rows_dev + (line % half_rows) // SUB) * 2
    pick = jnp.concatenate([jnp.where(place == first + slot, 1.0, 0.0).astype(BF16) for slot in range(2)], 0)
    for index in range(steps):
        moved = dot(pick, b_ref[index * in_rows : (index + 1) * in_rows, :]).astype(BF16)
        for slot, out in enumerate(outs):
            out[index * out_rows : (index + 1) * out_rows, :] = moved[slot * out_rows : (slot + 1) * out_rows]


def send_kernel(message, *refs):
    messages, (own0, own1), (virt_out, chosen, *outs) = by_distance(refs[2:6]), refs[:2], refs[6:]
    choice = Choice(message, messages)
    Chosen.leave(choice, chosen)
    at = 0
    for to_x, to_y in zip(outs[0::2], outs[1::2]):
        here = slice(at, at + to_x.shape[0])
        to_x[...] = jnp.where(choice.slot_x > 0.5, own1[here, :], own0[here, :])
        to_y[...] = jnp.where(choice.slot_y > 0.5, own1[here, :], own0[here, :])
        at += to_x.shape[0]
    me = lax.axis_index("orb")
    rows = message.virt.stop
    for slot, column in enumerate((choice.own[0], choice.own[1], choice.third)):
        total = jnp.zeros((rows, virt_out.shape[1]), F32)
        for distance in range(4):
            weight = equal(column, (me ^ distance).astype(F32))
            total = total + weight * messages[distance][message.virt, :].astype(F32)
        virt_out[slot * rows : (slot + 1) * rows, :] = total.astype(BF16)


def aux_steps(aux_count):
    steps = []
    distance = aux_count // 2
    while distance:
        steps.append(distance)
        distance //= 2
    return steps


def aux_order(aux_count):
    order = [0]
    for distance in aux_steps(aux_count):
        order = order + [value ^ distance for value in order]
    return order


def virt_kernel(sizes, *refs):
    aux_count, rows_dev, tau_count = sizes
    chosen, virt_ref, virt_out = refs
    choice = Chosen(chosen)
    aux_me = lax.axis_index("aux")
    tile = virt_ref.shape[1]
    part = tile // aux_count
    order = aux_order(aux_count)
    line = iota((tile, virt_ref.shape[0]), 0)
    place = iota((tile, virt_ref.shape[0]), 1)
    virts = []
    for slot in range(3):
        columns = []
        for moment in range(tau_count):
            held = pick_static((line // part) ^ aux_me, [order.index(value) for value in range(aux_count)])
            wanted = ((held * 3 + slot) * tau_count + moment) * part + line % part
            columns.append(dot(jnp.where(place == wanted, 1.0, 0.0).astype(BF16), virt_ref[...]))
        virts.append(jnp.concatenate(columns, 1))
    virt_out[0] = virts[0].astype(BF16)
    virt_out[1] = virts[1].astype(BF16)
    for at, column in enumerate(choice.got):
        one, two = equal(column, choice.own[0]), equal(column, choice.own[1])
        virt_out[2 + at] = (one * virts[0] + two * virts[1] + (1.0 - one - two) * virts[2]).astype(BF16)


def mix_kernel(sizes, message, live_ref, *refs):
    aux_count, rows_dev, tau_count = sizes
    messages, chosen, mix_out = by_distance(refs[:4]), refs[4], refs[5]
    choice = Chosen(chosen)
    me = lax.axis_index("orb")
    tile = messages[0].shape[1]
    rows = 4 * rows_dev
    half_rows = rows_dev * SUB
    groups = [me, me, me ^ 1, me ^ 2]
    occ_all = jnp.concatenate([messages[at][message.occ, :] for at in (0, 0, 1, 2)], 0)
    left_shape = (tau_count * rows * SUB, occ_all.shape[0])
    line = iota(left_shape, 0)
    row_of = (line % (rows * SUB)) // SUB
    wanted = ((row_of // rows_dev) * tau_count + line // (rows * SUB)) * rows_dev + row_of % rows_dev
    left = jnp.where(iota(left_shape, 1) == wanted, 1.0, 0.0).astype(BF16)
    right_shape = (tile, rows * SUB)
    col_of = iota(right_shape, 1) // SUB
    wanted = pick_static(col_of // rows_dev, groups) * rows_dev + col_of % rows_dev
    right = jnp.where(iota(right_shape, 0) == wanted, 1.0, 0.0).astype(BF16)
    spread = dot(dot(left, occ_all).astype(BF16), right)
    same = iota((half_rows, rows * SUB), 0) % SUB == iota((half_rows, rows * SUB), 1) % SUB
    group_of = iota((1, rows * SUB), 1) // half_rows
    for moment in range(tau_count):
        for one in range(4):
            live = jnp.zeros((1, rows * SUB), F32)
            for two in range(4):
                value = live_ref[moment, groups[one], groups[two]].astype(F32) * choice.pairs[one][two]
                live = jnp.where(group_of == two, value, live)
            at = (moment * 4 + one) * half_rows
            keep = jnp.logical_and(same, live != 0.0)
            mix_out[at : at + half_rows, :] = jnp.where(keep, spread[at : at + half_rows], 0.0).astype(BF16)


def four_products(rows_dev, tau_count, first, steps, owns, got, mix_ref, virt_ref, occ_ref, vir_ref):
    rows = 4 * rows_dev
    half_rows = rows_dev * SUB
    tile = owns[0].shape[1]
    blocks = [(own, first) for own in owns] + [(block, 0) for block in got]

    def step(index, carry):
        here = pl.ds(pl.multiple_of(index * PAIR, PAIR), PAIR)
        if occ_ref is not None:
            halves = []
            for half in range(2):
                halves.append(jnp.concatenate([
                    block[pl.ds(pl.multiple_of(((index + shift) * 2 + half) * half_rows, half_rows), half_rows), :]
                    for block, shift in blocks
                ], 0))
            occ = dot(mix_ref[...], jnp.concatenate(halves, 1))
            occ = [occ[:, half * tile : (half + 1) * tile].reshape(tau_count * rows, SUB, tile) for half in range(2)]
            occ = jnp.concatenate(occ, 1).astype(BF16)
            for row in range(tau_count * rows):
                occ_ref[here, row * tile : (row + 1) * tile] = occ[row]
        if vir_ref is not None:
            for group, (block, shift) in enumerate(blocks):
                at = pl.multiple_of((index + shift) * 2 * half_rows, half_rows)
                vir = dot(block[pl.ds(at, 2 * half_rows), :], virt_ref[group])
                vir = vir.reshape(2, rows_dev, SUB, tau_count * tile)
                vir = jnp.concatenate([vir[0], vir[1]], 1).astype(BF16)
                for moment in range(tau_count):
                    for row in range(rows_dev):
                        at = (moment * rows + group * rows_dev + row) * tile
                        vir_ref[here, at : at + tile] = vir[row, :, moment * tile : (moment + 1) * tile]
        return carry

    lax.fori_loop(0, steps, step, 0, unroll=min(steps, UNROLL))


def early_occ_kernel(rows_dev, tau_count, steps, mix_ref, own0, own1, from_x, from_y, occ_out):
    four_products(rows_dev, tau_count, 0, steps, [own0, own1], [from_x, from_y], mix_ref, None, occ_out, None)


def early_vir_kernel(rows_dev, tau_count, steps, virt_ref, own0, own1, from_x, from_y, vir_out):
    four_products(rows_dev, tau_count, 0, steps, [own0, own1], [from_x, from_y], None, virt_ref, None, vir_out)


def late_kernel(rows_dev, tau_count, first, steps, scale, tau_ref, mix_ref, virt_ref, *refs):
    (own0, own1, from_x, from_y, occ_early, vir_early), outs, (occ_ref, vir_ref) = refs[:6], refs[6:10], refs[10:]
    four_products(rows_dev, tau_count, first, steps, [own0, own1], [from_x, from_y], mix_ref, virt_ref, occ_ref, vir_ref)
    depth = 4 * rows_dev * own0.shape[1]
    chi = None
    for moment in range(tau_count):
        here = slice(moment * depth, (moment + 1) * depth)
        term = lax.dot_general(
            jnp.concatenate([occ_early[:, here], occ_ref[:, here]], 0),
            jnp.concatenate([vir_early[:, here], vir_ref[:, here]], 0),
            (((1,), (1,)), ((), ())), preferred_element_type=F32,
        ) * tau_ref[moment]
        chi = term if chi is None else chi + term
    chi = chi * scale
    me = lax.axis_index("orb")
    share_rows = outs[0].shape[0]
    for distance, out in zip(partners(4), outs):
        picked = chi[0:share_rows]
        for owner in range(1, 4):
            picked = jnp.where(me ^ distance == owner, chi[owner * share_rows : (owner + 1) * share_rows], picked)
        out[...] = picked


def on_device_square(b_rows, col_blocks, g_occ, occ_live, g_virt, tau_weight):
    orb_count = lax.axis_size("orb")
    aux_count = lax.axis_size("aux")
    aux_dev, rows_dev, slot_count, tile = b_rows.shape
    tau_count = g_occ.shape[0]
    rows = orb_count * rows_dev
    steps = aux_dev // PAIR
    share_rows = aux_dev // orb_count
    sizes = (aux_count, rows_dev, tau_count)
    scale = 1.0 / math.sqrt(rows * tile * orb_count)
    smem = pl.BlockSpec(memory_space=pltpu.SMEM)
    vmem = pl.BlockSpec(memory_space=pltpu.VMEM)
    hbm = pl.BlockSpec(memory_space=pl.ANY)

    def call(kernel, name, out_shape, in_specs, scratch, limit, out_spec=vmem, flops=0):
        return pl.pallas_call(
            kernel, out_shape=out_shape, in_specs=in_specs, out_specs=[out_spec] * len(out_shape),
            scratch_shapes=scratch, compiler_params=pltpu.CompilerParams(vmem_limit_bytes=limit << 20), name=name,
            cost_estimate=pl.CostEstimate(flops=flops, bytes_accessed=0, transcendentals=0) if flops else None,
        )

    def xor(value, axis, distance):
        return lax.ppermute(value, axis, [(i, i ^ distance) for i in range(lax.axis_size(axis))])

    def half(*shape):
        return jax.ShapeDtypeStruct(shape, BF16)

    flat = b_rows.reshape(-1, tile)
    virt = g_virt.reshape(-1, tile)
    occ = g_occ.reshape(tau_count * rows_dev, -1)
    message = Message(virt.shape[0], occ.shape[0])
    dma = pltpu.SemaphoreType.DMA
    sent = call(
        functools.partial(message_kernel, message), "message", [half(message.rows, tile)] * orb_count, [hbm] * 3,
        [
            pltpu.VMEM((message.rows, tile), BF16), pltpu.VMEM(occ.shape, BF16),
            pltpu.SMEM(col_blocks.shape, jnp.int32), dma((3 + orb_count,)),
        ], 60, hbm, 10**10,
    )(virt, occ, col_blocks)
    came = {distance: xor(part, "orb", distance) for distance, part in zip(partners(orb_count)[1:], sent[1:])}
    messages = [sent[0]] + [came[distance] for distance in partners(orb_count)[1:]]
    block = half(aux_dev * rows_dev, tile)
    owns = call(functools.partial(own_kernel, rows_dev, steps), "own", [block] * 2, [vmem], [], 6, vmem, 10**10)(flat)
    early = steps * 12 // 16
    chunks = (early, steps - early)
    virt, chosen, *sends = call(
        functools.partial(send_kernel, message), "send",
        [half(3 * message.virt.stop, tile), jax.ShapeDtypeStruct((8, tile), F32)]
        + [half(count * PAIR * rows_dev, tile) for count in chunks for _ in range(2)],
        [vmem] * 6, [], 6, vmem, 10**10,
    )(*owns, *messages)
    got = [(xor(to_x, "orb", 1), xor(to_y, "orb", 2)) for to_x, to_y in zip(sends[0::2], sends[1::2])]
    (mix,) = call(
        functools.partial(mix_kernel, sizes, message), "mix",
        [half(tau_count * rows * SUB, rows * SUB)], [smem] + [vmem] * 5, [], 8,
    )(occ_live, *messages, chosen)
    wide = tau_count * rows * tile
    first = half(early * PAIR, wide)
    (occ_early,) = call(
        functools.partial(early_occ_kernel, rows_dev, tau_count, early), "occ", [first], [vmem] * 5, [], 6
    )(mix, *owns, *got[0])
    distances = aux_steps(aux_count)
    for number, distance in enumerate(distances):
        pair, other = half(2 * virt.shape[0], tile), xor(virt, "aux", distance)
        anchor = {0: mix, len(distances) - 1: occ_early}.get(number)
        if anchor is None:
            (virt,) = call(join_kernel, "join", [pair], [vmem] * 2, [], 4)(virt, other)
        else:
            (virt,) = call(join_after_kernel, "join", [pair], [vmem] * 2 + [hbm], [], 4)(virt, other, anchor)
    (virt,) = call(
        functools.partial(virt_kernel, sizes), "virt", [half(4, tile, tau_count * tile)], [vmem] * 2, [], 8
    )(chosen, virt)
    (vir_early,) = call(
        functools.partial(early_vir_kernel, rows_dev, tau_count, early), "vir", [first], [vmem] * 5, [], 6
    )(virt, *owns, *got[0])
    shares = call(
        functools.partial(late_kernel, rows_dev, tau_count, early, steps - early, scale), "late",
        [jax.ShapeDtypeStruct((share_rows, aux_dev), F32)] * orb_count, [smem] + [vmem] * 8,
        [pltpu.VMEM(((steps - early) * PAIR, wide), BF16), pltpu.VMEM(((steps - early) * PAIR, wide), BF16)], 16,
    )(tau_weight, mix, virt, *owns, *got[1], occ_early, vir_early)
    total = shares[0]
    for distance, share in zip(partners(orb_count)[1:], shares[1:]):
        total = total + xor(share, "orb", distance)
    return total


def on_device(b_rows, col_blocks, g_occ, occ_live, g_virt, tau_weight):
    square = lax.axis_size("orb") == 4 and b_rows.shape[2] == 2
    plan = on_device_square if square else on_device_dense
    return plan(b_rows, col_blocks, g_occ, occ_live, g_virt, tau_weight)


def solution(mesh):
    in_specs = (
        P("aux", "orb", None, None),
        P("orb", None),
        P(None, "orb", None),
        P(),
        P(None, "orb", "aux", None),
        P(),
    )
    out_specs = P("orb", "aux")
    return jax.shard_map(
        on_device, mesh=mesh, in_specs=in_specs, out_specs=out_specs, check_vma=False
    )
```

```python
import functools
import math

import jax
import jax.numpy as jnp
from jax import lax
from jax.experimental import pallas as pl
from jax.experimental.pallas import tpu as pltpu
from jax.sharding import PartitionSpec as P

SUB = 8
PAIR = 16
UNROLL = 16
F32 = jnp.float32
BF16 = jnp.bfloat16


def iota(shape, dim):
    return lax.broadcasted_iota(jnp.int32, shape, dim)


def dot(a, b):
    return jnp.dot(a, b, preferred_element_type=F32)


def partners(count):
    return [0] + sorted(range(1, count), key=lambda distance: (-distance.bit_count(), distance))


def pick_static(index, values):
    found = jnp.zeros_like(index)
    for place, value in enumerate(values):
        found = jnp.where(index == place, value, found)
    return found


def pack_kernel(rows_dev, slot_count, chunks, pieces, col_hbm, b_hbm, occ_hbm, *refs):
    orb_count = lax.axis_size("orb")
    count = len(chunks) * orb_count
    outs, helds = refs[:count], refs[count : 2 * count]
    b_ref, occ_ref, col_ref, b_sem, occ_sem, col_sem, out_sem = refs[2 * count :]
    me = lax.axis_index("orb")
    half_rows = rows_dev * SUB
    out_rows = 2 * half_rows
    in_rows = PAIR * rows_dev * slot_count
    steps = sum(chunks)
    piece_steps = steps // pieces
    piece_rows = piece_steps * in_rows

    def fetch(piece):
        here = pl.ds(piece * piece_rows, piece_rows)
        return pltpu.make_async_copy(b_hbm.at[here], b_ref.at[here], b_sem.at[piece])

    occ_copy = pltpu.make_async_copy(occ_hbm, occ_ref, occ_sem)
    col_copy = pltpu.make_async_copy(col_hbm, col_ref, col_sem)
    col_copy.start()
    for piece in range(pieces):
        fetch(piece).start()
    occ_copy.start()
    line = iota((out_rows, in_rows), 0)
    place = iota((out_rows, in_rows), 1)
    half = line // half_rows
    row = (line % half_rows) // SUB
    func = half * SUB + line % SUB
    first = (func * rows_dev + row) * slot_count
    pick = jnp.concatenate(
        [jnp.where(place == first + slot, 1.0, 0.0).astype(BF16) for slot in range(slot_count)], 0
    )
    occ_copy.wait()
    total = chunks[0] * out_rows
    for held in helds[:orb_count]:
        held[total:, :] = jnp.zeros((held.shape[0] - total, held.shape[1]), BF16)
        held[total:, : occ_ref.shape[1]] = occ_ref[...]
    col_copy.wait()

    def step(index, group, start):
        at = pl.multiple_of(index * in_rows, in_rows)
        moved = dot(pick, b_ref[pl.ds(at, in_rows), :]).astype(BF16)
        slots = [moved[slot * out_rows : (slot + 1) * out_rows] for slot in range(slot_count)]
        zero = jnp.zeros_like(slots[0])
        for distance, held in zip(partners(orb_count), group):
            value = zero
            for slot in range(slot_count):
                value = jnp.where(col_ref[0, slot] == me ^ distance, slots[slot], value)
            held[pl.ds(pl.multiple_of((index - start) * out_rows, out_rows), out_rows), :] = value

    sent = []
    start = 0
    for number, chunk in enumerate(chunks):
        group = range(number * orb_count, (number + 1) * orb_count)
        for piece in range(start // piece_steps, (start + chunk) // piece_steps):
            fetch(piece).wait()
            low = piece * piece_steps
            lax.fori_loop(
                low, low + piece_steps,
                lambda index, carry: (step(index, [helds[at] for at in group], start), carry)[1],
                0, unroll=True,
            )
            top = low - start + piece_steps
            low_row = (low - start) * out_rows
            high_row = helds[group[0]].shape[0] if top == chunk else top * out_rows
            for place, at in enumerate(group):
                here = pl.ds(low_row, high_row - low_row)
                copy = pltpu.make_async_copy(helds[at].at[here], outs[at].at[here], out_sem.at[piece, place])
                copy.start()
                sent.append(copy)
        start += chunk
    for copy in sent:
        copy.wait()


def stage_kernel(orb_count, own_count, live_hbm, one_ref, two_ref, *refs):
    owns, outs = refs[:own_count], refs[own_count : 2 * own_count]
    live_out, join_out, live_ref, live_sem, own_sem = refs[2 * own_count :]
    live_copy = pltpu.make_async_copy(live_hbm, live_ref, live_sem)
    live_copy.start()
    copies = [pltpu.make_async_copy(own, out, own_sem.at[at]) for at, (own, out) in enumerate(zip(owns, outs))]
    for copy in copies:
        copy.start()
    join_out[: one_ref.shape[0], :] = one_ref[...]
    join_out[one_ref.shape[0] :, :] = two_ref[...]
    live_copy.wait()
    me = lax.axis_index("orb")
    order = partners(orb_count)
    tau_count = live_ref.shape[0]
    width = live_out.shape[1]
    group_of = iota((1, width), 1) // (width // orb_count)
    for moment in range(tau_count):
        for row_group in range(orb_count):
            live = jnp.zeros((1, width), jnp.int32)
            for col_group in range(orb_count):
                value = live_ref[moment, me ^ order[row_group], me ^ order[col_group]]
                live = jnp.where(group_of == col_group, value, live)
            at = moment * orb_count + row_group
            live_out[at : at + 1, :] = live
    for copy in copies:
        copy.wait()


def join_after_kernel(one_ref, two_ref, anchor, out_ref):
    join_kernel(one_ref, two_ref, out_ref)


def join_kernel(one_ref, two_ref, out_ref):
    out_ref[: one_ref.shape[0], :] = one_ref[...]
    out_ref[one_ref.shape[0] :, :] = two_ref[...]


def order_virt(sizes, virt_refs, virt_out):
    orb_count, aux_count, rows_dev, tau_count = sizes
    aux_me = lax.axis_index("aux")
    tile = virt_refs[0].shape[1]
    part = tile // aux_count
    virt_all = jnp.concatenate([ref[...] for ref in virt_refs], 0)
    line = iota((tile, virt_all.shape[0]), 0)
    place = iota((tile, virt_all.shape[0]), 1)
    for moment in range(tau_count):
        wanted = (((line // part) ^ aux_me) * tau_count + moment) * part + line % part
        chosen = dot(jnp.where(place == wanted, 1.0, 0.0).astype(BF16), virt_all)
        virt_out[:, moment * tile : (moment + 1) * tile] = chosen.astype(BF16)


def spread_occ(sizes, live_ref, blocks, total, mix_out):
    orb_count, aux_count, rows_dev, tau_count = sizes
    me = lax.axis_index("orb")
    rows = orb_count * rows_dev
    half_rows = rows_dev * SUB
    tile = blocks[0].shape[1]
    occ_all = jnp.concatenate([block[total : total + tau_count * rows_dev, :] for block in blocks], 0)
    left_shape = (tau_count * rows * SUB, occ_all.shape[0])
    line = iota(left_shape, 0)
    moment_of = line // (rows * SUB)
    row_of = (line % (rows * SUB)) // SUB
    wanted = ((row_of // rows_dev) * tau_count + moment_of) * rows_dev + row_of % rows_dev
    left = jnp.where(iota(left_shape, 1) == wanted, 1.0, 0.0).astype(BF16)
    right_shape = (tile, rows * SUB)
    col_of = iota(right_shape, 1) // SUB
    group = pick_static(col_of // rows_dev, partners(orb_count)) ^ me
    wanted = group * rows_dev + col_of % rows_dev
    right = jnp.where(iota(right_shape, 0) == wanted, 1.0, 0.0).astype(BF16)
    spread = dot(dot(left, occ_all).astype(BF16), right)
    same = iota((half_rows, rows * SUB), 0) % SUB == iota((half_rows, rows * SUB), 1) % SUB
    for at in range(tau_count * orb_count):
        here = slice(at * half_rows, (at + 1) * half_rows)
        keep = jnp.logical_and(same, live_ref[at : at + 1, :] != 0)
        mix_out[here, :] = jnp.where(keep, spread[here], 0.0).astype(BF16)


def products(sizes, steps, blocks, mix_ref, virt_ref, occ_out, vir_out):
    orb_count, aux_count, rows_dev, tau_count = sizes
    rows = orb_count * rows_dev
    half_rows = rows_dev * SUB
    tile = blocks[0].shape[1]

    def step(index, carry):
        here = pl.ds(pl.multiple_of(index * PAIR, PAIR), PAIR)
        halves = []
        for half in range(2):
            at = pl.multiple_of((index * 2 + half) * half_rows, half_rows)
            halves.append(jnp.concatenate([block[pl.ds(at, half_rows), :] for block in blocks], 0))
        if occ_out is not None:
            occ = dot(mix_ref[...], jnp.concatenate(halves, 1))
            occ = [occ[:, half * tile : (half + 1) * tile].reshape(tau_count * rows, SUB, tile) for half in range(2)]
            occ = jnp.concatenate(occ, 1).astype(BF16)
            for row in range(tau_count * rows):
                occ_out[here, row * tile : (row + 1) * tile] = occ[row]
        if vir_out is not None:
            vir = dot(jnp.concatenate(halves, 0), virt_ref[...]).reshape(2, rows, SUB, tau_count * tile)
            vir = jnp.concatenate([vir[0], vir[1]], 1).astype(BF16)
            for moment in range(tau_count):
                for row in range(rows):
                    at = (moment * rows + row) * tile
                    vir_out[here, at : at + tile] = vir[row, :, moment * tile : (moment + 1) * tile]
        return carry

    lax.fori_loop(0, steps, step, 0, unroll=min(steps, UNROLL))


def occ_kernel(sizes, steps, live_ref, *refs):
    blocks, (mix_out, occ_out) = refs[: sizes[0]], refs[sizes[0] :]
    spread_occ(sizes, live_ref, blocks, steps * 2 * sizes[2] * SUB, mix_out)
    products(sizes, steps, blocks, mix_out, None, occ_out, None)


def vir_kernel(sizes, steps, *refs):
    blocks, virt_refs = refs[: sizes[0]], refs[sizes[0] : -3]
    anchor, virt_out, vir_out = refs[-3:]
    order_virt(sizes, virt_refs, virt_out)
    products(sizes, steps, blocks, None, virt_out, None, vir_out)


def last_kernel(sizes, steps, share_rows, tau_ref, mix_ref, virt_ref, occ_first, vir_first, *refs):
    orb_count, aux_count, rows_dev, tau_count = sizes
    blocks, outs = refs[:orb_count], refs[orb_count : 2 * orb_count]
    occ_last, vir_last = refs[2 * orb_count :]
    products(sizes, steps, blocks, mix_ref, virt_ref, occ_last, vir_last)
    me = lax.axis_index("orb")
    rows = orb_count * rows_dev
    tile = blocks[0].shape[1]
    depth = rows * tile
    part = min(depth, 4096)
    chi = None
    for moment in range(tau_count):
        for piece in range(depth // part):
            here = slice(moment * depth + piece * part, moment * depth + (piece + 1) * part)
            term = lax.dot_general(
                jnp.concatenate([occ_first[:, here], occ_last[:, here]], 0),
                jnp.concatenate([vir_first[:, here], vir_last[:, here]], 0),
                (((1,), (1,)), ((), ())), preferred_element_type=F32,
            ) * tau_ref[moment]
            chi = term if chi is None else chi + term
    chi = chi * (1.0 / math.sqrt(rows * tile * orb_count))
    for distance, out in zip(partners(orb_count), outs):
        picked = chi[0:share_rows]
        for owner in range(1, orb_count):
            picked = jnp.where(me ^ distance == owner, chi[owner * share_rows : (owner + 1) * share_rows], picked)
        out[...] = picked


def on_device_dense(b_rows, col_blocks, g_occ, occ_live, g_virt, tau_weight):
    orb_count = lax.axis_size("orb")
    aux_count = lax.axis_size("aux")
    aux_dev, rows_dev, slot_count, tile = b_rows.shape
    tau_count = g_occ.shape[0]
    rows = orb_count * rows_dev
    share_rows = aux_dev // orb_count
    sizes = (orb_count, aux_count, rows_dev, tau_count)
    smem = pl.BlockSpec(memory_space=pltpu.SMEM)
    vmem = pl.BlockSpec(memory_space=pltpu.VMEM)

    def call(kernel, name, out_shape, in_specs, scratch, spare, out_spec=vmem):
        held = sum(math.prod(shape.shape) * 2 for shape in scratch if shape.dtype == BF16)
        return pl.pallas_call(
            kernel,
            out_shape=out_shape,
            in_specs=in_specs,
            out_specs=[out_spec] * len(out_shape),
            scratch_shapes=scratch,
            compiler_params=pltpu.CompilerParams(vmem_limit_bytes=min(held + (spare << 20), 60 << 20)),
            name=name,
        )

    def xor(value, axis, distance):
        return lax.ppermute(value, axis, [(i, i ^ distance) for i in range(lax.axis_size(axis))])

    def half(value):
        return jax.ShapeDtypeStruct(value, BF16)

    all_steps = aux_dev // PAIR
    chunks = (all_steps * 12 // 16, all_steps - all_steps * 12 // 16)
    occ_rows = tau_count * rows_dev
    b_flat = b_rows.reshape(-1, tile)
    occ_flat = g_occ.reshape(occ_rows, -1)
    hbm = pl.BlockSpec(memory_space=pl.ANY)
    pieces = math.gcd(4, all_steps)
    shapes = [
        (steps * PAIR * rows_dev + (0 if number else occ_rows), tile)
        for number, steps in enumerate(chunks) for _ in range(orb_count)
    ]
    blocks = call(
        functools.partial(pack_kernel, rows_dev, slot_count, chunks, pieces), "pack",
        [half(shape) for shape in shapes], [hbm] * 3,
        [pltpu.VMEM(shape, BF16) for shape in shapes] + [
            pltpu.VMEM(b_flat.shape, BF16), pltpu.VMEM(occ_flat.shape, BF16), pltpu.SMEM(col_blocks.shape, jnp.int32),
            pltpu.SemaphoreType.DMA((pieces,)), pltpu.SemaphoreType.DMA, pltpu.SemaphoreType.DMA,
            pltpu.SemaphoreType.DMA((pieces, orb_count)),
        ], 54, hbm,
    )(col_blocks, b_flat, occ_flat)
    order = partners(orb_count)
    dense = []
    for number in range(len(chunks)):
        own, *others = blocks[number * orb_count : (number + 1) * orb_count]
        dense.append([own] + [xor(value, "orb", d) for d, value in zip(order[1:], others)])
    virt = g_virt.reshape(-1, tile)
    owns = [blocks[number * orb_count] for number in range(len(chunks))]
    *owns, live, virt = call(
        functools.partial(stage_kernel, orb_count, len(chunks)), "stage",
        [half(own.shape) for own in owns]
        + [jax.ShapeDtypeStruct((tau_count * orb_count, rows * SUB), jnp.int32), half((2 * virt.shape[0], tile))],
        [hbm, vmem, vmem] + [hbm] * len(owns),
        [pltpu.SMEM(occ_live.shape, jnp.int32), pltpu.SemaphoreType.DMA, pltpu.SemaphoreType.DMA((len(owns),))], 4,
    )(occ_live, virt, xor(virt, "aux", 1), *owns)
    for own, group in zip(owns, dense):
        group[0] = own
    distance = 2
    while distance < aux_count:
        pair = half((2 * virt.shape[0], tile))
        virt = call(join_kernel, "join", [pair], [vmem] * 2, [], 2)(virt, xor(virt, "aux", distance))[0]
        distance *= 2
    virts = [virt]
    wide = half((chunks[0] * PAIR, tau_count * rows * tile))
    mix, occ_first = call(
        functools.partial(occ_kernel, sizes, chunks[0]), "occ",
        [half((tau_count * rows * SUB, rows * SUB)), wide],
        [vmem] * (1 + orb_count), [], 8,
    )(live, *dense[0])
    virt, vir_first = call(
        functools.partial(vir_kernel, sizes, chunks[0]), "vir",
        [half((tile, tau_count * tile)), wide],
        [vmem] * (orb_count + len(virts)) + [hbm], [], 8,
    )(*dense[0], *virts, mix)
    shares = call(
        functools.partial(last_kernel, sizes, chunks[1], share_rows), "last",
        [jax.ShapeDtypeStruct((share_rows, aux_dev), F32)] * orb_count,
        [smem] + [vmem] * (4 + orb_count),
        [pltpu.VMEM((chunks[1] * PAIR, tau_count * rows * tile), BF16)] * 2, 12,
    )(tau_weight, mix, virt, occ_first, vir_first, *dense[1])
    total = shares[0]
    for distance, share in zip(order[1:], shares[1:]):
        total = total + xor(share, "orb", distance)
    return total


class Message:
    def __init__(self, virt_rows, occ_rows):
        self.virt = slice(0, virt_rows)
        self.occ = slice(virt_rows, virt_rows + occ_rows)
        self.list = slice(virt_rows + occ_rows, virt_rows + occ_rows + 16)
        self.rows = virt_rows + occ_rows + 16


def equal(one, two):
    return jnp.where(one == two, 1.0, 0.0)


def by_distance(refs):
    return [refs[partners(4).index(distance)] for distance in range(4)]


def at_group(group, values):
    found = values[0]
    for place in range(1, len(values)):
        found = jnp.where(group == place, values[place], found)
    return found


class Choice:
    def __init__(self, message, refs):
        me = lax.axis_index("orb")
        near = []
        for ref in refs:
            row = ref[message.list, :].astype(F32)[0:1, :]
            near.append([row[:, slot : slot + 1] for slot in range(2)])
        lists = [[at_group(me ^ group, [near[d][slot] for d in range(4)]) for slot in range(2)] for group in range(4)]
        shape = (8, 128)
        index = iota(shape, 0) * shape[1] + iota(shape, 1)
        bits = [((index >> place) & 1).astype(F32) for place in range(8)]
        sent_x = [lists[g][0] + bits[g] * (lists[g][1] - lists[g][0]) for g in range(4)]
        sent_y = [lists[g][0] + bits[4 + g] * (lists[g][1] - lists[g][0]) for g in range(4)]
        good = jnp.where(index < 256, 1.0, 0.0)
        for one, two in ((0, 1), (2, 3), (0, 2), (1, 3), (0, 3), (1, 2)):
            for slot in range(2):
                column = lists[one][slot]
                shared = jnp.maximum(equal(column, lists[two][0]), equal(column, lists[two][1]))
                if two == one ^ 1:
                    met = jnp.maximum(equal(sent_x[one], column), equal(sent_x[two], column))
                elif two == one ^ 2:
                    met = jnp.maximum(equal(sent_y[one], column), equal(sent_y[two], column))
                else:
                    met = jnp.maximum(
                        equal(sent_x[one], column) * equal(sent_y[two], column),
                        equal(sent_y[one], column) * equal(sent_x[two], column),
                    )
                good = good * jnp.maximum(met, 1.0 - shared)
        number = jnp.where(good > 0.5, index.astype(F32), 1024.0)
        number = jnp.min(jnp.min(number, axis=1, keepdims=True), axis=0, keepdims=True)
        chosen = []
        for place in range(8):
            rest = jnp.floor(number * (1.0 / (1 << place)))
            chosen.append(rest - 2.0 * jnp.floor(rest * 0.5))
        all_x = [lists[g][0] + chosen[g] * (lists[g][1] - lists[g][0]) for g in range(4)]
        all_y = [lists[g][0] + chosen[4 + g] * (lists[g][1] - lists[g][0]) for g in range(4)]
        self.own = at_group(me, [lists[g][0] for g in range(4)]), at_group(me, [lists[g][1] for g in range(4)])
        self.slot_x = at_group(me, chosen[:4])
        self.slot_y = at_group(me, chosen[4:])
        got_x, got_y = at_group(me ^ 1, all_x), at_group(me ^ 2, all_y)
        self.got = got_x, got_y
        one = jnp.ones_like(got_x)
        foreign = one - jnp.maximum(equal(got_x, self.own[0]), equal(got_x, self.own[1]))
        self.third = foreign * got_x + (one - foreign) * got_y
        first_x = jnp.where(me < (me ^ 1), one, one - equal(at_group(me, all_x), got_x))
        first_y = jnp.where(me < (me ^ 2), one, one - equal(at_group(me, all_y), got_y))
        also = equal(at_group(me ^ 2, all_x), got_x) * equal(at_group(me ^ 1, all_y), got_x)
        first_far = jnp.where(me < (me ^ 3), one, one - also)
        zero = jnp.zeros_like(one)
        with_x = [equal(got_x, column) * first_x for column in self.own]
        with_y = [equal(got_y, column) * first_y for column in self.own]
        far = equal(got_x, got_y) * first_far
        self.pairs = [
            [one, zero, with_x[0], with_y[0]],
            [zero, one, with_x[1], with_y[1]],
            [with_x[0], with_x[1], zero, far],
            [with_y[0], with_y[1], far, zero],
        ]


class Chosen:
    def __init__(self, ref):
        values = [ref[0:1, place : place + 1] for place in range(20)]
        self.own, self.got = values[0:2], values[2:4]
        self.pairs = [values[4 + 4 * block : 8 + 4 * block] for block in range(4)]

    @staticmethod
    def leave(choice, ref):
        values = [*choice.own, *choice.got] + [value for row in choice.pairs for value in row]
        lane = iota(ref.shape, 1)
        total = jnp.zeros(ref.shape, F32)
        for place, value in enumerate(values):
            total = jnp.where(lane == place, value, total)
        ref[...] = total


def message_kernel(message, virt_hbm, occ_hbm, col_hbm, *refs):
    *outs, out_ref, occ_ref, col_ref, sem = refs
    copies = [
        pltpu.make_async_copy(virt_hbm, out_ref.at[message.virt], sem.at[0]),
        pltpu.make_async_copy(occ_hbm, occ_ref, sem.at[1]),
        pltpu.make_async_copy(col_hbm, col_ref, sem.at[2]),
    ]
    for copy in copies:
        copy.start()
    tile = out_ref.shape[1]
    out_ref[message.occ, :] = jnp.zeros((occ_ref.shape[0], tile), BF16)
    for copy in copies:
        copy.wait()
    out_ref[message.occ, : occ_ref.shape[1]] = occ_ref[...]
    row, lane = iota((16, tile), 0), iota((16, tile), 1)
    value = jnp.zeros((16, tile), F32)
    for slot in range(col_ref.shape[1]):
        here = jnp.logical_and(row == 0, lane == slot)
        value = jnp.where(here, col_ref[0, slot].astype(F32), value)
    out_ref[message.list, :] = value.astype(BF16)
    copies = [pltpu.make_async_copy(out_ref, out, sem.at[3 + at]) for at, out in enumerate(outs)]
    for copy in copies:
        copy.start()
    for copy in copies:
        copy.wait()


def own_kernel(rows_dev, steps, b_ref, *outs):
    half_rows = rows_dev * SUB
    out_rows = 2 * half_rows
    in_rows = PAIR * rows_dev * 2
    line = iota((out_rows, in_rows), 0)
    place = iota((out_rows, in_rows), 1)
    func = (line // half_rows) * SUB + line % SUB
    first = (func * rows_dev + (line % half_rows) // SUB) * 2
    pick = jnp.concatenate([jnp.where(place == first + slot, 1.0, 0.0).astype(BF16) for slot in range(2)], 0)
    for index in range(steps):
        moved = dot(pick, b_ref[index * in_rows : (index + 1) * in_rows, :]).astype(BF16)
        for slot, out in enumerate(outs):
            out[index * out_rows : (index + 1) * out_rows, :] = moved[slot * out_rows : (slot + 1) * out_rows]


def send_kernel(message, *refs):
    messages, (own0, own1), (virt_out, chosen, *outs) = by_distance(refs[2:6]), refs[:2], refs[6:]
    choice = Choice(message, messages)
    Chosen.leave(choice, chosen)
    at = 0
    for to_x, to_y in zip(outs[0::2], outs[1::2]):
        here = slice(at, at + to_x.shape[0])
        to_x[...] = jnp.where(choice.slot_x > 0.5, own1[here, :], own0[here, :])
        to_y[...] = jnp.where(choice.slot_y > 0.5, own1[here, :], own0[here, :])
        at += to_x.shape[0]
    me = lax.axis_index("orb")
    rows = message.virt.stop
    for slot, column in enumerate((choice.own[0], choice.own[1], choice.third)):
        total = jnp.zeros((rows, virt_out.shape[1]), F32)
        for distance in range(4):
            weight = equal(column, (me ^ distance).astype(F32))
            total = total + weight * messages[distance][message.virt, :].astype(F32)
        virt_out[slot * rows : (slot + 1) * rows, :] = total.astype(BF16)


def aux_steps(aux_count):
    steps = []
    distance = aux_count // 2
    while distance:
        steps.append(distance)
        distance //= 2
    return steps


def aux_order(aux_count):
    order = [0]
    for distance in aux_steps(aux_count):
        order = order + [value ^ distance for value in order]
    return order


def virt_kernel(sizes, *refs):
    aux_count, rows_dev, tau_count = sizes
    chosen, virt_ref, virt_out = refs
    choice = Chosen(chosen)
    aux_me = lax.axis_index("aux")
    tile = virt_ref.shape[1]
    part = tile // aux_count
    order = aux_order(aux_count)
    line = iota((tile, virt_ref.shape[0]), 0)
    place = iota((tile, virt_ref.shape[0]), 1)
    virts = []
    for slot in range(3):
        columns = []
        for moment in range(tau_count):
            held = pick_static((line // part) ^ aux_me, [order.index(value) for value in range(aux_count)])
            wanted = ((held * 3 + slot) * tau_count + moment) * part + line % part
            columns.append(dot(jnp.where(place == wanted, 1.0, 0.0).astype(BF16), virt_ref[...]))
        virts.append(jnp.concatenate(columns, 1))
    virt_out[0] = virts[0].astype(BF16)
    virt_out[1] = virts[1].astype(BF16)
    for at, column in enumerate(choice.got):
        one, two = equal(column, choice.own[0]), equal(column, choice.own[1])
        virt_out[2 + at] = (one * virts[0] + two * virts[1] + (1.0 - one - two) * virts[2]).astype(BF16)


def mix_kernel(sizes, message, live_ref, *refs):
    aux_count, rows_dev, tau_count = sizes
    messages, chosen, mix_out = by_distance(refs[:4]), refs[4], refs[5]
    choice = Chosen(chosen)
    me = lax.axis_index("orb")
    tile = messages[0].shape[1]
    rows = 4 * rows_dev
    half_rows = rows_dev * SUB
    groups = [me, me, me ^ 1, me ^ 2]
    occ_all = jnp.concatenate([messages[at][message.occ, :] for at in (0, 0, 1, 2)], 0)
    left_shape = (tau_count * rows * SUB, occ_all.shape[0])
    line = iota(left_shape, 0)
    row_of = (line % (rows * SUB)) // SUB
    wanted = ((row_of // rows_dev) * tau_count + line // (rows * SUB)) * rows_dev + row_of % rows_dev
    left = jnp.where(iota(left_shape, 1) == wanted, 1.0, 0.0).astype(BF16)
    right_shape = (tile, rows * SUB)
    col_of = iota(right_shape, 1) // SUB
    wanted = pick_static(col_of // rows_dev, groups) * rows_dev + col_of % rows_dev
    right = jnp.where(iota(right_shape, 0) == wanted, 1.0, 0.0).astype(BF16)
    spread = dot(dot(left, occ_all).astype(BF16), right)
    same = iota((half_rows, rows * SUB), 0) % SUB == iota((half_rows, rows * SUB), 1) % SUB
    group_of = iota((1, rows * SUB), 1) // half_rows
    for moment in range(tau_count):
        for one in range(4):
            live = jnp.zeros((1, rows * SUB), F32)
            for two in range(4):
                value = live_ref[moment, groups[one], groups[two]].astype(F32) * choice.pairs[one][two]
                live = jnp.where(group_of == two, value, live)
            at = (moment * 4 + one) * half_rows
            keep = jnp.logical_and(same, live != 0.0)
            mix_out[at : at + half_rows, :] = jnp.where(keep, spread[at : at + half_rows], 0.0).astype(BF16)


def virtual_products(rows_dev, tau_count, first, steps, blocks, virts, vir_ref):
    half_rows = rows_dev * SUB
    tile = blocks[0].shape[1]

    def step(index, carry):
        here = pl.ds(pl.multiple_of(index * PAIR, PAIR), PAIR)
        for group, (block, virt) in enumerate(zip(blocks, virts)):
            at = pl.multiple_of((index + first) * 2 * half_rows, half_rows)
            vir = dot(block[pl.ds(at, 2 * half_rows), :], virt).reshape(2, rows_dev, SUB, tau_count * tile)
            vir = jnp.concatenate([vir[0], vir[1]], 1).astype(BF16)
            for moment in range(tau_count):
                for row in range(rows_dev):
                    at = ((moment * len(blocks) + group) * rows_dev + row) * tile
                    vir_ref[here, at : at + tile] = vir[row, :, moment * tile : (moment + 1) * tile]
        return carry

    lax.fori_loop(0, steps, step, 0, unroll=min(steps, UNROLL))


def four_products(rows_dev, tau_count, first, steps, owns, got, mix_ref, virt_ref, occ_ref, vir_ref):
    rows = 4 * rows_dev
    half_rows = rows_dev * SUB
    tile = owns[0].shape[1]
    blocks = [(own, first) for own in owns] + [(block, 0) for block in got]

    def step(index, carry):
        here = pl.ds(pl.multiple_of(index * PAIR, PAIR), PAIR)
        if occ_ref is not None:
            halves = []
            for half in range(2):
                halves.append(jnp.concatenate([
                    block[pl.ds(pl.multiple_of(((index + shift) * 2 + half) * half_rows, half_rows), half_rows), :]
                    for block, shift in blocks
                ], 0))
            occ = dot(mix_ref[...], jnp.concatenate(halves, 1))
            occ = [occ[:, half * tile : (half + 1) * tile].reshape(tau_count * rows, SUB, tile) for half in range(2)]
            occ = jnp.concatenate(occ, 1).astype(BF16)
            for row in range(tau_count * rows):
                occ_ref[here, row * tile : (row + 1) * tile] = occ[row]
        if vir_ref is not None:
            for group, (block, shift) in enumerate(blocks):
                at = pl.multiple_of((index + shift) * 2 * half_rows, half_rows)
                vir = dot(block[pl.ds(at, 2 * half_rows), :], virt_ref[group])
                vir = vir.reshape(2, rows_dev, SUB, tau_count * tile)
                vir = jnp.concatenate([vir[0], vir[1]], 1).astype(BF16)
                for moment in range(tau_count):
                    for row in range(rows_dev):
                        at = (moment * rows + group * rows_dev + row) * tile
                        vir_ref[here, at : at + tile] = vir[row, :, moment * tile : (moment + 1) * tile]
        return carry

    lax.fori_loop(0, steps, step, 0, unroll=min(steps, UNROLL))


def early_occ_kernel(rows_dev, tau_count, steps, mix_ref, own0, own1, from_x, from_y, occ_out):
    four_products(rows_dev, tau_count, 0, steps, [own0, own1], [from_x, from_y], mix_ref, None, occ_out, None)


def early_vir_kernel(rows_dev, tau_count, steps, late_steps, virt_ref, own0, own1, from_x, from_y, vir_out, own_out):
    virts = [virt_ref[0], virt_ref[1]]
    four_products(rows_dev, tau_count, 0, steps, [own0, own1], [from_x, from_y], None, virt_ref, None, vir_out)
    virtual_products(rows_dev, tau_count, steps, late_steps, [own0, own1], virts, own_out)


def late_kernel(rows_dev, tau_count, first, steps, scale, tau_ref, mix_ref, virt_ref, *refs):
    (own0, own1, from_x, from_y, occ_early, vir_early, vir_own) = refs[:7]
    outs, (occ_ref, vir_ref) = refs[7:11], refs[11:]
    four_products(rows_dev, tau_count, first, steps, [own0, own1], [from_x, from_y], mix_ref, None, occ_ref, None)
    virtual_products(rows_dev, tau_count, 0, steps, [from_x, from_y], [virt_ref[2], virt_ref[3]], vir_ref)
    depth = 4 * rows_dev * own0.shape[1]
    chi = None
    for moment in range(tau_count):
        here = slice(moment * depth, (moment + 1) * depth)
        part = slice(moment * depth // 2, (moment + 1) * depth // 2)
        vir_late = jnp.concatenate([vir_own[:, part], vir_ref[:, part]], 1)
        term = lax.dot_general(
            jnp.concatenate([occ_early[:, here], occ_ref[:, here]], 0),
            jnp.concatenate([vir_early[:, here], vir_late], 0),
            (((1,), (1,)), ((), ())), preferred_element_type=F32,
        ) * tau_ref[moment]
        chi = term if chi is None else chi + term
    chi = chi * scale
    me = lax.axis_index("orb")
    share_rows = outs[0].shape[0]
    for distance, out in zip(partners(4), outs):
        picked = chi[0:share_rows]
        for owner in range(1, 4):
            picked = jnp.where(me ^ distance == owner, chi[owner * share_rows : (owner + 1) * share_rows], picked)
        out[...] = picked


def on_device_square(b_rows, col_blocks, g_occ, occ_live, g_virt, tau_weight):
    orb_count = lax.axis_size("orb")
    aux_count = lax.axis_size("aux")
    aux_dev, rows_dev, slot_count, tile = b_rows.shape
    tau_count = g_occ.shape[0]
    rows = orb_count * rows_dev
    steps = aux_dev // PAIR
    share_rows = aux_dev // orb_count
    sizes = (aux_count, rows_dev, tau_count)
    scale = 1.0 / math.sqrt(rows * tile * orb_count)
    smem = pl.BlockSpec(memory_space=pltpu.SMEM)
    vmem = pl.BlockSpec(memory_space=pltpu.VMEM)
    hbm = pl.BlockSpec(memory_space=pl.ANY)

    def call(kernel, name, out_shape, in_specs, scratch, limit, out_spec=vmem, flops=0):
        return pl.pallas_call(
            kernel, out_shape=out_shape, in_specs=in_specs, out_specs=[out_spec] * len(out_shape),
            scratch_shapes=scratch, compiler_params=pltpu.CompilerParams(vmem_limit_bytes=limit << 20), name=name,
            cost_estimate=pl.CostEstimate(flops=flops, bytes_accessed=0, transcendentals=0) if flops else None,
        )

    def xor(value, axis, distance):
        return lax.ppermute(value, axis, [(i, i ^ distance) for i in range(lax.axis_size(axis))])

    def half(*shape):
        return jax.ShapeDtypeStruct(shape, BF16)

    flat = b_rows.reshape(-1, tile)
    virt = g_virt.reshape(-1, tile)
    occ = g_occ.reshape(tau_count * rows_dev, -1)
    message = Message(virt.shape[0], occ.shape[0])
    dma = pltpu.SemaphoreType.DMA
    sent = call(
        functools.partial(message_kernel, message), "message", [half(message.rows, tile)] * orb_count, [hbm] * 3,
        [
            pltpu.VMEM((message.rows, tile), BF16), pltpu.VMEM(occ.shape, BF16),
            pltpu.SMEM(col_blocks.shape, jnp.int32), dma((3 + orb_count,)),
        ], 60, hbm, 10**10,
    )(virt, occ, col_blocks)
    came = {distance: xor(part, "orb", distance) for distance, part in zip(partners(orb_count)[1:], sent[1:])}
    messages = [sent[0]] + [came[distance] for distance in partners(orb_count)[1:]]
    block = half(aux_dev * rows_dev, tile)
    owns = call(functools.partial(own_kernel, rows_dev, steps), "own", [block] * 2, [vmem], [], 6, vmem, 10**10)(flat)
    early = steps * 12 // 16
    chunks = (early, steps - early)
    virt, chosen, *sends = call(
        functools.partial(send_kernel, message), "send",
        [half(3 * message.virt.stop, tile), jax.ShapeDtypeStruct((8, tile), F32)]
        + [half(count * PAIR * rows_dev, tile) for count in chunks for _ in range(2)],
        [vmem] * 6, [], 6, vmem, 10**10,
    )(*owns, *messages)
    got = [(xor(to_x, "orb", 1), xor(to_y, "orb", 2)) for to_x, to_y in zip(sends[0::2], sends[1::2])]
    (mix,) = call(
        functools.partial(mix_kernel, sizes, message), "mix",
        [half(tau_count * rows * SUB, rows * SUB)], [smem] + [vmem] * 5, [], 8,
    )(occ_live, *messages, chosen)
    wide = tau_count * rows * tile
    first = half(early * PAIR, wide)
    (occ_early,) = call(
        functools.partial(early_occ_kernel, rows_dev, tau_count, early), "occ", [first], [vmem] * 5, [], 6
    )(mix, *owns, *got[0])
    distances = aux_steps(aux_count)
    for number, distance in enumerate(distances):
        pair, other = half(2 * virt.shape[0], tile), xor(virt, "aux", distance)
        anchor = {0: mix, len(distances) - 1: occ_early}.get(number)
        if anchor is None:
            (virt,) = call(join_kernel, "join", [pair], [vmem] * 2, [], 4)(virt, other)
        else:
            (virt,) = call(join_after_kernel, "join", [pair], [vmem] * 2 + [hbm], [], 4)(virt, other, anchor)
    (virt,) = call(
        functools.partial(virt_kernel, sizes), "virt", [half(4, tile, tau_count * tile)], [vmem] * 2, [], 8
    )(chosen, virt)
    vir_early, vir_own = call(
        functools.partial(early_vir_kernel, rows_dev, tau_count, early, steps - early), "vir",
        [first, half((steps - early) * PAIR, wide // 2)], [vmem] * 5, [], 6
    )(virt, *owns, *got[0])
    shares = call(
        functools.partial(late_kernel, rows_dev, tau_count, early, steps - early, scale), "late",
        [jax.ShapeDtypeStruct((share_rows, aux_dev), F32)] * orb_count, [smem] + [vmem] * 9,
        [pltpu.VMEM(((steps - early) * PAIR, wide), BF16), pltpu.VMEM(((steps - early) * PAIR, wide // 2), BF16)], 16,
    )(tau_weight, mix, virt, *owns, *got[1], occ_early, vir_early, vir_own)
    total = shares[0]
    for distance, share in zip(partners(orb_count)[1:], shares[1:]):
        total = total + xor(share, "orb", distance)
    return total


def on_device(b_rows, col_blocks, g_occ, occ_live, g_virt, tau_weight):
    square = lax.axis_size("orb") == 4 and b_rows.shape[2] == 2
    plan = on_device_square if square else on_device_dense
    return plan(b_rows, col_blocks, g_occ, occ_live, g_virt, tau_weight)


def solution(mesh):
    in_specs = (
        P("aux", "orb", None, None),
        P("orb", None),
        P(None, "orb", None),
        P(),
        P(None, "orb", "aux", None),
        P(),
    )
    out_specs = P("orb", "aux")
    return jax.shard_map(
        on_device, mesh=mesh, in_specs=in_specs, out_specs=out_specs, check_vma=False
    )
```

```python
import functools
import math

import jax
import jax.numpy as jnp
from jax import lax
from jax.experimental import pallas as pl
from jax.experimental.pallas import tpu as pltpu
from jax.sharding import PartitionSpec as P

SUB = 8
PAIR = 16
UNROLL = 16
F32 = jnp.float32
BF16 = jnp.bfloat16


def iota(shape, dim):
    return lax.broadcasted_iota(jnp.int32, shape, dim)


def dot(a, b):
    return jnp.dot(a, b, preferred_element_type=F32)


def partners(count):
    return [0] + sorted(range(1, count), key=lambda distance: (-distance.bit_count(), distance))


def pick_static(index, values):
    found = jnp.zeros_like(index)
    for place, value in enumerate(values):
        found = jnp.where(index == place, value, found)
    return found


def pack_kernel(rows_dev, slot_count, chunks, pieces, col_hbm, b_hbm, occ_hbm, *refs):
    orb_count = lax.axis_size("orb")
    count = len(chunks) * orb_count
    outs, helds = refs[:count], refs[count : 2 * count]
    b_ref, occ_ref, col_ref, b_sem, occ_sem, col_sem, out_sem = refs[2 * count :]
    me = lax.axis_index("orb")
    half_rows = rows_dev * SUB
    out_rows = 2 * half_rows
    in_rows = PAIR * rows_dev * slot_count
    steps = sum(chunks)
    piece_steps = steps // pieces
    piece_rows = piece_steps * in_rows

    def fetch(piece):
        here = pl.ds(piece * piece_rows, piece_rows)
        return pltpu.make_async_copy(b_hbm.at[here], b_ref.at[here], b_sem.at[piece])

    occ_copy = pltpu.make_async_copy(occ_hbm, occ_ref, occ_sem)
    col_copy = pltpu.make_async_copy(col_hbm, col_ref, col_sem)
    col_copy.start()
    for piece in range(pieces):
        fetch(piece).start()
    occ_copy.start()
    line = iota((out_rows, in_rows), 0)
    place = iota((out_rows, in_rows), 1)
    half = line // half_rows
    row = (line % half_rows) // SUB
    func = half * SUB + line % SUB
    first = (func * rows_dev + row) * slot_count
    pick = jnp.concatenate(
        [jnp.where(place == first + slot, 1.0, 0.0).astype(BF16) for slot in range(slot_count)], 0
    )
    occ_copy.wait()
    total = chunks[0] * out_rows
    for held in helds[:orb_count]:
        held[total:, :] = jnp.zeros((held.shape[0] - total, held.shape[1]), BF16)
        held[total:, : occ_ref.shape[1]] = occ_ref[...]
    col_copy.wait()

    def step(index, group, start):
        at = pl.multiple_of(index * in_rows, in_rows)
        moved = dot(pick, b_ref[pl.ds(at, in_rows), :]).astype(BF16)
        slots = [moved[slot * out_rows : (slot + 1) * out_rows] for slot in range(slot_count)]
        zero = jnp.zeros_like(slots[0])
        for distance, held in zip(partners(orb_count), group):
            value = zero
            for slot in range(slot_count):
                value = jnp.where(col_ref[0, slot] == me ^ distance, slots[slot], value)
            held[pl.ds(pl.multiple_of((index - start) * out_rows, out_rows), out_rows), :] = value

    sent = []
    start = 0
    for number, chunk in enumerate(chunks):
        group = range(number * orb_count, (number + 1) * orb_count)
        for piece in range(start // piece_steps, (start + chunk) // piece_steps):
            fetch(piece).wait()
            low = piece * piece_steps
            lax.fori_loop(
                low, low + piece_steps,
                lambda index, carry: (step(index, [helds[at] for at in group], start), carry)[1],
                0, unroll=True,
            )
            top = low - start + piece_steps
            low_row = (low - start) * out_rows
            high_row = helds[group[0]].shape[0] if top == chunk else top * out_rows
            for place, at in enumerate(group):
                here = pl.ds(low_row, high_row - low_row)
                copy = pltpu.make_async_copy(helds[at].at[here], outs[at].at[here], out_sem.at[piece, place])
                copy.start()
                sent.append(copy)
        start += chunk
    for copy in sent:
        copy.wait()


def stage_kernel(orb_count, own_count, live_hbm, one_ref, two_ref, *refs):
    owns, outs = refs[:own_count], refs[own_count : 2 * own_count]
    live_out, join_out, live_ref, live_sem, own_sem = refs[2 * own_count :]
    live_copy = pltpu.make_async_copy(live_hbm, live_ref, live_sem)
    live_copy.start()
    copies = [pltpu.make_async_copy(own, out, own_sem.at[at]) for at, (own, out) in enumerate(zip(owns, outs))]
    for copy in copies:
        copy.start()
    join_out[: one_ref.shape[0], :] = one_ref[...]
    join_out[one_ref.shape[0] :, :] = two_ref[...]
    live_copy.wait()
    me = lax.axis_index("orb")
    order = partners(orb_count)
    tau_count = live_ref.shape[0]
    width = live_out.shape[1]
    group_of = iota((1, width), 1) // (width // orb_count)
    for moment in range(tau_count):
        for row_group in range(orb_count):
            live = jnp.zeros((1, width), jnp.int32)
            for col_group in range(orb_count):
                value = live_ref[moment, me ^ order[row_group], me ^ order[col_group]]
                live = jnp.where(group_of == col_group, value, live)
            at = moment * orb_count + row_group
            live_out[at : at + 1, :] = live
    for copy in copies:
        copy.wait()


def join_after_kernel(one_ref, two_ref, anchor, out_ref):
    join_kernel(one_ref, two_ref, out_ref)


def join_kernel(one_ref, two_ref, out_ref):
    out_ref[: one_ref.shape[0], :] = one_ref[...]
    out_ref[one_ref.shape[0] :, :] = two_ref[...]


def order_virt(sizes, virt_refs, virt_out):
    orb_count, aux_count, rows_dev, tau_count = sizes
    aux_me = lax.axis_index("aux")
    tile = virt_refs[0].shape[1]
    part = tile // aux_count
    virt_all = jnp.concatenate([ref[...] for ref in virt_refs], 0)
    line = iota((tile, virt_all.shape[0]), 0)
    place = iota((tile, virt_all.shape[0]), 1)
    for moment in range(tau_count):
        wanted = (((line // part) ^ aux_me) * tau_count + moment) * part + line % part
        chosen = dot(jnp.where(place == wanted, 1.0, 0.0).astype(BF16), virt_all)
        virt_out[:, moment * tile : (moment + 1) * tile] = chosen.astype(BF16)


def spread_occ(sizes, live_ref, blocks, total, mix_out):
    orb_count, aux_count, rows_dev, tau_count = sizes
    me = lax.axis_index("orb")
    rows = orb_count * rows_dev
    half_rows = rows_dev * SUB
    tile = blocks[0].shape[1]
    occ_all = jnp.concatenate([block[total : total + tau_count * rows_dev, :] for block in blocks], 0)
    left_shape = (tau_count * rows * SUB, occ_all.shape[0])
    line = iota(left_shape, 0)
    moment_of = line // (rows * SUB)
    row_of = (line % (rows * SUB)) // SUB
    wanted = ((row_of // rows_dev) * tau_count + moment_of) * rows_dev + row_of % rows_dev
    left = jnp.where(iota(left_shape, 1) == wanted, 1.0, 0.0).astype(BF16)
    right_shape = (tile, rows * SUB)
    col_of = iota(right_shape, 1) // SUB
    group = pick_static(col_of // rows_dev, partners(orb_count)) ^ me
    wanted = group * rows_dev + col_of % rows_dev
    right = jnp.where(iota(right_shape, 0) == wanted, 1.0, 0.0).astype(BF16)
    spread = dot(dot(left, occ_all).astype(BF16), right)
    same = iota((half_rows, rows * SUB), 0) % SUB == iota((half_rows, rows * SUB), 1) % SUB
    for at in range(tau_count * orb_count):
        here = slice(at * half_rows, (at + 1) * half_rows)
        keep = jnp.logical_and(same, live_ref[at : at + 1, :] != 0)
        mix_out[here, :] = jnp.where(keep, spread[here], 0.0).astype(BF16)


def products(sizes, steps, blocks, mix_ref, virt_ref, occ_out, vir_out):
    orb_count, aux_count, rows_dev, tau_count = sizes
    rows = orb_count * rows_dev
    half_rows = rows_dev * SUB
    tile = blocks[0].shape[1]

    def step(index, carry):
        here = pl.ds(pl.multiple_of(index * PAIR, PAIR), PAIR)
        halves = []
        for half in range(2):
            at = pl.multiple_of((index * 2 + half) * half_rows, half_rows)
            halves.append(jnp.concatenate([block[pl.ds(at, half_rows), :] for block in blocks], 0))
        if occ_out is not None:
            occ = dot(mix_ref[...], jnp.concatenate(halves, 1))
            occ = [occ[:, half * tile : (half + 1) * tile].reshape(tau_count * rows, SUB, tile) for half in range(2)]
            occ = jnp.concatenate(occ, 1).astype(BF16)
            for row in range(tau_count * rows):
                occ_out[here, row * tile : (row + 1) * tile] = occ[row]
        if vir_out is not None:
            vir = dot(jnp.concatenate(halves, 0), virt_ref[...]).reshape(2, rows, SUB, tau_count * tile)
            vir = jnp.concatenate([vir[0], vir[1]], 1).astype(BF16)
            for moment in range(tau_count):
                for row in range(rows):
                    at = (moment * rows + row) * tile
                    vir_out[here, at : at + tile] = vir[row, :, moment * tile : (moment + 1) * tile]
        return carry

    lax.fori_loop(0, steps, step, 0, unroll=min(steps, UNROLL))


def occ_kernel(sizes, steps, live_ref, *refs):
    blocks, (mix_out, occ_out) = refs[: sizes[0]], refs[sizes[0] :]
    spread_occ(sizes, live_ref, blocks, steps * 2 * sizes[2] * SUB, mix_out)
    products(sizes, steps, blocks, mix_out, None, occ_out, None)


def vir_kernel(sizes, steps, *refs):
    blocks, virt_refs = refs[: sizes[0]], refs[sizes[0] : -3]
    anchor, virt_out, vir_out = refs[-3:]
    order_virt(sizes, virt_refs, virt_out)
    products(sizes, steps, blocks, None, virt_out, None, vir_out)


def last_kernel(sizes, steps, share_rows, tau_ref, mix_ref, virt_ref, occ_first, vir_first, *refs):
    orb_count, aux_count, rows_dev, tau_count = sizes
    blocks, outs = refs[:orb_count], refs[orb_count : 2 * orb_count]
    occ_last, vir_last = refs[2 * orb_count :]
    products(sizes, steps, blocks, mix_ref, virt_ref, occ_last, vir_last)
    me = lax.axis_index("orb")
    rows = orb_count * rows_dev
    tile = blocks[0].shape[1]
    depth = rows * tile
    part = min(depth, 4096)
    chi = None
    for moment in range(tau_count):
        for piece in range(depth // part):
            here = slice(moment * depth + piece * part, moment * depth + (piece + 1) * part)
            term = lax.dot_general(
                jnp.concatenate([occ_first[:, here], occ_last[:, here]], 0),
                jnp.concatenate([vir_first[:, here], vir_last[:, here]], 0),
                (((1,), (1,)), ((), ())), preferred_element_type=F32,
            ) * tau_ref[moment]
            chi = term if chi is None else chi + term
    chi = chi * (1.0 / math.sqrt(rows * tile * orb_count))
    for distance, out in zip(partners(orb_count), outs):
        picked = chi[0:share_rows]
        for owner in range(1, orb_count):
            picked = jnp.where(me ^ distance == owner, chi[owner * share_rows : (owner + 1) * share_rows], picked)
        out[...] = picked


def on_device_dense(b_rows, col_blocks, g_occ, occ_live, g_virt, tau_weight):
    orb_count = lax.axis_size("orb")
    aux_count = lax.axis_size("aux")
    aux_dev, rows_dev, slot_count, tile = b_rows.shape
    tau_count = g_occ.shape[0]
    rows = orb_count * rows_dev
    share_rows = aux_dev // orb_count
    sizes = (orb_count, aux_count, rows_dev, tau_count)
    smem = pl.BlockSpec(memory_space=pltpu.SMEM)
    vmem = pl.BlockSpec(memory_space=pltpu.VMEM)

    def call(kernel, name, out_shape, in_specs, scratch, spare, out_spec=vmem):
        held = sum(math.prod(shape.shape) * 2 for shape in scratch if shape.dtype == BF16)
        return pl.pallas_call(
            kernel,
            out_shape=out_shape,
            in_specs=in_specs,
            out_specs=[out_spec] * len(out_shape),
            scratch_shapes=scratch,
            compiler_params=pltpu.CompilerParams(vmem_limit_bytes=min(held + (spare << 20), 60 << 20)),
            name=name,
        )

    def xor(value, axis, distance):
        return lax.ppermute(value, axis, [(i, i ^ distance) for i in range(lax.axis_size(axis))])

    def half(value):
        return jax.ShapeDtypeStruct(value, BF16)

    all_steps = aux_dev // PAIR
    chunks = (all_steps * 12 // 16, all_steps - all_steps * 12 // 16)
    occ_rows = tau_count * rows_dev
    b_flat = b_rows.reshape(-1, tile)
    occ_flat = g_occ.reshape(occ_rows, -1)
    hbm = pl.BlockSpec(memory_space=pl.ANY)
    pieces = math.gcd(4, all_steps)
    shapes = [
        (steps * PAIR * rows_dev + (0 if number else occ_rows), tile)
        for number, steps in enumerate(chunks) for _ in range(orb_count)
    ]
    blocks = call(
        functools.partial(pack_kernel, rows_dev, slot_count, chunks, pieces), "pack",
        [half(shape) for shape in shapes], [hbm] * 3,
        [pltpu.VMEM(shape, BF16) for shape in shapes] + [
            pltpu.VMEM(b_flat.shape, BF16), pltpu.VMEM(occ_flat.shape, BF16), pltpu.SMEM(col_blocks.shape, jnp.int32),
            pltpu.SemaphoreType.DMA((pieces,)), pltpu.SemaphoreType.DMA, pltpu.SemaphoreType.DMA,
            pltpu.SemaphoreType.DMA((pieces, orb_count)),
        ], 54, hbm,
    )(col_blocks, b_flat, occ_flat)
    order = partners(orb_count)
    dense = []
    for number in range(len(chunks)):
        own, *others = blocks[number * orb_count : (number + 1) * orb_count]
        dense.append([own] + [xor(value, "orb", d) for d, value in zip(order[1:], others)])
    virt = g_virt.reshape(-1, tile)
    owns = [blocks[number * orb_count] for number in range(len(chunks))]
    *owns, live, virt = call(
        functools.partial(stage_kernel, orb_count, len(chunks)), "stage",
        [half(own.shape) for own in owns]
        + [jax.ShapeDtypeStruct((tau_count * orb_count, rows * SUB), jnp.int32), half((2 * virt.shape[0], tile))],
        [hbm, vmem, vmem] + [hbm] * len(owns),
        [pltpu.SMEM(occ_live.shape, jnp.int32), pltpu.SemaphoreType.DMA, pltpu.SemaphoreType.DMA((len(owns),))], 4,
    )(occ_live, virt, xor(virt, "aux", 1), *owns)
    for own, group in zip(owns, dense):
        group[0] = own
    distance = 2
    while distance < aux_count:
        pair = half((2 * virt.shape[0], tile))
        virt = call(join_kernel, "join", [pair], [vmem] * 2, [], 2)(virt, xor(virt, "aux", distance))[0]
        distance *= 2
    virts = [virt]
    wide = half((chunks[0] * PAIR, tau_count * rows * tile))
    mix, occ_first = call(
        functools.partial(occ_kernel, sizes, chunks[0]), "occ",
        [half((tau_count * rows * SUB, rows * SUB)), wide],
        [vmem] * (1 + orb_count), [], 8,
    )(live, *dense[0])
    virt, vir_first = call(
        functools.partial(vir_kernel, sizes, chunks[0]), "vir",
        [half((tile, tau_count * tile)), wide],
        [vmem] * (orb_count + len(virts)) + [hbm], [], 8,
    )(*dense[0], *virts, mix)
    shares = call(
        functools.partial(last_kernel, sizes, chunks[1], share_rows), "last",
        [jax.ShapeDtypeStruct((share_rows, aux_dev), F32)] * orb_count,
        [smem] + [vmem] * (4 + orb_count),
        [pltpu.VMEM((chunks[1] * PAIR, tau_count * rows * tile), BF16)] * 2, 12,
    )(tau_weight, mix, virt, occ_first, vir_first, *dense[1])
    total = shares[0]
    for distance, share in zip(order[1:], shares[1:]):
        total = total + xor(share, "orb", distance)
    return total


class Message:
    def __init__(self, virt_rows, occ_rows):
        self.virt = slice(0, virt_rows)
        self.occ = slice(virt_rows, virt_rows + occ_rows)
        self.list = slice(virt_rows + occ_rows, virt_rows + occ_rows + 16)
        self.rows = virt_rows + occ_rows + 16


def equal(one, two):
    return jnp.where(one == two, 1.0, 0.0)


def by_distance(refs):
    return [refs[partners(4).index(distance)] for distance in range(4)]


def at_group(group, values):
    found = values[0]
    for place in range(1, len(values)):
        found = jnp.where(group == place, values[place], found)
    return found


class Choice:
    def __init__(self, message, refs):
        me = lax.axis_index("orb")
        near = []
        for ref in refs:
            row = ref[message.list, :].astype(F32)[0:1, :]
            near.append([row[:, slot : slot + 1] for slot in range(2)])
        lists = [[at_group(me ^ group, [near[d][slot] for d in range(4)]) for slot in range(2)] for group in range(4)]
        shape = (8, 128)
        index = iota(shape, 0) * shape[1] + iota(shape, 1)
        bits = [((index >> place) & 1).astype(F32) for place in range(8)]
        sent_x = [lists[g][0] + bits[g] * (lists[g][1] - lists[g][0]) for g in range(4)]
        sent_y = [lists[g][0] + bits[4 + g] * (lists[g][1] - lists[g][0]) for g in range(4)]
        good = jnp.where(index < 256, 1.0, 0.0)
        for one, two in ((0, 1), (2, 3), (0, 2), (1, 3), (0, 3), (1, 2)):
            for slot in range(2):
                column = lists[one][slot]
                shared = jnp.maximum(equal(column, lists[two][0]), equal(column, lists[two][1]))
                if two == one ^ 1:
                    met = jnp.maximum(equal(sent_x[one], column), equal(sent_x[two], column))
                elif two == one ^ 2:
                    met = jnp.maximum(equal(sent_y[one], column), equal(sent_y[two], column))
                else:
                    met = jnp.maximum(
                        equal(sent_x[one], column) * equal(sent_y[two], column),
                        equal(sent_y[one], column) * equal(sent_x[two], column),
                    )
                good = good * jnp.maximum(met, 1.0 - shared)
        number = jnp.where(good > 0.5, index.astype(F32), 1024.0)
        number = jnp.min(jnp.min(number, axis=1, keepdims=True), axis=0, keepdims=True)
        chosen = []
        for place in range(8):
            rest = jnp.floor(number * (1.0 / (1 << place)))
            chosen.append(rest - 2.0 * jnp.floor(rest * 0.5))
        all_x = [lists[g][0] + chosen[g] * (lists[g][1] - lists[g][0]) for g in range(4)]
        all_y = [lists[g][0] + chosen[4 + g] * (lists[g][1] - lists[g][0]) for g in range(4)]
        self.own = at_group(me, [lists[g][0] for g in range(4)]), at_group(me, [lists[g][1] for g in range(4)])
        self.slot_x = at_group(me, chosen[:4])
        self.slot_y = at_group(me, chosen[4:])
        got_x, got_y = at_group(me ^ 1, all_x), at_group(me ^ 2, all_y)
        self.got = got_x, got_y
        one = jnp.ones_like(got_x)
        foreign = one - jnp.maximum(equal(got_x, self.own[0]), equal(got_x, self.own[1]))
        self.third = foreign * got_x + (one - foreign) * got_y
        first_x = jnp.where(me < (me ^ 1), one, one - equal(at_group(me, all_x), got_x))
        first_y = jnp.where(me < (me ^ 2), one, one - equal(at_group(me, all_y), got_y))
        also = equal(at_group(me ^ 2, all_x), got_x) * equal(at_group(me ^ 1, all_y), got_x)
        first_far = jnp.where(me < (me ^ 3), one, one - also)
        zero = jnp.zeros_like(one)
        with_x = [equal(got_x, column) * first_x for column in self.own]
        with_y = [equal(got_y, column) * first_y for column in self.own]
        far = equal(got_x, got_y) * first_far
        self.pairs = [
            [one, zero, with_x[0], with_y[0]],
            [zero, one, with_x[1], with_y[1]],
            [with_x[0], with_x[1], zero, far],
            [with_y[0], with_y[1], far, zero],
        ]


class Chosen:
    def __init__(self, ref):
        values = [ref[0:1, place : place + 1] for place in range(20)]
        self.own, self.got = values[0:2], values[2:4]
        self.pairs = [values[4 + 4 * block : 8 + 4 * block] for block in range(4)]

    @staticmethod
    def leave(choice, ref):
        values = [*choice.own, *choice.got] + [value for row in choice.pairs for value in row]
        lane = iota(ref.shape, 1)
        total = jnp.zeros(ref.shape, F32)
        for place, value in enumerate(values):
            total = jnp.where(lane == place, value, total)
        ref[...] = total


def message_kernel(message, virt_hbm, occ_hbm, col_hbm, *refs):
    *outs, out_ref, occ_ref, col_ref, sem = refs
    copies = [
        pltpu.make_async_copy(virt_hbm, out_ref.at[message.virt], sem.at[0]),
        pltpu.make_async_copy(occ_hbm, occ_ref, sem.at[1]),
        pltpu.make_async_copy(col_hbm, col_ref, sem.at[2]),
    ]
    for copy in copies:
        copy.start()
    tile = out_ref.shape[1]
    out_ref[message.occ, :] = jnp.zeros((occ_ref.shape[0], tile), BF16)
    for copy in copies:
        copy.wait()
    out_ref[message.occ, : occ_ref.shape[1]] = occ_ref[...]
    row, lane = iota((16, tile), 0), iota((16, tile), 1)
    value = jnp.zeros((16, tile), F32)
    for slot in range(col_ref.shape[1]):
        here = jnp.logical_and(row == 0, lane == slot)
        value = jnp.where(here, col_ref[0, slot].astype(F32), value)
    out_ref[message.list, :] = value.astype(BF16)
    copies = [pltpu.make_async_copy(out_ref, out, sem.at[3 + at]) for at, out in enumerate(outs)]
    for copy in copies:
        copy.start()
    for copy in copies:
        copy.wait()


def own_kernel(rows_dev, steps, b_ref, *outs):
    half_rows = rows_dev * SUB
    out_rows = 2 * half_rows
    in_rows = PAIR * rows_dev * 2
    line = iota((out_rows, in_rows), 0)
    place = iota((out_rows, in_rows), 1)
    func = (line // half_rows) * SUB + line % SUB
    first = (func * rows_dev + (line % half_rows) // SUB) * 2
    pick = jnp.concatenate([jnp.where(place == first + slot, 1.0, 0.0).astype(BF16) for slot in range(2)], 0)
    for index in range(steps):
        moved = dot(pick, b_ref[index * in_rows : (index + 1) * in_rows, :]).astype(BF16)
        for slot, out in enumerate(outs):
            out[index * out_rows : (index + 1) * out_rows, :] = moved[slot * out_rows : (slot + 1) * out_rows]


def send_kernel(message, *refs):
    messages, (own0, own1), (virt_out, chosen, *outs) = by_distance(refs[2:6]), refs[:2], refs[6:]
    choice = Choice(message, messages)
    Chosen.leave(choice, chosen)
    at = 0
    for to_x, to_y in zip(outs[0::2], outs[1::2]):
        here = slice(at, at + to_x.shape[0])
        to_x[...] = jnp.where(choice.slot_x > 0.5, own1[here, :], own0[here, :])
        to_y[...] = jnp.where(choice.slot_y > 0.5, own1[here, :], own0[here, :])
        at += to_x.shape[0]
    me = lax.axis_index("orb")
    rows = message.virt.stop
    for slot, column in enumerate((choice.own[0], choice.own[1], choice.third)):
        total = jnp.zeros((rows, virt_out.shape[1]), F32)
        for distance in range(4):
            weight = equal(column, (me ^ distance).astype(F32))
            total = total + weight * messages[distance][message.virt, :].astype(F32)
        virt_out[slot * rows : (slot + 1) * rows, :] = total.astype(BF16)


def aux_steps(aux_count):
    steps = []
    distance = aux_count // 2
    while distance:
        steps.append(distance)
        distance //= 2
    return steps


def aux_order(aux_count):
    order = [0]
    for distance in aux_steps(aux_count):
        order = order + [value ^ distance for value in order]
    return order


def virt_kernel(sizes, *refs):
    aux_count, rows_dev, tau_count = sizes
    chosen, virt_ref, virt_out = refs
    choice = Chosen(chosen)
    aux_me = lax.axis_index("aux")
    tile = virt_ref.shape[1]
    part = tile // aux_count
    order = aux_order(aux_count)
    line = iota((tile, virt_ref.shape[0]), 0)
    place = iota((tile, virt_ref.shape[0]), 1)
    virts = []
    for slot in range(3):
        columns = []
        for moment in range(tau_count):
            held = pick_static((line // part) ^ aux_me, [order.index(value) for value in range(aux_count)])
            wanted = ((held * 3 + slot) * tau_count + moment) * part + line % part
            columns.append(dot(jnp.where(place == wanted, 1.0, 0.0).astype(BF16), virt_ref[...]))
        virts.append(jnp.concatenate(columns, 1))
    virt_out[0] = virts[0].astype(BF16)
    virt_out[1] = virts[1].astype(BF16)
    for at, column in enumerate(choice.got):
        one, two = equal(column, choice.own[0]), equal(column, choice.own[1])
        virt_out[2 + at] = (one * virts[0] + two * virts[1] + (1.0 - one - two) * virts[2]).astype(BF16)


def mix_kernel(sizes, message, live_ref, *refs):
    aux_count, rows_dev, tau_count = sizes
    messages, chosen, mix_out = by_distance(refs[:4]), refs[4], refs[5]
    choice = Chosen(chosen)
    me = lax.axis_index("orb")
    tile = messages[0].shape[1]
    rows = 4 * rows_dev
    half_rows = rows_dev * SUB
    groups = [me, me, me ^ 1, me ^ 2]
    occ_all = jnp.concatenate([messages[at][message.occ, :] for at in (0, 0, 1, 2)], 0)
    left_shape = (tau_count * rows * SUB, occ_all.shape[0])
    line = iota(left_shape, 0)
    row_of = (line % (rows * SUB)) // SUB
    wanted = ((row_of // rows_dev) * tau_count + line // (rows * SUB)) * rows_dev + row_of % rows_dev
    left = jnp.where(iota(left_shape, 1) == wanted, 1.0, 0.0).astype(BF16)
    right_shape = (tile, rows * SUB)
    col_of = iota(right_shape, 1) // SUB
    wanted = pick_static(col_of // rows_dev, groups) * rows_dev + col_of % rows_dev
    right = jnp.where(iota(right_shape, 0) == wanted, 1.0, 0.0).astype(BF16)
    spread = dot(dot(left, occ_all).astype(BF16), right)
    same = iota((half_rows, rows * SUB), 0) % SUB == iota((half_rows, rows * SUB), 1) % SUB
    group_of = iota((1, rows * SUB), 1) // half_rows
    for moment in range(tau_count):
        for one in range(4):
            live = jnp.zeros((1, rows * SUB), F32)
            for two in range(4):
                value = live_ref[moment, groups[one], groups[two]].astype(F32) * choice.pairs[one][two]
                live = jnp.where(group_of == two, value, live)
            at = (moment * 4 + one) * half_rows
            keep = jnp.logical_and(same, live != 0.0)
            mix_out[at : at + half_rows, :] = jnp.where(keep, spread[at : at + half_rows], 0.0).astype(BF16)


def virtual_products(rows_dev, tau_count, first, steps, blocks, virts, vir_ref):
    half_rows = rows_dev * SUB
    tile = blocks[0].shape[1]

    def step(index, carry):
        here = pl.ds(pl.multiple_of(index * PAIR, PAIR), PAIR)
        for group, (block, virt) in enumerate(zip(blocks, virts)):
            at = pl.multiple_of((index + first) * 2 * half_rows, half_rows)
            vir = dot(block[pl.ds(at, 2 * half_rows), :], virt).reshape(2, rows_dev, SUB, tau_count * tile)
            vir = jnp.concatenate([vir[0], vir[1]], 1).astype(BF16)
            for moment in range(tau_count):
                for row in range(rows_dev):
                    at = ((moment * len(blocks) + group) * rows_dev + row) * tile
                    vir_ref[here, at : at + tile] = vir[row, :, moment * tile : (moment + 1) * tile]
        return carry

    lax.fori_loop(0, steps, step, 0, unroll=min(steps, UNROLL))


def four_products(rows_dev, tau_count, first, steps, owns, got, mix_ref, virt_ref, occ_ref, vir_ref):
    rows = 4 * rows_dev
    half_rows = rows_dev * SUB
    tile = owns[0].shape[1]
    blocks = [(own, first) for own in owns] + [(block, 0) for block in got]

    def step(index, carry):
        here = pl.ds(pl.multiple_of(index * PAIR, PAIR), PAIR)
        if occ_ref is not None:
            halves = []
            for half in range(2):
                halves.append(jnp.concatenate([
                    block[pl.ds(pl.multiple_of(((index + shift) * 2 + half) * half_rows, half_rows), half_rows), :]
                    for block, shift in blocks
                ], 0))
            occ = dot(mix_ref[...], jnp.concatenate(halves, 1))
            occ = [occ[:, half * tile : (half + 1) * tile].reshape(tau_count * rows, SUB, tile) for half in range(2)]
            occ = jnp.concatenate(occ, 1).astype(BF16)
            for row in range(tau_count * rows):
                occ_ref[here, row * tile : (row + 1) * tile] = occ[row]
        if vir_ref is not None:
            for group, (block, shift) in enumerate(blocks):
                at = pl.multiple_of((index + shift) * 2 * half_rows, half_rows)
                vir = dot(block[pl.ds(at, 2 * half_rows), :], virt_ref[group])
                vir = vir.reshape(2, rows_dev, SUB, tau_count * tile)
                vir = jnp.concatenate([vir[0], vir[1]], 1).astype(BF16)
                for moment in range(tau_count):
                    for row in range(rows_dev):
                        at = (moment * rows + group * rows_dev + row) * tile
                        vir_ref[here, at : at + tile] = vir[row, :, moment * tile : (moment + 1) * tile]
        return carry

    lax.fori_loop(0, steps, step, 0, unroll=min(steps, UNROLL))


def early_occ_kernel(rows_dev, tau_count, steps, mix_ref, own0, own1, from_x, from_y, occ_out):
    four_products(rows_dev, tau_count, 0, steps, [own0, own1], [from_x, from_y], mix_ref, None, occ_out, None)


def early_vir_kernel(rows_dev, tau_count, steps, late_steps, virt_ref, own0, own1, from_x, from_y, vir_out, own_out):
    virts = [virt_ref[0], virt_ref[1]]
    four_products(rows_dev, tau_count, 0, steps, [own0, own1], [from_x, from_y], None, virt_ref, None, vir_out)
    virtual_products(rows_dev, tau_count, steps, late_steps, [own0, own1], virts, own_out)


def late_kernel(rows_dev, tau_count, first, steps, scale, tau_ref, mix_ref, virt_ref, *refs):
    (own0, own1, from_x, from_y, occ_early, vir_early, vir_own) = refs[:7]
    outs, (occ_ref, vir_ref) = refs[7:11], refs[11:]
    four_products(rows_dev, tau_count, first, steps, [own0, own1], [from_x, from_y], mix_ref, None, occ_ref, None)
    virtual_products(rows_dev, tau_count, 0, steps, [from_x, from_y], [virt_ref[2], virt_ref[3]], vir_ref)
    depth = 4 * rows_dev * own0.shape[1]
    chi = None
    for moment in range(tau_count):
        here = slice(moment * depth, (moment + 1) * depth)
        part = slice(moment * depth // 2, (moment + 1) * depth // 2)
        vir_late = jnp.concatenate([vir_own[:, part], vir_ref[:, part]], 1)
        term = lax.dot_general(
            jnp.concatenate([occ_early[:, here], occ_ref[:, here]], 0),
            jnp.concatenate([vir_early[:, here], vir_late], 0),
            (((1,), (1,)), ((), ())), preferred_element_type=F32,
        ) * tau_ref[moment]
        chi = term if chi is None else chi + term
    chi = chi * scale
    me = lax.axis_index("orb")
    share_rows = outs[0].shape[0]
    for distance, out in zip(partners(4), outs):
        picked = chi[0:share_rows]
        for owner in range(1, 4):
            picked = jnp.where(me ^ distance == owner, chi[owner * share_rows : (owner + 1) * share_rows], picked)
        out[...] = picked.astype(out.dtype)


def on_device_square(b_rows, col_blocks, g_occ, occ_live, g_virt, tau_weight):
    orb_count = lax.axis_size("orb")
    aux_count = lax.axis_size("aux")
    aux_dev, rows_dev, slot_count, tile = b_rows.shape
    tau_count = g_occ.shape[0]
    rows = orb_count * rows_dev
    steps = aux_dev // PAIR
    share_rows = aux_dev // orb_count
    sizes = (aux_count, rows_dev, tau_count)
    scale = 1.0 / math.sqrt(rows * tile * orb_count)
    smem = pl.BlockSpec(memory_space=pltpu.SMEM)
    vmem = pl.BlockSpec(memory_space=pltpu.VMEM)
    hbm = pl.BlockSpec(memory_space=pl.ANY)

    def call(kernel, name, out_shape, in_specs, scratch, limit, out_spec=vmem, flops=0):
        return pl.pallas_call(
            kernel, out_shape=out_shape, in_specs=in_specs, out_specs=[out_spec] * len(out_shape),
            scratch_shapes=scratch, compiler_params=pltpu.CompilerParams(vmem_limit_bytes=limit << 20), name=name,
            cost_estimate=pl.CostEstimate(flops=flops, bytes_accessed=0, transcendentals=0) if flops else None,
        )

    def xor(value, axis, distance):
        return lax.ppermute(value, axis, [(i, i ^ distance) for i in range(lax.axis_size(axis))])

    def half(*shape):
        return jax.ShapeDtypeStruct(shape, BF16)

    flat = b_rows.reshape(-1, tile)
    virt = g_virt.reshape(-1, tile)
    occ = g_occ.reshape(tau_count * rows_dev, -1)
    message = Message(virt.shape[0], occ.shape[0])
    dma = pltpu.SemaphoreType.DMA
    sent = call(
        functools.partial(message_kernel, message), "message", [half(message.rows, tile)] * orb_count, [hbm] * 3,
        [
            pltpu.VMEM((message.rows, tile), BF16), pltpu.VMEM(occ.shape, BF16),
            pltpu.SMEM(col_blocks.shape, jnp.int32), dma((3 + orb_count,)),
        ], 60, hbm, 10**10,
    )(virt, occ, col_blocks)
    came = {distance: xor(part, "orb", distance) for distance, part in zip(partners(orb_count)[1:], sent[1:])}
    messages = [sent[0]] + [came[distance] for distance in partners(orb_count)[1:]]
    block = half(aux_dev * rows_dev, tile)
    owns = call(functools.partial(own_kernel, rows_dev, steps), "own", [block] * 2, [vmem], [], 6, vmem, 10**10)(flat)
    early = steps * 12 // 16
    chunks = (early, steps - early)
    virt, chosen, *sends = call(
        functools.partial(send_kernel, message), "send",
        [half(3 * message.virt.stop, tile), jax.ShapeDtypeStruct((8, tile), F32)]
        + [half(count * PAIR * rows_dev, tile) for count in chunks for _ in range(2)],
        [vmem] * 6, [], 6, vmem, 10**10,
    )(*owns, *messages)
    got = [(xor(to_x, "orb", 1), xor(to_y, "orb", 2)) for to_x, to_y in zip(sends[0::2], sends[1::2])]
    (mix,) = call(
        functools.partial(mix_kernel, sizes, message), "mix",
        [half(tau_count * rows * SUB, rows * SUB)], [smem] + [vmem] * 5, [], 8,
    )(occ_live, *messages, chosen)
    wide = tau_count * rows * tile
    first = half(early * PAIR, wide)
    (occ_early,) = call(
        functools.partial(early_occ_kernel, rows_dev, tau_count, early), "occ", [first], [vmem] * 5, [], 6
    )(mix, *owns, *got[0])
    distances = aux_steps(aux_count)
    for number, distance in enumerate(distances):
        pair, other = half(2 * virt.shape[0], tile), xor(virt, "aux", distance)
        anchor = {0: mix, len(distances) - 1: occ_early}.get(number)
        if anchor is None:
            (virt,) = call(join_kernel, "join", [pair], [vmem] * 2, [], 4)(virt, other)
        else:
            (virt,) = call(join_after_kernel, "join", [pair], [vmem] * 2 + [hbm], [], 4)(virt, other, anchor)
    (virt,) = call(
        functools.partial(virt_kernel, sizes), "virt", [half(4, tile, tau_count * tile)], [vmem] * 2, [], 8
    )(chosen, virt)
    vir_early, vir_own = call(
        functools.partial(early_vir_kernel, rows_dev, tau_count, early, steps - early), "vir",
        [first, half((steps - early) * PAIR, wide // 2)], [vmem] * 5, [], 6
    )(virt, *owns, *got[0])
    shares = call(
        functools.partial(late_kernel, rows_dev, tau_count, early, steps - early, scale), "late",
        [jax.ShapeDtypeStruct((share_rows, aux_dev), F32)] + [half(share_rows, aux_dev)] * (orb_count - 1), [smem] + [vmem] * 9,
        [pltpu.VMEM(((steps - early) * PAIR, wide), BF16), pltpu.VMEM(((steps - early) * PAIR, wide // 2), BF16)], 16,
    )(tau_weight, mix, virt, *owns, *got[1], occ_early, vir_early, vir_own)
    total = shares[0]
    for distance, share in zip(partners(orb_count)[1:], shares[1:]):
        total = total + xor(share, "orb", distance).astype(F32)
    return total


def on_device(b_rows, col_blocks, g_occ, occ_live, g_virt, tau_weight):
    square = lax.axis_size("orb") == 4 and b_rows.shape[2] == 2
    plan = on_device_square if square else on_device_dense
    return plan(b_rows, col_blocks, g_occ, occ_live, g_virt, tau_weight)


def solution(mesh):
    in_specs = (
        P("aux", "orb", None, None),
        P("orb", None),
        P(None, "orb", None),
        P(),
        P(None, "orb", "aux", None),
        P(),
    )
    out_specs = P("orb", "aux")
    return jax.shard_map(
        on_device, mesh=mesh, in_specs=in_specs, out_specs=out_specs, check_vma=False
    )
```

```python
import functools
import math

import jax
import jax.numpy as jnp
from jax import lax
from jax.experimental import pallas as pl
from jax.experimental.pallas import tpu as pltpu
from jax.sharding import PartitionSpec as P

SUB = 8
PAIR = 16
UNROLL = 16
F32 = jnp.float32
BF16 = jnp.bfloat16


def iota(shape, dim):
    return lax.broadcasted_iota(jnp.int32, shape, dim)


def dot(a, b):
    return jnp.dot(a, b, preferred_element_type=F32)


def partners(count):
    return [0] + sorted(range(1, count), key=lambda distance: (-distance.bit_count(), distance))


def pick_static(index, values):
    found = jnp.zeros_like(index)
    for place, value in enumerate(values):
        found = jnp.where(index == place, value, found)
    return found


def pack_kernel(rows_dev, slot_count, chunks, pieces, col_hbm, b_hbm, occ_hbm, *refs):
    orb_count = lax.axis_size("orb")
    count = len(chunks) * orb_count
    outs, helds = refs[:count], refs[count : 2 * count]
    b_ref, occ_ref, col_ref, b_sem, occ_sem, col_sem, out_sem = refs[2 * count :]
    me = lax.axis_index("orb")
    half_rows = rows_dev * SUB
    out_rows = 2 * half_rows
    in_rows = PAIR * rows_dev * slot_count
    steps = sum(chunks)
    piece_steps = steps // pieces
    piece_rows = piece_steps * in_rows

    def fetch(piece):
        here = pl.ds(piece * piece_rows, piece_rows)
        return pltpu.make_async_copy(b_hbm.at[here], b_ref.at[here], b_sem.at[piece])

    occ_copy = pltpu.make_async_copy(occ_hbm, occ_ref, occ_sem)
    col_copy = pltpu.make_async_copy(col_hbm, col_ref, col_sem)
    col_copy.start()
    for piece in range(pieces):
        fetch(piece).start()
    occ_copy.start()
    line = iota((out_rows, in_rows), 0)
    place = iota((out_rows, in_rows), 1)
    half = line // half_rows
    row = (line % half_rows) // SUB
    func = half * SUB + line % SUB
    first = (func * rows_dev + row) * slot_count
    pick = jnp.concatenate(
        [jnp.where(place == first + slot, 1.0, 0.0).astype(BF16) for slot in range(slot_count)], 0
    )
    occ_copy.wait()
    total = chunks[0] * out_rows
    for held in helds[:orb_count]:
        held[total:, :] = jnp.zeros((held.shape[0] - total, held.shape[1]), BF16)
        held[total:, : occ_ref.shape[1]] = occ_ref[...]
    col_copy.wait()

    def step(index, group, start):
        at = pl.multiple_of(index * in_rows, in_rows)
        moved = dot(pick, b_ref[pl.ds(at, in_rows), :]).astype(BF16)
        slots = [moved[slot * out_rows : (slot + 1) * out_rows] for slot in range(slot_count)]
        zero = jnp.zeros_like(slots[0])
        for distance, held in zip(partners(orb_count), group):
            value = zero
            for slot in range(slot_count):
                value = jnp.where(col_ref[0, slot] == me ^ distance, slots[slot], value)
            held[pl.ds(pl.multiple_of((index - start) * out_rows, out_rows), out_rows), :] = value

    sent = []
    start = 0
    for number, chunk in enumerate(chunks):
        group = range(number * orb_count, (number + 1) * orb_count)
        for piece in range(start // piece_steps, (start + chunk) // piece_steps):
            fetch(piece).wait()
            low = piece * piece_steps
            lax.fori_loop(
                low, low + piece_steps,
                lambda index, carry: (step(index, [helds[at] for at in group], start), carry)[1],
                0, unroll=True,
            )
            top = low - start + piece_steps
            low_row = (low - start) * out_rows
            high_row = helds[group[0]].shape[0] if top == chunk else top * out_rows
            for place, at in enumerate(group):
                here = pl.ds(low_row, high_row - low_row)
                copy = pltpu.make_async_copy(helds[at].at[here], outs[at].at[here], out_sem.at[piece, place])
                copy.start()
                sent.append(copy)
        start += chunk
    for copy in sent:
        copy.wait()


def stage_kernel(orb_count, own_count, live_hbm, one_ref, two_ref, *refs):
    owns, outs = refs[:own_count], refs[own_count : 2 * own_count]
    live_out, join_out, live_ref, live_sem, own_sem = refs[2 * own_count :]
    live_copy = pltpu.make_async_copy(live_hbm, live_ref, live_sem)
    live_copy.start()
    copies = [pltpu.make_async_copy(own, out, own_sem.at[at]) for at, (own, out) in enumerate(zip(owns, outs))]
    for copy in copies:
        copy.start()
    join_out[: one_ref.shape[0], :] = one_ref[...]
    join_out[one_ref.shape[0] :, :] = two_ref[...]
    live_copy.wait()
    me = lax.axis_index("orb")
    order = partners(orb_count)
    tau_count = live_ref.shape[0]
    width = live_out.shape[1]
    group_of = iota((1, width), 1) // (width // orb_count)
    for moment in range(tau_count):
        for row_group in range(orb_count):
            live = jnp.zeros((1, width), jnp.int32)
            for col_group in range(orb_count):
                value = live_ref[moment, me ^ order[row_group], me ^ order[col_group]]
                live = jnp.where(group_of == col_group, value, live)
            at = moment * orb_count + row_group
            live_out[at : at + 1, :] = live
    for copy in copies:
        copy.wait()


def join_after_kernel(one_ref, two_ref, anchor, out_ref):
    join_kernel(one_ref, two_ref, out_ref)


def join_kernel(one_ref, two_ref, out_ref):
    out_ref[: one_ref.shape[0], :] = one_ref[...]
    out_ref[one_ref.shape[0] :, :] = two_ref[...]


def order_virt(sizes, virt_refs, virt_out):
    orb_count, aux_count, rows_dev, tau_count = sizes
    aux_me = lax.axis_index("aux")
    tile = virt_refs[0].shape[1]
    part = tile // aux_count
    virt_all = jnp.concatenate([ref[...] for ref in virt_refs], 0)
    line = iota((tile, virt_all.shape[0]), 0)
    place = iota((tile, virt_all.shape[0]), 1)
    for moment in range(tau_count):
        wanted = (((line // part) ^ aux_me) * tau_count + moment) * part + line % part
        chosen = dot(jnp.where(place == wanted, 1.0, 0.0).astype(BF16), virt_all)
        virt_out[:, moment * tile : (moment + 1) * tile] = chosen.astype(BF16)


def spread_occ(sizes, live_ref, blocks, total, mix_out):
    orb_count, aux_count, rows_dev, tau_count = sizes
    me = lax.axis_index("orb")
    rows = orb_count * rows_dev
    half_rows = rows_dev * SUB
    tile = blocks[0].shape[1]
    occ_all = jnp.concatenate([block[total : total + tau_count * rows_dev, :] for block in blocks], 0)
    left_shape = (tau_count * rows * SUB, occ_all.shape[0])
    line = iota(left_shape, 0)
    moment_of = line // (rows * SUB)
    row_of = (line % (rows * SUB)) // SUB
    wanted = ((row_of // rows_dev) * tau_count + moment_of) * rows_dev + row_of % rows_dev
    left = jnp.where(iota(left_shape, 1) == wanted, 1.0, 0.0).astype(BF16)
    right_shape = (tile, rows * SUB)
    col_of = iota(right_shape, 1) // SUB
    group = pick_static(col_of // rows_dev, partners(orb_count)) ^ me
    wanted = group * rows_dev + col_of % rows_dev
    right = jnp.where(iota(right_shape, 0) == wanted, 1.0, 0.0).astype(BF16)
    spread = dot(dot(left, occ_all).astype(BF16), right)
    same = iota((half_rows, rows * SUB), 0) % SUB == iota((half_rows, rows * SUB), 1) % SUB
    for at in range(tau_count * orb_count):
        here = slice(at * half_rows, (at + 1) * half_rows)
        keep = jnp.logical_and(same, live_ref[at : at + 1, :] != 0)
        mix_out[here, :] = jnp.where(keep, spread[here], 0.0).astype(BF16)


def products(sizes, steps, blocks, mix_ref, virt_ref, occ_out, vir_out):
    orb_count, aux_count, rows_dev, tau_count = sizes
    rows = orb_count * rows_dev
    half_rows = rows_dev * SUB
    tile = blocks[0].shape[1]

    def step(index, carry):
        here = pl.ds(pl.multiple_of(index * PAIR, PAIR), PAIR)
        halves = []
        for half in range(2):
            at = pl.multiple_of((index * 2 + half) * half_rows, half_rows)
            halves.append(jnp.concatenate([block[pl.ds(at, half_rows), :] for block in blocks], 0))
        if occ_out is not None:
            occ = dot(mix_ref[...], jnp.concatenate(halves, 1))
            occ = [occ[:, half * tile : (half + 1) * tile].reshape(tau_count * rows, SUB, tile) for half in range(2)]
            occ = jnp.concatenate(occ, 1).astype(BF16)
            for row in range(tau_count * rows):
                occ_out[here, row * tile : (row + 1) * tile] = occ[row]
        if vir_out is not None:
            vir = dot(jnp.concatenate(halves, 0), virt_ref[...]).reshape(2, rows, SUB, tau_count * tile)
            vir = jnp.concatenate([vir[0], vir[1]], 1).astype(BF16)
            for moment in range(tau_count):
                for row in range(rows):
                    at = (moment * rows + row) * tile
                    vir_out[here, at : at + tile] = vir[row, :, moment * tile : (moment + 1) * tile]
        return carry

    lax.fori_loop(0, steps, step, 0, unroll=min(steps, UNROLL))


def occ_kernel(sizes, steps, live_ref, *refs):
    blocks, (mix_out, occ_out) = refs[: sizes[0]], refs[sizes[0] :]
    spread_occ(sizes, live_ref, blocks, steps * 2 * sizes[2] * SUB, mix_out)
    products(sizes, steps, blocks, mix_out, None, occ_out, None)


def vir_kernel(sizes, steps, *refs):
    blocks, virt_refs = refs[: sizes[0]], refs[sizes[0] : -3]
    anchor, virt_out, vir_out = refs[-3:]
    order_virt(sizes, virt_refs, virt_out)
    products(sizes, steps, blocks, None, virt_out, None, vir_out)


def last_kernel(sizes, steps, share_rows, tau_ref, mix_ref, virt_ref, occ_first, vir_first, *refs):
    orb_count, aux_count, rows_dev, tau_count = sizes
    blocks, outs = refs[:orb_count], refs[orb_count : 2 * orb_count]
    occ_last, vir_last = refs[2 * orb_count :]
    products(sizes, steps, blocks, mix_ref, virt_ref, occ_last, vir_last)
    me = lax.axis_index("orb")
    rows = orb_count * rows_dev
    tile = blocks[0].shape[1]
    depth = rows * tile
    part = min(depth, 4096)
    chi = None
    for moment in range(tau_count):
        for piece in range(depth // part):
            here = slice(moment * depth + piece * part, moment * depth + (piece + 1) * part)
            term = lax.dot_general(
                jnp.concatenate([occ_first[:, here], occ_last[:, here]], 0),
                jnp.concatenate([vir_first[:, here], vir_last[:, here]], 0),
                (((1,), (1,)), ((), ())), preferred_element_type=F32,
            ) * tau_ref[moment]
            chi = term if chi is None else chi + term
    chi = chi * (1.0 / math.sqrt(rows * tile * orb_count))
    for distance, out in zip(partners(orb_count), outs):
        picked = chi[0:share_rows]
        for owner in range(1, orb_count):
            picked = jnp.where(me ^ distance == owner, chi[owner * share_rows : (owner + 1) * share_rows], picked)
        out[...] = picked


def on_device_dense(b_rows, col_blocks, g_occ, occ_live, g_virt, tau_weight):
    orb_count = lax.axis_size("orb")
    aux_count = lax.axis_size("aux")
    aux_dev, rows_dev, slot_count, tile = b_rows.shape
    tau_count = g_occ.shape[0]
    rows = orb_count * rows_dev
    share_rows = aux_dev // orb_count
    sizes = (orb_count, aux_count, rows_dev, tau_count)
    smem = pl.BlockSpec(memory_space=pltpu.SMEM)
    vmem = pl.BlockSpec(memory_space=pltpu.VMEM)

    def call(kernel, name, out_shape, in_specs, scratch, spare, out_spec=vmem):
        held = sum(math.prod(shape.shape) * 2 for shape in scratch if shape.dtype == BF16)
        return pl.pallas_call(
            kernel,
            out_shape=out_shape,
            in_specs=in_specs,
            out_specs=[out_spec] * len(out_shape),
            scratch_shapes=scratch,
            compiler_params=pltpu.CompilerParams(vmem_limit_bytes=min(held + (spare << 20), 60 << 20)),
            name=name,
        )

    def xor(value, axis, distance):
        return lax.ppermute(value, axis, [(i, i ^ distance) for i in range(lax.axis_size(axis))])

    def half(value):
        return jax.ShapeDtypeStruct(value, BF16)

    all_steps = aux_dev // PAIR
    chunks = (all_steps * 12 // 16, all_steps - all_steps * 12 // 16)
    occ_rows = tau_count * rows_dev
    b_flat = b_rows.reshape(-1, tile)
    occ_flat = g_occ.reshape(occ_rows, -1)
    hbm = pl.BlockSpec(memory_space=pl.ANY)
    pieces = math.gcd(4, all_steps)
    shapes = [
        (steps * PAIR * rows_dev + (0 if number else occ_rows), tile)
        for number, steps in enumerate(chunks) for _ in range(orb_count)
    ]
    blocks = call(
        functools.partial(pack_kernel, rows_dev, slot_count, chunks, pieces), "pack",
        [half(shape) for shape in shapes], [hbm] * 3,
        [pltpu.VMEM(shape, BF16) for shape in shapes] + [
            pltpu.VMEM(b_flat.shape, BF16), pltpu.VMEM(occ_flat.shape, BF16), pltpu.SMEM(col_blocks.shape, jnp.int32),
            pltpu.SemaphoreType.DMA((pieces,)), pltpu.SemaphoreType.DMA, pltpu.SemaphoreType.DMA,
            pltpu.SemaphoreType.DMA((pieces, orb_count)),
        ], 54, hbm,
    )(col_blocks, b_flat, occ_flat)
    order = partners(orb_count)
    dense = []
    for number in range(len(chunks)):
        own, *others = blocks[number * orb_count : (number + 1) * orb_count]
        dense.append([own] + [xor(value, "orb", d) for d, value in zip(order[1:], others)])
    virt = g_virt.reshape(-1, tile)
    owns = [blocks[number * orb_count] for number in range(len(chunks))]
    *owns, live, virt = call(
        functools.partial(stage_kernel, orb_count, len(chunks)), "stage",
        [half(own.shape) for own in owns]
        + [jax.ShapeDtypeStruct((tau_count * orb_count, rows * SUB), jnp.int32), half((2 * virt.shape[0], tile))],
        [hbm, vmem, vmem] + [hbm] * len(owns),
        [pltpu.SMEM(occ_live.shape, jnp.int32), pltpu.SemaphoreType.DMA, pltpu.SemaphoreType.DMA((len(owns),))], 4,
    )(occ_live, virt, xor(virt, "aux", 1), *owns)
    for own, group in zip(owns, dense):
        group[0] = own
    distance = 2
    while distance < aux_count:
        pair = half((2 * virt.shape[0], tile))
        virt = call(join_kernel, "join", [pair], [vmem] * 2, [], 2)(virt, xor(virt, "aux", distance))[0]
        distance *= 2
    virts = [virt]
    wide = half((chunks[0] * PAIR, tau_count * rows * tile))
    mix, occ_first = call(
        functools.partial(occ_kernel, sizes, chunks[0]), "occ",
        [half((tau_count * rows * SUB, rows * SUB)), wide],
        [vmem] * (1 + orb_count), [], 8,
    )(live, *dense[0])
    virt, vir_first = call(
        functools.partial(vir_kernel, sizes, chunks[0]), "vir",
        [half((tile, tau_count * tile)), wide],
        [vmem] * (orb_count + len(virts)) + [hbm], [], 8,
    )(*dense[0], *virts, mix)
    shares = call(
        functools.partial(last_kernel, sizes, chunks[1], share_rows), "last",
        [jax.ShapeDtypeStruct((share_rows, aux_dev), F32)] * orb_count,
        [smem] + [vmem] * (4 + orb_count),
        [pltpu.VMEM((chunks[1] * PAIR, tau_count * rows * tile), BF16)] * 2, 12,
    )(tau_weight, mix, virt, occ_first, vir_first, *dense[1])
    total = shares[0]
    for distance, share in zip(order[1:], shares[1:]):
        total = total + xor(share, "orb", distance)
    return total


class Message:
    def __init__(self, virt_rows, occ_rows):
        self.virt = slice(0, virt_rows)
        self.occ = slice(virt_rows, virt_rows + occ_rows)
        self.list = slice(virt_rows + occ_rows, virt_rows + occ_rows + 16)
        self.rows = virt_rows + occ_rows + 16


def equal(one, two):
    return jnp.where(one == two, 1.0, 0.0)


def by_distance(refs):
    return [refs[[0, 3, 1, 2].index(distance)] for distance in range(4)]


def at_group(group, values):
    found = values[0]
    for place in range(1, len(values)):
        found = jnp.where(group == place, values[place], found)
    return found


class Choice:
    def __init__(self, message, refs):
        me = lax.axis_index("orb")
        near = []
        for ref in refs:
            row = ref[message.list, :].astype(F32)[0:1, :]
            near.append([row[:, slot : slot + 1] for slot in range(2)])
        lists = [[at_group(me ^ group, [near[d][slot] for d in range(4)]) for slot in range(2)] for group in range(4)]
        shape = (8, 128)
        index = iota(shape, 0) * shape[1] + iota(shape, 1)
        bits = [((index >> place) & 1).astype(F32) for place in range(8)]
        sent_x = [lists[g][0] + bits[g] * (lists[g][1] - lists[g][0]) for g in range(4)]
        sent_y = [lists[g][0] + bits[4 + g] * (lists[g][1] - lists[g][0]) for g in range(4)]
        good = jnp.where(index < 256, 1.0, 0.0)
        for one, two in ((0, 1), (2, 3), (0, 2), (1, 3), (0, 3), (1, 2)):
            for slot in range(2):
                column = lists[one][slot]
                shared = jnp.maximum(equal(column, lists[two][0]), equal(column, lists[two][1]))
                if two == one ^ 1:
                    met = jnp.maximum(equal(sent_x[one], column), equal(sent_x[two], column))
                elif two == one ^ 2:
                    met = jnp.maximum(equal(sent_y[one], column), equal(sent_y[two], column))
                else:
                    met = jnp.maximum(
                        equal(sent_x[one], column) * equal(sent_y[two], column),
                        equal(sent_y[one], column) * equal(sent_x[two], column),
                    )
                good = good * jnp.maximum(met, 1.0 - shared)
        number = jnp.where(good > 0.5, index.astype(F32), 1024.0)
        number = jnp.min(jnp.min(number, axis=1, keepdims=True), axis=0, keepdims=True)
        chosen = []
        for place in range(8):
            rest = jnp.floor(number * (1.0 / (1 << place)))
            chosen.append(rest - 2.0 * jnp.floor(rest * 0.5))
        all_x = [lists[g][0] + chosen[g] * (lists[g][1] - lists[g][0]) for g in range(4)]
        all_y = [lists[g][0] + chosen[4 + g] * (lists[g][1] - lists[g][0]) for g in range(4)]
        self.own = at_group(me, [lists[g][0] for g in range(4)]), at_group(me, [lists[g][1] for g in range(4)])
        self.slot_x = at_group(me, chosen[:4])
        self.slot_y = at_group(me, chosen[4:])
        got_x, got_y = at_group(me ^ 1, all_x), at_group(me ^ 2, all_y)
        self.got = got_x, got_y
        one = jnp.ones_like(got_x)
        foreign = one - jnp.maximum(equal(got_x, self.own[0]), equal(got_x, self.own[1]))
        self.third = foreign * got_x + (one - foreign) * got_y
        first_x = jnp.where(me < (me ^ 1), one, one - equal(at_group(me, all_x), got_x))
        first_y = jnp.where(me < (me ^ 2), one, one - equal(at_group(me, all_y), got_y))
        also = equal(at_group(me ^ 2, all_x), got_x) * equal(at_group(me ^ 1, all_y), got_x)
        first_far = jnp.where(me < (me ^ 3), one, one - also)
        zero = jnp.zeros_like(one)
        with_x = [equal(got_x, column) * first_x for column in self.own]
        with_y = [equal(got_y, column) * first_y for column in self.own]
        far = equal(got_x, got_y) * first_far
        self.pairs = [
            [one, zero, with_x[0], with_y[0]],
            [zero, one, with_x[1], with_y[1]],
            [with_x[0], with_x[1], zero, far],
            [with_y[0], with_y[1], far, zero],
        ]


class Chosen:
    def __init__(self, ref):
        values = [ref[0:1, place : place + 1] for place in range(20)]
        self.own, self.got = values[0:2], values[2:4]
        self.pairs = [values[4 + 4 * block : 8 + 4 * block] for block in range(4)]

    @staticmethod
    def leave(choice, ref):
        values = [*choice.own, *choice.got] + [value for row in choice.pairs for value in row]
        lane = iota(ref.shape, 1)
        total = jnp.zeros(ref.shape, F32)
        for place, value in enumerate(values):
            total = jnp.where(lane == place, value, total)
        ref[...] = total


def message_kernel(message, virt_hbm, occ_hbm, col_hbm, *refs):
    *outs, out_ref, occ_ref, col_ref, sem = refs
    copies = [
        pltpu.make_async_copy(virt_hbm, out_ref.at[message.virt], sem.at[0]),
        pltpu.make_async_copy(occ_hbm, occ_ref, sem.at[1]),
        pltpu.make_async_copy(col_hbm, col_ref, sem.at[2]),
    ]
    for copy in copies:
        copy.start()
    tile = out_ref.shape[1]
    out_ref[message.occ, :] = jnp.zeros((occ_ref.shape[0], tile), BF16)
    for copy in copies:
        copy.wait()
    out_ref[message.occ, : occ_ref.shape[1]] = occ_ref[...]
    row, lane = iota((16, tile), 0), iota((16, tile), 1)
    value = jnp.zeros((16, tile), F32)
    for slot in range(col_ref.shape[1]):
        here = jnp.logical_and(row == 0, lane == slot)
        value = jnp.where(here, col_ref[0, slot].astype(F32), value)
    out_ref[message.list, :] = value.astype(BF16)
    copies = [pltpu.make_async_copy(out_ref, out, sem.at[3 + at]) for at, out in enumerate(outs)]
    for copy in copies:
        copy.start()
    for copy in copies:
        copy.wait()


def own_kernel(rows_dev, steps, b_ref, *outs):
    half_rows = rows_dev * SUB
    out_rows = 2 * half_rows
    in_rows = PAIR * rows_dev * 2
    line = iota((out_rows, in_rows), 0)
    place = iota((out_rows, in_rows), 1)
    func = (line // half_rows) * SUB + line % SUB
    first = (func * rows_dev + (line % half_rows) // SUB) * 2
    pick = jnp.concatenate([jnp.where(place == first + slot, 1.0, 0.0).astype(BF16) for slot in range(2)], 0)
    for index in range(steps):
        moved = dot(pick, b_ref[index * in_rows : (index + 1) * in_rows, :]).astype(BF16)
        for slot, out in enumerate(outs):
            out[index * out_rows : (index + 1) * out_rows, :] = moved[slot * out_rows : (slot + 1) * out_rows]


def send_kernel(message, *refs):
    messages, (own0, own1), (virt_out, chosen, *outs) = by_distance(refs[2:6]), refs[:2], refs[6:]
    choice = Choice(message, messages)
    Chosen.leave(choice, chosen)
    at = 0
    for to_x, to_y in zip(outs[0::2], outs[1::2]):
        here = slice(at, at + to_x.shape[0])
        to_x[...] = jnp.where(choice.slot_x > 0.5, own1[here, :], own0[here, :])
        to_y[...] = jnp.where(choice.slot_y > 0.5, own1[here, :], own0[here, :])
        at += to_x.shape[0]
    me = lax.axis_index("orb")
    rows = message.virt.stop
    for slot, column in enumerate((choice.own[0], choice.own[1], choice.third)):
        total = jnp.zeros((rows, virt_out.shape[1]), F32)
        for distance in range(4):
            weight = equal(column, (me ^ distance).astype(F32))
            total = total + weight * messages[distance][message.virt, :].astype(F32)
        virt_out[slot * rows : (slot + 1) * rows, :] = total.astype(BF16)


def aux_steps(aux_count):
    steps = []
    distance = aux_count // 2
    while distance:
        steps.append(distance)
        distance //= 2
    return steps


def aux_order(aux_count):
    order = [0]
    for distance in aux_steps(aux_count):
        order = order + [value ^ distance for value in order]
    return order


def virt_kernel(sizes, *refs):
    aux_count, rows_dev, tau_count = sizes
    chosen, virt_ref, virt_out = refs
    choice = Chosen(chosen)
    aux_me = lax.axis_index("aux")
    tile = virt_ref.shape[1]
    part = tile // aux_count
    order = aux_order(aux_count)
    line = iota((tile, virt_ref.shape[0]), 0)
    place = iota((tile, virt_ref.shape[0]), 1)
    virts = []
    for slot in range(3):
        columns = []
        for moment in range(tau_count):
            held = pick_static((line // part) ^ aux_me, [order.index(value) for value in range(aux_count)])
            wanted = ((held * 3 + slot) * tau_count + moment) * part + line % part
            columns.append(dot(jnp.where(place == wanted, 1.0, 0.0).astype(BF16), virt_ref[...]))
        virts.append(jnp.concatenate(columns, 1))
    virt_out[0] = virts[0].astype(BF16)
    virt_out[1] = virts[1].astype(BF16)
    for at, column in enumerate(choice.got):
        one, two = equal(column, choice.own[0]), equal(column, choice.own[1])
        virt_out[2 + at] = (one * virts[0] + two * virts[1] + (1.0 - one - two) * virts[2]).astype(BF16)


def mix_kernel(sizes, message, live_ref, *refs):
    aux_count, rows_dev, tau_count = sizes
    messages, chosen, mix_out = by_distance(refs[:4]), refs[4], refs[5]
    choice = Chosen(chosen)
    me = lax.axis_index("orb")
    tile = messages[0].shape[1]
    rows = 4 * rows_dev
    half_rows = rows_dev * SUB
    groups = [me, me, me ^ 1, me ^ 2]
    occ_all = jnp.concatenate([messages[at][message.occ, :] for at in (0, 0, 1, 2)], 0)
    left_shape = (tau_count * rows * SUB, occ_all.shape[0])
    line = iota(left_shape, 0)
    row_of = (line % (rows * SUB)) // SUB
    wanted = ((row_of // rows_dev) * tau_count + line // (rows * SUB)) * rows_dev + row_of % rows_dev
    left = jnp.where(iota(left_shape, 1) == wanted, 1.0, 0.0).astype(BF16)
    right_shape = (tile, rows * SUB)
    col_of = iota(right_shape, 1) // SUB
    wanted = pick_static(col_of // rows_dev, groups) * rows_dev + col_of % rows_dev
    right = jnp.where(iota(right_shape, 0) == wanted, 1.0, 0.0).astype(BF16)
    spread = dot(dot(left, occ_all).astype(BF16), right)
    same = iota((half_rows, rows * SUB), 0) % SUB == iota((half_rows, rows * SUB), 1) % SUB
    group_of = iota((1, rows * SUB), 1) // half_rows
    for moment in range(tau_count):
        for one in range(4):
            live = jnp.zeros((1, rows * SUB), F32)
            for two in range(4):
                value = live_ref[moment, groups[one], groups[two]].astype(F32) * choice.pairs[one][two]
                live = jnp.where(group_of == two, value, live)
            at = (moment * 4 + one) * half_rows
            keep = jnp.logical_and(same, live != 0.0)
            mix_out[at : at + half_rows, :] = jnp.where(keep, spread[at : at + half_rows], 0.0).astype(BF16)


def four_products(rows_dev, tau_count, first, steps, owns, got, mix_ref, virt_ref, occ_ref, vir_ref):
    rows = 4 * rows_dev
    half_rows = rows_dev * SUB
    tile = owns[0].shape[1]
    blocks = [(own, first) for own in owns] + [(block, 0) for block in got]

    def step(index, carry):
        here = pl.ds(pl.multiple_of(index * PAIR, PAIR), PAIR)
        if occ_ref is not None:
            halves = []
            for half in range(2):
                halves.append(jnp.concatenate([
                    block[pl.ds(pl.multiple_of(((index + shift) * 2 + half) * half_rows, half_rows), half_rows), :]
                    for block, shift in blocks
                ], 0))
            occ = dot(mix_ref[...], jnp.concatenate(halves, 1))
            occ = [occ[:, half * tile : (half + 1) * tile].reshape(tau_count * rows, SUB, tile) for half in range(2)]
            occ = jnp.concatenate(occ, 1).astype(BF16)
            for row in range(tau_count * rows):
                occ_ref[here, row * tile : (row + 1) * tile] = occ[row]
        if vir_ref is not None:
            for group, (block, shift) in enumerate(blocks):
                at = pl.multiple_of((index + shift) * 2 * half_rows, half_rows)
                vir = dot(block[pl.ds(at, 2 * half_rows), :], virt_ref[group])
                vir = vir.reshape(2, rows_dev, SUB, tau_count * tile)
                vir = jnp.concatenate([vir[0], vir[1]], 1).astype(BF16)
                for moment in range(tau_count):
                    for row in range(rows_dev):
                        at = (moment * rows + group * rows_dev + row) * tile
                        vir_ref[here, at : at + tile] = vir[row, :, moment * tile : (moment + 1) * tile]
        return carry

    lax.fori_loop(0, steps, step, 0, unroll=min(steps, UNROLL))


def early_occ_kernel(rows_dev, tau_count, steps, mix_ref, own0, own1, from_x, from_y, occ_out):
    four_products(rows_dev, tau_count, 0, steps, [own0, own1], [from_x, from_y], mix_ref, None, occ_out, None)


def early_vir_kernel(rows_dev, tau_count, steps, virt_ref, own0, own1, from_x, from_y, vir_out):
    four_products(rows_dev, tau_count, 0, steps, [own0, own1], [from_x, from_y], None, virt_ref, None, vir_out)


def late_kernel(rows_dev, tau_count, first, steps, scale, tau_ref, mix_ref, virt_ref, *refs):
    (own0, own1, from_x, from_y, occ_early, vir_early), outs, (occ_ref, vir_ref) = refs[:6], refs[6:10], refs[10:]
    four_products(rows_dev, tau_count, first, steps, [own0, own1], [from_x, from_y], mix_ref, virt_ref, occ_ref, vir_ref)
    depth = 4 * rows_dev * own0.shape[1]
    chi = None
    for moment in range(tau_count):
        here = slice(moment * depth, (moment + 1) * depth)
        term = lax.dot_general(
            jnp.concatenate([occ_early[:, here], occ_ref[:, here]], 0),
            jnp.concatenate([vir_early[:, here], vir_ref[:, here]], 0),
            (((1,), (1,)), ((), ())), preferred_element_type=F32,
        ) * tau_ref[moment]
        chi = term if chi is None else chi + term
    chi = chi * scale
    me = lax.axis_index("orb")
    share_rows = outs[0].shape[0]
    for distance, out in zip([0, 3, 2, 1], outs):
        picked = chi[0:share_rows]
        for owner in range(1, 4):
            picked = jnp.where(me ^ distance == owner, chi[owner * share_rows : (owner + 1) * share_rows], picked)
        out[...] = picked


def on_device_square(b_rows, col_blocks, g_occ, occ_live, g_virt, tau_weight):
    orb_count = lax.axis_size("orb")
    aux_count = lax.axis_size("aux")
    aux_dev, rows_dev, slot_count, tile = b_rows.shape
    tau_count = g_occ.shape[0]
    rows = orb_count * rows_dev
    steps = aux_dev // PAIR
    share_rows = aux_dev // orb_count
    sizes = (aux_count, rows_dev, tau_count)
    scale = 1.0 / math.sqrt(rows * tile * orb_count)
    smem = pl.BlockSpec(memory_space=pltpu.SMEM)
    vmem = pl.BlockSpec(memory_space=pltpu.VMEM)
    hbm = pl.BlockSpec(memory_space=pl.ANY)

    def call(kernel, name, out_shape, in_specs, scratch, limit, out_spec=vmem, flops=0):
        return pl.pallas_call(
            kernel, out_shape=out_shape, in_specs=in_specs, out_specs=[out_spec] * len(out_shape),
            scratch_shapes=scratch, compiler_params=pltpu.CompilerParams(vmem_limit_bytes=limit << 20), name=name,
            cost_estimate=pl.CostEstimate(flops=flops, bytes_accessed=0, transcendentals=0) if flops else None,
        )

    def xor(value, axis, distance):
        return lax.ppermute(value, axis, [(i, i ^ distance) for i in range(lax.axis_size(axis))])

    def half(*shape):
        return jax.ShapeDtypeStruct(shape, BF16)

    flat = b_rows.reshape(-1, tile)
    virt = g_virt.reshape(-1, tile)
    occ = g_occ.reshape(tau_count * rows_dev, -1)
    message = Message(virt.shape[0], occ.shape[0])
    dma = pltpu.SemaphoreType.DMA
    sent = call(
        functools.partial(message_kernel, message), "message", [half(message.rows, tile)] * orb_count, [hbm] * 3,
        [
            pltpu.VMEM((message.rows, tile), BF16), pltpu.VMEM(occ.shape, BF16),
            pltpu.SMEM(col_blocks.shape, jnp.int32), dma((3 + orb_count,)),
        ], 60, hbm, 10**10,
    )(virt, occ, col_blocks)
    came = {distance: xor(part, "orb", distance) for distance, part in zip([3, 1, 2], sent[1:])}
    messages = [sent[0]] + [came[distance] for distance in [3, 1, 2]]
    block = half(aux_dev * rows_dev, tile)
    owns = call(functools.partial(own_kernel, rows_dev, steps), "own", [block] * 2, [vmem], [], 6, vmem, 10**10)(flat)
    early = steps * 12 // 16
    chunks = (early, steps - early)
    virt, chosen, *sends = call(
        functools.partial(send_kernel, message), "send",
        [half(3 * message.virt.stop, tile), jax.ShapeDtypeStruct((8, tile), F32)]
        + [half(count * PAIR * rows_dev, tile) for count in chunks for _ in range(2)],
        [vmem] * 6, [], 6, vmem, 10**10,
    )(*owns, *messages)
    got = [(xor(to_x, "orb", 1), xor(to_y, "orb", 2)) for to_x, to_y in zip(sends[0::2], sends[1::2])]
    (mix,) = call(
        functools.partial(mix_kernel, sizes, message), "mix",
        [half(tau_count * rows * SUB, rows * SUB)], [smem] + [vmem] * 5, [], 8,
    )(occ_live, *messages, chosen)
    wide = tau_count * rows * tile
    first = half(early * PAIR, wide)
    (occ_early,) = call(
        functools.partial(early_occ_kernel, rows_dev, tau_count, early), "occ", [first], [vmem] * 5, [], 6
    )(mix, *owns, *got[0])
    distances = aux_steps(aux_count)
    for number, distance in enumerate(distances):
        pair, other = half(2 * virt.shape[0], tile), xor(virt, "aux", distance)
        anchor = {0: mix, len(distances) - 1: occ_early}.get(number)
        if anchor is None:
            (virt,) = call(join_kernel, "join", [pair], [vmem] * 2, [], 4)(virt, other)
        else:
            (virt,) = call(join_after_kernel, "join", [pair], [vmem] * 2 + [hbm], [], 4)(virt, other, anchor)
    (virt,) = call(
        functools.partial(virt_kernel, sizes), "virt", [half(4, tile, tau_count * tile)], [vmem] * 2, [], 8
    )(chosen, virt)
    (vir_early,) = call(
        functools.partial(early_vir_kernel, rows_dev, tau_count, early), "vir", [first], [vmem] * 5, [], 6
    )(virt, *owns, *got[0])
    shares = call(
        functools.partial(late_kernel, rows_dev, tau_count, early, steps - early, scale), "late",
        [jax.ShapeDtypeStruct((share_rows, aux_dev), F32)] * orb_count, [smem] + [vmem] * 8,
        [pltpu.VMEM(((steps - early) * PAIR, wide), BF16), pltpu.VMEM(((steps - early) * PAIR, wide), BF16)], 16,
    )(tau_weight, mix, virt, *owns, *got[1], occ_early, vir_early)
    total = shares[0]
    for distance, share in zip([3, 2, 1], shares[1:]):
        total = total + xor(share, "orb", distance)
    return total


def on_device(b_rows, col_blocks, g_occ, occ_live, g_virt, tau_weight):
    square = lax.axis_size("orb") == 4 and b_rows.shape[2] == 2
    plan = on_device_square if square else on_device_dense
    return plan(b_rows, col_blocks, g_occ, occ_live, g_virt, tau_weight)


def solution(mesh):
    in_specs = (
        P("aux", "orb", None, None),
        P("orb", None),
        P(None, "orb", None),
        P(),
        P(None, "orb", "aux", None),
        P(),
    )
    out_specs = P("orb", "aux")
    return jax.shard_map(
        on_device, mesh=mesh, in_specs=in_specs, out_specs=out_specs, check_vma=False
    )
```
